128 devices in a mesh: row: 16 (over x, y_lo, core), col: 8 (over y_hi, z).
Axes of the slice: x: 4, y: 4 (y_hi: 2, y_lo: 2; y = y_hi * 2 + y_lo), z: 4, core: 2. Of those that a mesh axis runs over, the one named last changes fastest.
Arguments:
- corr: float32 [2, 9216, 9216], P(None, 'row', 'col'), may hold values from -1.8 to 1.8, as said below
- bonds_down: float32 [96, 96], replicated, may hold values from 0.5 to 1.5
- bonds_across: float32 [96, 96], replicated, may hold values from 0.5 to 1.5
- repulsion: float32 [96, 96], replicated, may hold values from 1 to 4
Outputs:
- corr_next: float32 [2, 9216, 9216], P(None, 'row', 'col')
The draws below stay inside these ranges and needn't reach their ends.
Inputs may be any that keep to these rules, and one draw needn't show every extreme that they name: `corr`: the real part's diagonal entries lie between 0 and 1.
All inputs are finite; a program needn't handle non-finite values.
Results may differ from the reference program's by a relative error of at most 0.00002.
Values sent between devices are 32-bit elements; how exact they have to be, the bound alone decides.
No kernel may reach another device: no remote copies, remote signals or barrier semaphores. Data moves between devices by JAX's collectives and lax.ppermute only.
A program may use at most 192 MiB of HBM per device.

```python
import math
import jax
import jax.numpy as jnp
from jax import lax

PATCH = 24
STEPS = 1
GX = 4
LX = 96
LY = 96
SITES = 9216


def draw_corr(key, part):
    key = jax.random.fold_in(key, 11)
    off_key, dens_key = jax.random.split(key)
    spread_vals = jnp.clip(0.3 * jax.random.normal(off_key, (2, SITES, SITES), jnp.float32), -1.8, 1.8)
    density = jax.random.uniform(dens_key, (SITES,), jnp.float32, 0.05, 0.95)
    row_ids = lax.broadcasted_iota(jnp.int32, (SITES, SITES), 0)
    col_ids = lax.broadcasted_iota(jnp.int32, (SITES, SITES), 1)
    real_part = jnp.where(row_ids == col_ids, density[:, None], spread_vals[0])
    return jnp.stack([real_part, spread_vals[1]])


def setup_inputs(seed: int = 0) -> dict:
    key_of = jax.random.split(jax.random.key(seed), 5)
    corr = draw_corr(jax.random.fold_in(key_of[4], 71), 0)
    bonds_down = jnp.clip(jnp.exp(jax.random.uniform(key_of[1], (LX, LY), jnp.float32, math.log(0.5), math.log(1.5))), 0.5, 1.5)
    bonds_across = jnp.clip(jnp.exp(jax.random.uniform(key_of[2], (LX, LY), jnp.float32, math.log(0.5), math.log(1.5))), 0.5, 1.5)
    repulsion = jnp.clip(jax.random.uniform(key_of[3], (LX, LY), jnp.float32, 1.0, 4.0), 1.0, 4.0)
    return {"corr": corr, "bonds_down": bonds_down, "bonds_across": bonds_across, "repulsion": repulsion}


time_step = 0.04


def padded_bonds(bonds_down, bonds_across):
    rows_axis = lax.broadcasted_iota(jnp.int32, bonds_down.shape, 0)
    cols_axis = lax.broadcasted_iota(jnp.int32, bonds_across.shape, 1)
    down_open = jnp.where(rows_axis < bonds_down.shape[0] - 1, bonds_down, 0.0)
    across_open = jnp.where(cols_axis < bonds_across.shape[1] - 1, bonds_across, 0.0)
    return jnp.pad(down_open, ((1, 0), (0, 0))), jnp.pad(across_open, ((0, 0), (1, 0)))


def to_lattice(field):
    extra = field.shape[1]
    return field.reshape(GX, 4, PATCH, PATCH, extra).transpose(0, 2, 1, 3, 4).reshape(LX, LY, extra)


def from_lattice(field):
    extra = field.shape[2]
    return field.reshape(GX, PATCH, 4, PATCH, extra).transpose(0, 2, 1, 3, 4).reshape(SITES, extra)


def site_values(values):
    return values.reshape(GX, PATCH, 4, PATCH).transpose(0, 2, 1, 3).reshape(SITES)


def hop_rows(field, down_pad, across_pad):
    lattice = jnp.pad(to_lattice(field), ((1, 1), (1, 1), (0, 0)))
    summed = down_pad[1:, :, None] * lattice[2:, 1:-1] + down_pad[:-1, :, None] * lattice[:-2, 1:-1]
    summed = summed + across_pad[:, 1:, None] * lattice[1:-1, 2:] + across_pad[:, :-1, None] * lattice[1:-1, :-2]
    return -from_lattice(summed)


def drift(state, down_pad, across_pad, repulsion):
    energy = site_values(repulsion) * jnp.diagonal(state[0])
    rates = []
    for member in range(2):
        field = state[member]
        rate = hop_rows(field, down_pad, across_pad) - hop_rows(field.T, down_pad, across_pad).T
        rate = rate + (energy[:, None] - energy[None, :]) * field
        rates.append(rate)
    return jnp.stack([rates[1], -rates[0]])


def reference(corr, bonds_down, bonds_across, repulsion):
    down_pad, across_pad = padded_bonds(bonds_down, bonds_across)
    state = corr
    for step_number in range(STEPS):
        first_rate = drift(state, down_pad, across_pad, repulsion)
        middle = state + time_step * first_rate
        second_rate = drift(middle, down_pad, across_pad, repulsion)
        state = state + (0.5 * time_step) * (first_rate + second_rate)
    return state
```

```python
import functools

import jax
import jax.numpy as jnp
from jax import lax
from jax.experimental import pallas as pl
from jax.experimental.pallas import tpu as pltpu
from jax.sharding import PartitionSpec as P

PATCH = 24
SQUARE = PATCH * PATCH
COLUMNS = 2 * SQUARE
LANES = 128
TILES = COLUMNS // LANES
LATTICE = 4 * PATCH
TIME_STEP = 0.04
F32 = jnp.float32
VMEM_LIMIT = 8 * 1024 * 1024

DN_IN, UP_IN, RT_IN, LF_IN, DN_RIM, UP_RIM, RT_RIM, LF_RIM, ROW_U = range(9)
C_DN, C_UP, C_RT, C_LF, C_DN_RIM, C_UP_RIM, C_RT_E, C_RT_F, C_LF_E, C_LF_F, C_X_E, C_X_F, COL_U = range(13)


def iota(shape, dim):
    return lax.broadcasted_iota(jnp.int32, shape, dim)


def over24(x):
    return ((x.astype(F32) + 0.5) * (1.0 / PATCH)).astype(jnp.int32)


def on(mask):
    return jnp.where(mask, 1.0, 0.0).astype(F32)


def within(x, lo, hi):
    return on(x >= lo) * on(x <= hi)


def place():
    return lax.axis_index("row"), lax.axis_index("col")


def tile(t):
    return pl.ds(t * LANES, LANES)


def weights_kernel(down_ref, across_ref, rep_ref, roww, colw):
    row_id, col_id = place()
    side = (LATTICE, LATTICE)
    down = jnp.where(iota(side, 0) < LATTICE - 1, down_ref[...], 0.0)
    across = jnp.where(iota(side, 1) < LATTICE - 1, across_ref[...], 0.0)
    rep = rep_ref[...]
    dot = functools.partial(jnp.dot, precision=lax.Precision.HIGHEST, preferred_element_type=F32)

    s = iota((SQUARE, LATTICE), 0)
    lane = iota((SQUARE, LATTICE), 1)
    a = over24(s)
    b = s - PATCH * a
    ga = PATCH * (row_id // 4) + a
    gb = PATCH * (row_id % 4) + b

    def pick_rows(table, da, db):
        rows = dot(on(lane == ga + da), table)
        return jnp.sum(jnp.where(lane == gb + db, rows, 0.0), axis=1, keepdims=True)

    a1 = a[:, 0:1]
    b1 = b[:, 0:1]
    last = PATCH - 1
    dn = -TIME_STEP * pick_rows(down, 0, 0)
    up = -TIME_STEP * pick_rows(down, -1, 0)
    rt = -TIME_STEP * pick_rows(across, 0, 0)
    lf = -TIME_STEP * pick_rows(across, 0, -1)
    values = {
        DN_IN: dn * on(a1 < last), UP_IN: up * on(a1 > 0), RT_IN: rt * on(b1 < last), LF_IN: lf * on(b1 > 0),
        DN_RIM: dn * on(a1 == last), UP_RIM: up * on(a1 == 0), RT_RIM: rt * on(b1 == last), LF_RIM: lf * on(b1 == 0),
        ROW_U: TIME_STEP * pick_rows(rep, 0, 0),
    }
    for k, v in values.items():
        roww[k] = jnp.broadcast_to(v, (SQUARE, LANES))

    wide = (LATTICE, COLUMNS)
    j = iota(wide, 1)
    g = (j >= SQUARE).astype(jnp.int32)
    jj = j - SQUARE * g
    a = over24(jj)
    b = jj - PATCH * a
    sub = iota(wide, 0)
    parity = col_id % 2
    ga = PATCH * (col_id // 2) + a
    gb = PATCH * (2 * parity + g) + b

    def pick_cols(table, da, db):
        cols = dot(table, on(sub == gb + db))
        return jnp.sum(jnp.where(sub == ga + da, cols, 0.0), axis=0, keepdims=True)

    a = a[0:1]
    b = b[0:1]
    g = g[0:1]
    dn = TIME_STEP * pick_cols(down, 0, 0)
    up = TIME_STEP * pick_cols(down, -1, 0)
    rt = TIME_STEP * pick_cols(across, 0, 0)
    lf = TIME_STEP * pick_cols(across, 0, -1)
    tails0 = rt * on(b == last) * on(g == 0)
    heads1 = lf * on(b == 0) * on(g == 1)
    tails1 = rt * on(b == last) * on(g == 1)
    heads0 = lf * on(b == 0) * on(g == 0)
    even = on(jnp.full(a.shape, parity, jnp.int32) == 0)
    x_even = even * tails1
    x_odd = (1.0 - even) * heads0
    rt_e = within(a, 3, 18)
    lf_e = within(a, 5, 20)
    xe_e = within(a, 6, 21)
    xo_e = within(a, 2, 17)
    values = {
        C_DN: dn * on(a < last), C_UP: up * on(a > 0), C_RT: rt * on(b < last), C_LF: lf * on(b > 0),
        C_DN_RIM: dn * on(a == last), C_UP_RIM: up * on(a == 0),
        C_RT_E: tails0 * rt_e, C_RT_F: tails0 * (1.0 - rt_e),
        C_LF_E: heads1 * lf_e, C_LF_F: heads1 * (1.0 - lf_e),
        C_X_E: x_even * xe_e + x_odd * xo_e, C_X_F: x_even * (1.0 - xe_e) + x_odd * (1.0 - xo_e),
        COL_U: TIME_STEP * pick_cols(rep, 0, 0),
    }
    for k, v in values.items():
        colw[k] = jnp.broadcast_to(v, (8, COLUMNS))


STRIP = (PATCH, LANES)


def squeeze_cols(tiles, lane24, m1, m2, n0):
    e = jnp.where(lane24 == m1, tiles[1], jnp.where(lane24 == m2, tiles[2], tiles[3]))
    f = jnp.where(lane24 == n0, tiles[0], tiles[4])
    return e, f


def lane_maps(shape=STRIP):
    lane = iota(shape, 1)
    return lane, lane - PATCH * over24(lane)


def parities():
    row_id, col_id = place()
    return lax.rem(col_id // 2, 2) == 0, lax.rem(col_id, 2) == 0, lax.rem(row_id // 4, 2) == 0, lax.rem(row_id, 2) == 0


FOLDS = (((0, 24, 16), (16, 88, 8), (40, 96, 8)), ((48, 24, 16), (64, 88, 16)), ((80, 24, 8), (104, 32, 8), (112, 88, 16)))
QUARTER = SQUARE // 4


def pack_faces(src, face_a, face_b, side, down_a, down_b, across_a, across_b, diag):
    up_first, even, row_up_first, row_even = parities()
    base = jnp.where(even, 4 * LANES, 0)
    lane, lane24 = lane_maps()
    lane8 = lax.rem(lane, 8)
    m1 = jnp.where(even, 7, 16)
    m2 = jnp.where(even, 23, 8)
    n0 = jnp.where(even, 15, 0)
    v0 = jnp.where(even, 7, 0)
    low = lane < 64
    half = lax.rem(lane, 64)
    first_part = half < PATCH
    last_part = half >= 64 - PATCH

    def faces(rows):
        edge = [[src[p, rows, tile(t)] for t in (0, 4, 8)] for p in range(2)]
        top = [jnp.where(low, e[0], e[1]) for e in edge]
        bot = [jnp.where(low, e[1], e[2]) for e in edge]
        top = jnp.where(last_part, pltpu.roll(top[0], 40, 1), top[1])
        bot = jnp.where(first_part, pltpu.roll(bot[0], 88, 1), bot[1])
        return jnp.where(up_first, bot, top), jnp.where(up_first, top, bot)

    def squeezed(rows):
        out = []
        for p in range(2):
            tiles = [src[p, rows, pl.ds(pl.multiple_of(base + LANES * t, LANES), LANES)] for t in range(5)]
            out += squeeze_cols(tiles, lane24, m1, m2, n0)
        return out

    def step(k, carry):
        at = [pl.ds(pl.multiple_of(q * QUARTER + k * PATCH, 8), PATCH) for q in range(4)]
        whole = [faces(rows) for rows in at]
        for n, msg in enumerate((face_a, face_b)):
            turned = {d: pltpu.roll(whole[3][n], d, 1) for d in (24, 56, 72, 104)}
            for q in range(3):
                value = whole[q][n]
                for source, to, count in FOLDS[q]:
                    value = jnp.where(jnp.logical_and(lane >= to, lane < to + count), turned[(to - source) % LANES], value)
                msg[at[q], :] = value
        for h in range(2):
            msg = None
            for slot, v in enumerate(squeezed(at[h]) + squeezed(at[h + 2])):
                msg = v if slot == 0 else jnp.where(lane8 == lax.rem(v0 + slot, 8), pltpu.roll(v, slot, 1), msg)
            side[at[h], :] = msg
        return carry

    lax.fori_loop(0, PATCH // 4, step, 0)
    for p in range(2):
        for out, flip in ((down_a, row_up_first), (down_b, jnp.logical_not(row_up_first))):
            out[p] = src[p, pl.ds(pl.multiple_of(jnp.where(flip, SQUARE - PATCH, 0), 8), PATCH), :]
        for a in range(PATCH):
            left = src[p, a * PATCH : a * PATCH + 1, :]
            right = src[p, a * PATCH + PATCH - 1 : a * PATCH + PATCH, :]
            across_a[p, a : a + 1, :] = jnp.where(row_even, right, left)
            across_b[p, a : a + 1, :] = jnp.where(row_even, left, right)
    pack_diag(src, diag)


def pack_diag(src, diag):
    row_id, col_id = place()
    diag[...] = jnp.zeros(diag.shape, F32)

    @pl.when(row_id // 2 == col_id)
    def _():
        odd = row_id % 2
        lane = iota((8, LANES), 1) - iota((8, LANES), 0)
        for t in range(5):
            total = jnp.zeros((8, LANES), F32)
            first = t * LANES - 64 * odd
            for k in range(LANES // 8):
                row = first + 8 * k
                inside = jnp.logical_and(row >= 0, row < SQUARE)
                at = pl.multiple_of(jnp.clip(row, 0, SQUARE - 8), 8)
                value = src[0, pl.ds(at, 8), pl.ds(pl.multiple_of((4 * odd + t) * LANES, LANES), LANES)]
                total = total + jnp.where(jnp.logical_and(lane == 8 * k, inside), value, 0.0)
            diag[pl.ds(4 * odd + t, 1), :] = jnp.sum(total, axis=0, keepdims=True)


def hop_strip(src, q, a, roww, colw):
    sub = iota((8, LANES), 0)
    lane, lane24 = lane_maps((8, LANES))
    here = pl.multiple_of(a * PATCH, 8)
    above = pl.multiple_of(jnp.maximum(a - 1, 0) * PATCH, 8)
    below = pl.multiple_of(jnp.minimum(a + 1, PATCH - 1) * PATCH, 8)
    x = [[src[q, pl.ds(here + 8 * k, 8), tile(t)] for t in range(TILES)] for k in range(3)]
    out = [[None] * TILES for _ in range(3)]
    rw = [[roww[n, pl.ds(here + 8 * k, 8), :] for n in (DN_IN, UP_IN, RT_IN, LF_IN)] for k in range(3)]
    for t in range(TILES):
        fwd = [pltpu.roll(x[k][t], 1, 0) for k in range(3)]
        bwd = [pltpu.roll(x[k][t], 7, 0) for k in range(3)]
        for k in range(3):
            left = fwd[0] if k == 0 else jnp.where(sub == 0, fwd[k - 1], fwd[k])
            right = bwd[2] if k == 2 else jnp.where(sub == 7, bwd[k + 1], bwd[k])
            dn, up, rt, lf = rw[k]
            out[k][t] = (
                dn * src[q, pl.ds(below + 8 * k, 8), tile(t)]
                + up * src[q, pl.ds(above + 8 * k, 8), tile(t)]
                + rt * right
                + lf * left
            )
    for k in range(3):
        row = x[k]
        r1 = [pltpu.roll(v, 1, 1) for v in row]
        l1 = [pltpu.roll(v, LANES - 1, 1) for v in row]
        r24 = [pltpu.roll(v, PATCH, 1) for v in row]
        l24 = [pltpu.roll(v, LANES - PATCH, 1) for v in row]
        te, tf = [pltpu.roll(v, 41, 1) for v in squeeze_cols(row[0:5], lane24, 15, 7, 23)]
        he, hf = [pltpu.roll(v, 87, 1) for v in squeeze_cols(row[4:9], lane24, 8, 0, 16)]
        for t in range(TILES):
            w = lambda n: colw[n, :, tile(t)]
            minus_b = r1[t] if t == 0 else jnp.where(lane < 1, r1[t - 1], r1[t])
            plus_b = l1[t] if t == TILES - 1 else jnp.where(lane >= LANES - 1, l1[t + 1], l1[t])
            minus_a = r24[t] if t == 0 else jnp.where(lane < PATCH, r24[t - 1], r24[t])
            plus_a = l24[t] if t == TILES - 1 else jnp.where(lane >= LANES - PATCH, l24[t + 1], l24[t])
            acc = out[k][t] + w(C_DN) * plus_a + w(C_UP) * minus_a + w(C_RT) * plus_b + w(C_LF) * minus_b
            if t <= 3:
                acc = acc + w(C_RT_E) * he
            if t in (0, 3, 4):
                acc = acc + w(C_RT_F) * hf
            if 5 <= t <= 8:
                acc = acc + w(C_LF_E) * te
            if t in (4, 5, 8):
                acc = acc + w(C_LF_F) * tf
            out[k][t] = acc
    return out


def interior_kernel(final, first, last, *refs):
    y1, y, roww, colw, out = refs[-5:]

    def step(a, carry):
        here = pl.multiple_of(a * PATCH, 8)
        for p in range(2):
            hops = hop_strip(y1, 1 - p, a, roww, colw)
            for k in range(3):
                rows = pl.ds(here + 8 * k, 8)
                for t in range(TILES):
                    old = y1[p, rows, tile(t)]
                    if final:
                        old = old + y[p, rows, tile(t)]
                    new = old + hops[k][t] if p == 0 else old - hops[k][t]
                    out[p, rows, tile(t)] = 0.5 * new if final else new
        return carry

    lax.fori_loop(first, last, step, 0)


def unfolded(msg, at, lane):
    value = None
    for q in range(3):
        carrier = msg[pl.ds(pl.multiple_of(q * QUARTER + at, 8), 8), :]
        for source, to, count in FOLDS[q]:
            turned = pltpu.roll(carrier, (source - to) % LANES, 1)
            inside = jnp.logical_and(lane >= source, lane < source + count)
            value = turned if value is None else jnp.where(inside, turned, value)
    return value


def finish(scale, base, y, halos, roww, colw, out, e_row, e_col, chunk_done=None):
    face_a, face_b, side, down_a, down_b, across_a, across_b, col_diag, row_diag = halos
    row_id, col_id = place()
    up_first, even, row_up_first, row_even = parities()
    row_odd = lax.rem(row_id, 2)
    shift = jnp.where(even, 87, 41)
    lane = iota((8, LANES), 1)
    for t in range(5):
        strip = jnp.where(row_odd == 1, row_diag[4 + t : 5 + t, :], row_diag[t : t + 1, :])
        e_row[t * LANES : (t + 1) * LANES, :] = jnp.broadcast_to(strip, (LANES, LANES)).T
    for t in range(TILES):
        e_col[:, tile(t)] = col_diag[t : t + 1, :] * colw[COL_U, :, tile(t)]

    def strip(a, folded):
        here = pl.multiple_of(a * PATCH, 8)
        near = pl.ds(pl.multiple_of(8 * (a // 8), 8), 8)
        to_first = lax.rem(8 - lax.rem(a, 8), 8)
        to_last = 7 - lax.rem(a, 8)
        half = a // (PATCH // 2)
        for k in range(3):
            rows = pl.ds(here + 8 * k, 8)
            es = e_row[pl.ds(64 * row_odd + here + 8 * k, 8), :] * roww[ROW_U, rows, :]
            if folded:
                got = [unfolded(m, here - 3 * QUARTER + 8 * k, lane) for m in (face_a, face_b)]
            else:
                got = [m[rows, :] for m in (face_a, face_b)]
            lower = jnp.where(up_first, got[0], got[1])
            upper = jnp.where(up_first, got[1], got[0])
            lowers = (lower, pltpu.roll(lower, 40, 1))
            uppers = (upper, pltpu.roll(upper, 88, 1))
            packed = side[pl.ds(pl.multiple_of(here - half * (SQUARE // 2), 8) + 8 * k, 8), :]
            gaps = [es - e_col[:, tile(t)] for t in range(TILES)]
            for p in range(2):
                q = 1 - p
                se, sf = [pltpu.roll(packed, lax.rem(shift + LANES - (4 * half + 2 * q + n), LANES), 1) for n in range(2)]
                for t in range(TILES):
                    w = lambda n: colw[n, :, tile(t)]
                    acc = gaps[t] * y[q, rows, tile(t)]
                    if t in (0, 4):
                        acc = acc + w(C_UP_RIM) * uppers[q]
                    if t in (4, 8):
                        acc = acc + w(C_DN_RIM) * lowers[q]
                    if t != 4:
                        acc = acc + w(C_X_E) * se
                    if t in (0, 3, 4, 5, 8):
                        acc = acc + w(C_X_F) * sf
                    if k != 1:
                        pair = [m[q, near, tile(t)] for m in (across_a, across_b)]
                    if k == 0:
                        left = pltpu.roll(jnp.where(row_even, pair[1], pair[0]), to_first, 0)
                        acc = acc + roww[LF_RIM, rows, :] * left
                    if k == 2:
                        right = pltpu.roll(jnp.where(row_even, pair[0], pair[1]), to_last, 0)
                        acc = acc + roww[RT_RIM, rows, :] * right
                    if scale != 1.0:
                        acc = scale * acc
                    old = base[p, rows, tile(t)]
                    out[p, rows, tile(t)] = old + acc if p == 0 else old - acc

    def rim(a, weight, first, second):
        for p in range(2):
            for k in range(3):
                rows = pl.ds(a * PATCH + 8 * k, 8)
                w = roww[weight, rows, :] * (scale if p == 0 else -scale)
                for t in range(TILES):
                    pair = [m[1 - p, 8 * k : 8 * k + 8, tile(t)] for m in (first, second)]
                    out[p, rows, tile(t)] += w * jnp.where(row_up_first, pair[0], pair[1])

    fold = 3 * PATCH // 4
    lax.fori_loop(0, fold, lambda a, c: (strip(a, False), c)[1], 0)
    rim(0, UP_RIM, down_b, down_a)
    if chunk_done is not None:
        chunk_done(0, fold * PATCH)
    lax.fori_loop(fold, PATCH, lambda a, c: (strip(a, True), c)[1], 0)
    rim(PATCH - 1, DN_RIM, down_a, down_b)
    if chunk_done is not None:
        chunk_done(fold * PATCH, SQUARE)


def middle_kernel(base, y, *refs):
    halos, (roww, colw), (y1, *faces), (e_row, e_col) = refs[:9], refs[9:11], refs[11:20], refs[20:]
    finish(1.0, base, y, halos, roww, colw, y1, e_row, e_col)
    pack_faces(y1, *faces)


def last_kernel(base, y1, *refs):
    halos, (roww, colw), out_hbm, (e_row, e_col, out, sems) = refs[:9], refs[9:11], refs[11], refs[12:]
    copies = []

    def chunk_done(first, last):
        for p in range(2):
            rows = pl.ds(first, last - first)
            copies.append(pltpu.make_async_copy(out.at[p, rows], out_hbm.at[p, rows], sems.at[len(copies)]))
            copies[-1].start()

    finish(0.5, base, y1, halos, roww, colw, out, e_row, e_col, chunk_done)
    for c in copies:
        c.wait()


def on_chip(*shape):
    return pltpu.VMEM(shape, F32)


VM = pl.BlockSpec(memory_space=pltpu.VMEM)
STATE = (2, SQUARE, COLUMNS)
FACES = (((3 * QUARTER, LANES),) * 2 + ((SQUARE // 2, LANES),) + ((2, PATCH, COLUMNS),) * 4 + ((16, LANES),))


def call(kernel, args, out_shapes, scratch=(), flops=1000, out_specs=None, aliases=None):
    many = isinstance(out_shapes, (list, tuple))
    return pl.pallas_call(
        kernel,
        out_shape=out_shapes,
        in_specs=[VM] * len(args),
        out_specs=out_specs or ([VM] * len(out_shapes) if many else VM),
        scratch_shapes=list(scratch),
        input_output_aliases=aliases or {},
        compiler_params=pltpu.CompilerParams(vmem_limit_bytes=VMEM_LIMIT),
        cost_estimate=pl.CostEstimate(flops=flops, bytes_accessed=1000, transcendentals=0),
    )(*[pltpu.with_memory_space_constraint(x, pltpu.VMEM) for x in args])


def pairs(axis, linked):
    n = lax.axis_size(axis)
    found = [(i, j) for i in range(n) for j in range(i + 1, n) if linked(i, j)]
    return found + [(j, i) for i, j in found]


def traded(block, axis, linked):
    return lax.ppermute(block, axis, pairs(axis, linked))


def flipped(block, axis, bit):
    return traded(block, axis, lambda i, j: j == i ^ bit)


def tie(value, *after):
    def kernel(*refs):
        refs[-1][...] = refs[0][...]

    return call(kernel, (value, *after), on_chip(*value.shape), flops=0)


def exchange(faces, piece):
    face_a, face_b, side, down_a, down_b, across_a, across_b, diag = faces
    face_a = flipped(face_a, "col", 2)
    face_b = traded(face_b, "col", lambda i, j: j == i + 2 and (i // 2) % 2 == 1)
    side = flipped(side, "col", 1)
    down_a = flipped(down_a, "row", 4)
    down_b = traded(down_b, "row", lambda i, j: j == i + 4 and (i // 4) % 2 == 1)
    col_diag = diag + flipped(diag, "row", 4)
    row_diag = diag + flipped(diag, "col", 4)
    part = piece(0, None)
    col_diag = tie(col_diag, part)
    col_got = flipped(col_diag, "row", 8)
    part = piece(1, part, col_diag, row_diag)
    col_diag = tie(col_diag + col_got, part, side)
    col_got = flipped(col_diag, "row", 1)
    part = piece(2, part, col_diag)
    across_a = flipped(tie(across_a, part), "row", 1)
    across_b = traded(tie(across_b, part), "row", lambda i, j: j == i + 1 and i % 4 == 1)
    col_diag = tie(col_diag + col_got, part)
    col_diag = col_diag + flipped(col_diag, "row", 2)
    row_diag = tie(row_diag, face_a, face_b, part)
    row_got = flipped(row_diag, "col", 1)
    part = piece(3, part, row_diag)
    row_diag = row_diag + row_got
    row_diag = row_diag + flipped(row_diag, "col", 2)
    return part, (face_a, face_b, side, down_a, down_b, across_a, across_b, col_diag, row_diag)


PIECES = 4


def interior(final, y1, y, weights):
    def piece(n, part, *after):
        step = PATCH // PIECES
        kernel = functools.partial(interior_kernel, final, n * step, (n + 1) * step)
        args = (*after, y1, y, *weights)
        if n == 0:
            return call(kernel, args, on_chip(*STATE))
        return call(kernel, (part, *args), on_chip(*STATE), aliases={0: 0})

    return piece


def local(corr, bonds_down, bonds_across, repulsion):
    faces_out = [on_chip(*s) for s in FACES]
    e_scratch = [pltpu.VMEM((5 * LANES, LANES), F32), pltpu.VMEM((8, COLUMNS), F32)]
    weights = call(
        weights_kernel,
        (bonds_down, bonds_across, repulsion),
        [on_chip(9, SQUARE, LANES), on_chip(13, 8, COLUMNS)],
    )
    faces = call(pack_faces, (corr,), faces_out)
    part, halos = exchange(faces, interior(False, corr, corr, weights))
    y1, *faces = call(middle_kernel, (part, corr, *halos, *weights), [on_chip(*STATE), *faces_out], e_scratch)
    part, halos = exchange(faces, interior(True, y1, corr, weights))
    return call(
        last_kernel,
        (part, y1, *halos, *weights),
        jax.ShapeDtypeStruct(STATE, F32),
        [*e_scratch, pltpu.VMEM(STATE, F32), pltpu.SemaphoreType.DMA((4,))],
        out_specs=pl.BlockSpec(memory_space=pl.ANY),
    )


def solution(mesh):
    in_specs = (P(None, "row", "col"), P(), P(), P())
    out_specs = P(None, "row", "col")
    return jax.shard_map(local, mesh=mesh, in_specs=in_specs, out_specs=out_specs, check_vma=False)
```

```python
import functools

import jax
import jax.numpy as jnp
from jax import lax
from jax.experimental import pallas as pl
from jax.experimental.pallas import tpu as pltpu
from jax.sharding import PartitionSpec as P

PATCH = 24
SQUARE = PATCH * PATCH
COLUMNS = 2 * SQUARE
LANES = 128
TILES = COLUMNS // LANES
LATTICE = 4 * PATCH
TIME_STEP = 0.04
F32 = jnp.float32
VMEM_LIMIT = 8 * 1024 * 1024

DN_IN, UP_IN, RT_IN, LF_IN, DN_RIM, UP_RIM, RT_RIM, LF_RIM, ROW_U = range(9)
C_DN, C_UP, C_RT, C_LF, C_DN_RIM, C_UP_RIM, C_RT_E, C_RT_F, C_LF_E, C_LF_F, C_X_E, C_X_F, COL_U, C_DN_ALL, C_UP_ALL, C_RT_ALL, C_LF_ALL = range(17)


def iota(shape, dim):
    return lax.broadcasted_iota(jnp.int32, shape, dim)


def over24(x):
    return ((x.astype(F32) + 0.5) * (1.0 / PATCH)).astype(jnp.int32)


def on(mask):
    return jnp.where(mask, 1.0, 0.0).astype(F32)


def within(x, lo, hi):
    return on(x >= lo) * on(x <= hi)


def place():
    return lax.axis_index("row"), lax.axis_index("col")


def tile(t):
    return pl.ds(t * LANES, LANES)


def weights(bonds, roww, colw):
    row_id, col_id = place()
    side = (LATTICE, LATTICE)
    down = jnp.where(iota(side, 0) < LATTICE - 1, bonds[0], 0.0)
    across = jnp.where(iota(side, 1) < LATTICE - 1, bonds[1], 0.0)
    rep = bonds[2]
    dot = functools.partial(jnp.dot, precision=lax.Precision.HIGHEST, preferred_element_type=F32)

    s = iota((SQUARE, LATTICE), 0)
    lane = iota((SQUARE, LATTICE), 1)
    a = over24(s)
    b = s - PATCH * a
    ga = PATCH * (row_id // 4) + a
    gb = PATCH * (row_id % 4) + b

    def pick_rows(table, da, db):
        rows = dot(on(lane == ga + da), table)
        return jnp.sum(jnp.where(lane == gb + db, rows, 0.0), axis=1, keepdims=True)

    a1 = a[:, 0:1]
    b1 = b[:, 0:1]
    last = PATCH - 1
    dn = -TIME_STEP * pick_rows(down, 0, 0)
    up = -TIME_STEP * pick_rows(down, -1, 0)
    rt = -TIME_STEP * pick_rows(across, 0, 0)
    lf = -TIME_STEP * pick_rows(across, 0, -1)
    values = {
        DN_IN: dn * on(a1 < last), UP_IN: up * on(a1 > 0), RT_IN: rt * on(b1 < last), LF_IN: lf * on(b1 > 0),
        DN_RIM: dn * on(a1 == last), UP_RIM: up * on(a1 == 0), RT_RIM: rt * on(b1 == last), LF_RIM: lf * on(b1 == 0),
        ROW_U: TIME_STEP * pick_rows(rep, 0, 0),
    }
    for k, v in values.items():
        roww[k] = jnp.broadcast_to(v, (SQUARE, LANES))

    wide = (LATTICE, COLUMNS)
    j = iota(wide, 1)
    g = (j >= SQUARE).astype(jnp.int32)
    jj = j - SQUARE * g
    a = over24(jj)
    b = jj - PATCH * a
    sub = iota(wide, 0)
    parity = col_id % 2
    ga = PATCH * (col_id // 2) + a
    gb = PATCH * (2 * parity + g) + b

    def pick_cols(table, da, db):
        cols = dot(table, on(sub == gb + db))
        return jnp.sum(jnp.where(sub == ga + da, cols, 0.0), axis=0, keepdims=True)

    a = a[0:1]
    b = b[0:1]
    g = g[0:1]
    dn = TIME_STEP * pick_cols(down, 0, 0)
    up = TIME_STEP * pick_cols(down, -1, 0)
    rt = TIME_STEP * pick_cols(across, 0, 0)
    lf = TIME_STEP * pick_cols(across, 0, -1)
    tails0 = rt * on(b == last) * on(g == 0)
    heads1 = lf * on(b == 0) * on(g == 1)
    tails1 = rt * on(b == last) * on(g == 1)
    heads0 = lf * on(b == 0) * on(g == 0)
    even = on(jnp.full(a.shape, parity, jnp.int32) == 0)
    x_even = even * tails1
    x_odd = (1.0 - even) * heads0
    rt_e = within(a, 3, 18)
    lf_e = within(a, 5, 20)
    xe_e = within(a, 6, 21)
    xo_e = within(a, 2, 17)
    values = {
        C_DN: dn * on(a < last), C_UP: up * on(a > 0), C_RT: rt * on(b < last), C_LF: lf * on(b > 0),
        C_DN_RIM: dn * on(a == last), C_UP_RIM: up * on(a == 0),
        C_RT_E: tails0 * rt_e, C_RT_F: tails0 * (1.0 - rt_e),
        C_LF_E: heads1 * lf_e, C_LF_F: heads1 * (1.0 - lf_e),
        C_X_E: x_even * xe_e + x_odd * xo_e, C_X_F: x_even * (1.0 - xe_e) + x_odd * (1.0 - xo_e),
        COL_U: TIME_STEP * pick_cols(rep, 0, 0),
        C_DN_ALL: dn, C_UP_ALL: up, C_RT_ALL: rt, C_LF_ALL: lf,
    }
    for k, v in values.items():
        colw[k] = jnp.broadcast_to(v, (8, COLUMNS))


STRIP = (PATCH, LANES)


def squeeze_cols(tiles, lane24, m1, m2, n0):
    e = jnp.where(lane24 == m1, tiles[1], jnp.where(lane24 == m2, tiles[2], tiles[3]))
    f = jnp.where(lane24 == n0, tiles[0], tiles[4])
    return e, f


def lane_maps(shape=STRIP):
    lane = iota(shape, 1)
    return lane, lane - PATCH * over24(lane)


def parities():
    row_id, col_id = place()
    return lax.rem(col_id // 2, 2) == 0, lax.rem(col_id, 2) == 0, lax.rem(row_id // 4, 2) == 0, lax.rem(row_id, 2) == 0


FOLDS = (((0, 24, 16), (16, 88, 8), (40, 96, 8)), ((48, 24, 16), (64, 88, 16)), ((80, 24, 8), (104, 32, 8), (112, 88, 16)))
QUARTER = SQUARE // 4


def pack_faces(src, face_a, face_b, side, down_a, down_b, across_a, across_b):
    up_first, even, row_up_first, row_even = parities()
    base = jnp.where(even, 4 * LANES, 0)
    lane, lane24 = lane_maps()
    lane8 = lax.rem(lane, 8)
    m1 = jnp.where(even, 7, 16)
    m2 = jnp.where(even, 23, 8)
    n0 = jnp.where(even, 15, 0)
    v0 = jnp.where(even, 7, 0)
    low = lane < 64
    half = lax.rem(lane, 64)
    first_part = half < PATCH
    last_part = half >= 64 - PATCH

    def faces(rows):
        edge = [[src[p, rows, tile(t)] for t in (0, 4, 8)] for p in range(2)]
        top = [jnp.where(low, e[0], e[1]) for e in edge]
        bot = [jnp.where(low, e[1], e[2]) for e in edge]
        top = jnp.where(last_part, pltpu.roll(top[0], 40, 1), top[1])
        bot = jnp.where(first_part, pltpu.roll(bot[0], 88, 1), bot[1])
        return jnp.where(up_first, bot, top), jnp.where(up_first, top, bot)

    def squeezed(rows):
        out = []
        for p in range(2):
            tiles = [src[p, rows, pl.ds(pl.multiple_of(base + LANES * t, LANES), LANES)] for t in range(5)]
            out += squeeze_cols(tiles, lane24, m1, m2, n0)
        return out

    def step(k, carry):
        at = [pl.ds(pl.multiple_of(q * QUARTER + k * PATCH, 8), PATCH) for q in range(4)]
        whole = [faces(rows) for rows in at]
        for n, msg in enumerate((face_a, face_b)):
            turned = {d: pltpu.roll(whole[3][n], d, 1) for d in (24, 56, 72, 104)}
            for q in range(3):
                value = whole[q][n]
                for source, to, count in FOLDS[q]:
                    value = jnp.where(jnp.logical_and(lane >= to, lane < to + count), turned[(to - source) % LANES], value)
                msg[at[q], :] = value
        for h in range(2):
            msg = None
            for slot, v in enumerate(squeezed(at[h]) + squeezed(at[h + 2])):
                msg = v if slot == 0 else jnp.where(lane8 == lax.rem(v0 + slot, 8), pltpu.roll(v, slot, 1), msg)
            side[at[h], :] = msg
        return carry

    lax.fori_loop(0, PATCH // 4, step, 0)
    for p in range(2):
        for out, flip in ((down_a, row_up_first), (down_b, jnp.logical_not(row_up_first))):
            out[p] = src[p, pl.ds(pl.multiple_of(jnp.where(flip, SQUARE - PATCH, 0), 8), PATCH), :]
        for a in range(PATCH):
            left = src[p, a * PATCH : a * PATCH + 1, :]
            right = src[p, a * PATCH + PATCH - 1 : a * PATCH + PATCH, :]
            across_a[p, a : a + 1, :] = jnp.where(row_even, right, left)
            across_b[p, a : a + 1, :] = jnp.where(row_even, left, right)


SLOT = 24


def pack_densities(src, colw, table, row_sums, slots):
    row_id, col_id = place()
    odd = lax.rem(row_id, 2)
    across = lax.rem(row_id, 4) - 2 * lax.rem(col_id, 2)
    along = row_id // 4 - col_id // 2
    beside = jnp.logical_and(along == 0, jnp.logical_and(across >= -1, across <= 2))
    over = jnp.logical_and(jnp.abs(along) == 1, jnp.logical_and(across >= 0, across <= 1))
    table[...] = jnp.zeros(table.shape, F32)

    @pl.when(jnp.logical_or(beside, over))
    def _():
        slots[...] = jnp.zeros(slots.shape, F32)
        row_sums[...] = jnp.zeros(row_sums.shape, F32)
        lane = iota((8, LANES), 1)
        sub = iota((8, LANES), 0)
        codes = []
        for t in range(TILES):
            j = lane + t * LANES
            g = (j >= SQUARE).astype(jnp.int32)
            a = over24(j - SQUARE * g)
            b = j - SQUARE * g - PATCH * a
            codes.append(100 * (PATCH * (col_id // 2) + a) + PATCH * (2 * lax.rem(col_id, 2) + g) + b)
        first = 100 * PATCH * (row_id // 4) + PATCH * lax.rem(row_id, 4)

        def step(a, sums):
            sums = list(sums)
            for k in range(3):
                here = pl.multiple_of(a * PATCH + 8 * k, 8)
                mine = first + 100 * a + 8 * k + sub
                along_row = None
                for t in range(TILES):
                    apart = mine - codes[t]
                    w = jnp.where(apart == 100, colw[C_DN_ALL, :, tile(t)], 0.0)
                    w = jnp.where(apart == -100, colw[C_UP_ALL, :, tile(t)], w)
                    w = jnp.where(apart == 1, colw[C_RT_ALL, :, tile(t)], w)
                    w = jnp.where(apart == -1, colw[C_LF_ALL, :, tile(t)], w)
                    flow = w * src[1, pl.ds(here, 8), tile(t)]
                    sums[t] = sums[t] - flow + jnp.where(apart == 0, src[0, pl.ds(here, 8), tile(t)], 0.0)
                    sums[TILES + t] = sums[TILES + t] + jnp.where(apart == 0, src[0, pl.ds(here, 8), tile(t)], 0.0)
                    along_row = flow if along_row is None else along_row + flow
                row_sums[pl.ds(64 * odd + here, 8), :] = along_row
            return tuple(sums)

        sums = lax.fori_loop(0, PATCH, step, (jnp.zeros((8, LANES), F32),) * (2 * TILES))
        for t in range(TILES):
            slots[0, t : t + 1, :] = jnp.sum(sums[TILES + t], axis=0, keepdims=True)
            slots[0, TILES + t : TILES + t + 1, :] = jnp.sum(sums[t], axis=0, keepdims=True)
        for t in range(5):
            got = jnp.sum(row_sums[t * LANES : (t + 1) * LANES, :].T, axis=0, keepdims=True)
            slots[1, pl.ds(TILES + 4 * odd + t, 1), :] = got
        table[pl.ds(pl.multiple_of(SLOT * col_id, 8), SLOT), :] = slots[0]
        table[pl.ds(pl.multiple_of(SLOT * (row_id // 2), 8), SLOT), :] += slots[1]


def first_kernel(corr, down, across, rep, y, roww, colw, *refs):
    faces, table, (row_sums, slots, bonds, sems) = refs[:7], refs[7], refs[8:]
    copies = [pltpu.make_async_copy(v, bonds.at[n], sems.at[n]) for n, v in enumerate((down, across, rep))]
    copies += [pltpu.make_async_copy(corr.at[p], y.at[p], sems.at[3 + p]) for p in range(2)]
    for c in copies:
        c.start()
    for c in copies[:3]:
        c.wait()
    weights(bonds, roww, colw)
    for c in copies[3:]:
        c.wait()
    pack_faces(y, *faces)
    pack_densities(y, colw, table, row_sums, slots)


def hop_strip(src, q, a, roww, colw):
    sub = iota((8, LANES), 0)
    lane, lane24 = lane_maps((8, LANES))
    here = pl.multiple_of(a * PATCH, 8)
    above = pl.multiple_of(jnp.maximum(a - 1, 0) * PATCH, 8)
    below = pl.multiple_of(jnp.minimum(a + 1, PATCH - 1) * PATCH, 8)
    x = [[src[q, pl.ds(here + 8 * k, 8), tile(t)] for t in range(TILES)] for k in range(3)]
    out = [[None] * TILES for _ in range(3)]
    rw = [[roww[n, pl.ds(here + 8 * k, 8), :] for n in (DN_IN, UP_IN, RT_IN, LF_IN)] for k in range(3)]
    for t in range(TILES):
        fwd = [pltpu.roll(x[k][t], 1, 0) for k in range(3)]
        bwd = [pltpu.roll(x[k][t], 7, 0) for k in range(3)]
        for k in range(3):
            left = fwd[0] if k == 0 else jnp.where(sub == 0, fwd[k - 1], fwd[k])
            right = bwd[2] if k == 2 else jnp.where(sub == 7, bwd[k + 1], bwd[k])
            dn, up, rt, lf = rw[k]
            out[k][t] = (
                dn * src[q, pl.ds(below + 8 * k, 8), tile(t)]
                + up * src[q, pl.ds(above + 8 * k, 8), tile(t)]
                + rt * right
                + lf * left
            )
    for k in range(3):
        row = x[k]
        r1 = [pltpu.roll(v, 1, 1) for v in row]
        l1 = [pltpu.roll(v, LANES - 1, 1) for v in row]
        r24 = [pltpu.roll(v, PATCH, 1) for v in row]
        l24 = [pltpu.roll(v, LANES - PATCH, 1) for v in row]
        te, tf = [pltpu.roll(v, 41, 1) for v in squeeze_cols(row[0:5], lane24, 15, 7, 23)]
        he, hf = [pltpu.roll(v, 87, 1) for v in squeeze_cols(row[4:9], lane24, 8, 0, 16)]
        for t in range(TILES):
            w = lambda n: colw[n, :, tile(t)]
            minus_b = r1[t] if t == 0 else jnp.where(lane < 1, r1[t - 1], r1[t])
            plus_b = l1[t] if t == TILES - 1 else jnp.where(lane >= LANES - 1, l1[t + 1], l1[t])
            minus_a = r24[t] if t == 0 else jnp.where(lane < PATCH, r24[t - 1], r24[t])
            plus_a = l24[t] if t == TILES - 1 else jnp.where(lane >= LANES - PATCH, l24[t + 1], l24[t])
            acc = out[k][t] + w(C_DN) * plus_a + w(C_UP) * minus_a + w(C_RT) * plus_b + w(C_LF) * minus_b
            if t <= 3:
                acc = acc + w(C_RT_E) * he
            if t in (0, 3, 4):
                acc = acc + w(C_RT_F) * hf
            if 5 <= t <= 8:
                acc = acc + w(C_LF_E) * te
            if t in (4, 5, 8):
                acc = acc + w(C_LF_F) * tf
            out[k][t] = acc
    return out


def interior_kernel(final, first, last, *refs):
    y1, y, roww, colw, out = refs[-5:]

    def step(a, carry):
        here = pl.multiple_of(a * PATCH, 8)
        for p in range(2):
            hops = hop_strip(y1, 1 - p, a, roww, colw)
            for k in range(3):
                rows = pl.ds(here + 8 * k, 8)
                for t in range(TILES):
                    old = y1[p, rows, tile(t)]
                    if final:
                        old = old + y[p, rows, tile(t)]
                    new = old + hops[k][t] if p == 0 else old - hops[k][t]
                    out[p, rows, tile(t)] = 0.5 * new if final else new
        return carry

    lax.fori_loop(first, last, step, 0)


def unfolded(msg, at, lane):
    value = None
    for q in range(3):
        carrier = msg[pl.ds(pl.multiple_of(q * QUARTER + at, 8), 8), :]
        for source, to, count in FOLDS[q]:
            turned = pltpu.roll(carrier, (source - to) % LANES, 1)
            inside = jnp.logical_and(lane >= source, lane < source + count)
            value = turned if value is None else jnp.where(inside, turned, value)
    return value


def finish(stage, base, y, halos, roww, colw, out, e_row, e_col, chunk_done=None):
    face_a, face_b, side, down_a, down_b, across_a, across_b, table = halos
    scale = 0.5 if stage else 1.0
    row_id, col_id = place()
    up_first, even, row_up_first, row_even = parities()
    row_odd = lax.rem(row_id, 2)
    shift = jnp.where(even, 87, 41)
    lane = iota((8, LANES), 1)
    row_slot = table[pl.ds(pl.multiple_of(SLOT * (row_id // 2), 8), SLOT), :]
    col_slot = table[pl.ds(pl.multiple_of(SLOT * col_id, 8), SLOT), :]
    for t in range(5):
        u = stage * TILES + t
        strip = jnp.where(row_odd == 1, row_slot[4 + u : 5 + u, :], row_slot[u : u + 1, :])
        e_row[t * LANES : (t + 1) * LANES, :] = jnp.broadcast_to(strip, (LANES, LANES)).T
    for t in range(TILES):
        e_col[:, tile(t)] = col_slot[stage * TILES + t : stage * TILES + t + 1, :] * colw[COL_U, :, tile(t)]

    def strip(a, folded):
        here = pl.multiple_of(a * PATCH, 8)
        near = pl.ds(pl.multiple_of(8 * (a // 8), 8), 8)
        to_first = lax.rem(8 - lax.rem(a, 8), 8)
        to_last = 7 - lax.rem(a, 8)
        half = a // (PATCH // 2)
        for k in range(3):
            rows = pl.ds(here + 8 * k, 8)
            es = e_row[pl.ds(64 * row_odd + here + 8 * k, 8), :] * roww[ROW_U, rows, :]
            if folded:
                got = [unfolded(m, here - 3 * QUARTER + 8 * k, lane) for m in (face_a, face_b)]
            else:
                got = [m[rows, :] for m in (face_a, face_b)]
            lower = jnp.where(up_first, got[0], got[1])
            upper = jnp.where(up_first, got[1], got[0])
            lowers = (lower, pltpu.roll(lower, 40, 1))
            uppers = (upper, pltpu.roll(upper, 88, 1))
            packed = side[pl.ds(pl.multiple_of(here - half * (SQUARE // 2), 8) + 8 * k, 8), :]
            gaps = [es - e_col[:, tile(t)] for t in range(TILES)]
            for p in range(2):
                q = 1 - p
                se, sf = [pltpu.roll(packed, lax.rem(shift + LANES - (4 * half + 2 * q + n), LANES), 1) for n in range(2)]
                for t in range(TILES):
                    w = lambda n: colw[n, :, tile(t)]
                    acc = gaps[t] * y[q, rows, tile(t)]
                    if t in (0, 4):
                        acc = acc + w(C_UP_RIM) * uppers[q]
                    if t in (4, 8):
                        acc = acc + w(C_DN_RIM) * lowers[q]
                    if t != 4:
                        acc = acc + w(C_X_E) * se
                    if t in (0, 3, 4, 5, 8):
                        acc = acc + w(C_X_F) * sf
                    if k != 1:
                        pair = [m[q, near, tile(t)] for m in (across_a, across_b)]
                    if k == 0:
                        left = pltpu.roll(jnp.where(row_even, pair[1], pair[0]), to_first, 0)
                        acc = acc + roww[LF_RIM, rows, :] * left
                    if k == 2:
                        right = pltpu.roll(jnp.where(row_even, pair[0], pair[1]), to_last, 0)
                        acc = acc + roww[RT_RIM, rows, :] * right
                    if scale != 1.0:
                        acc = scale * acc
                    old = base[p, rows, tile(t)]
                    out[p, rows, tile(t)] = old + acc if p == 0 else old - acc

    def rim(a, weight, first, second):
        for p in range(2):
            for k in range(3):
                rows = pl.ds(a * PATCH + 8 * k, 8)
                w = roww[weight, rows, :] * (scale if p == 0 else -scale)
                for t in range(TILES):
                    pair = [m[1 - p, 8 * k : 8 * k + 8, tile(t)] for m in (first, second)]
                    out[p, rows, tile(t)] += w * jnp.where(row_up_first, pair[0], pair[1])

    fold = 3 * PATCH // 4
    lax.fori_loop(0, fold, lambda a, c: (strip(a, False), c)[1], 0)
    rim(0, UP_RIM, down_b, down_a)
    if chunk_done is not None:
        chunk_done(0, fold * PATCH)
    lax.fori_loop(fold, PATCH, lambda a, c: (strip(a, True), c)[1], 0)
    rim(PATCH - 1, DN_RIM, down_a, down_b)
    if chunk_done is not None:
        chunk_done(fold * PATCH, SQUARE)


def middle_kernel(base, y, *refs):
    halos, (roww, colw), (y1, *faces), (e_row, e_col) = refs[:8], refs[8:10], refs[10:18], refs[18:]
    finish(0, base, y, halos, roww, colw, y1, e_row, e_col)
    pack_faces(y1, *faces)


def last_kernel(base, y1, *refs):
    halos, (roww, colw), out_hbm, (e_row, e_col, out, sems) = refs[:8], refs[8:10], refs[10], refs[11:]
    copies = []

    def chunk_done(first, last):
        for p in range(2):
            rows = pl.ds(first, last - first)
            copies.append(pltpu.make_async_copy(out.at[p, rows], out_hbm.at[p, rows], sems.at[len(copies)]))
            copies[-1].start()

    finish(1, base, y1, halos, roww, colw, out, e_row, e_col, chunk_done)
    for c in copies:
        c.wait()


def on_chip(*shape):
    return pltpu.VMEM(shape, F32)


VM = pl.BlockSpec(memory_space=pltpu.VMEM)
STATE = (2, SQUARE, COLUMNS)
FACES = ((3 * QUARTER, LANES),) * 2 + ((SQUARE // 2, LANES),) + ((2, PATCH, COLUMNS),) * 4
TABLE = (8 * SLOT, LANES)


def call(kernel, args, out_shapes, scratch=(), out_specs=None, aliases=None, loads=False):
    many = isinstance(out_shapes, (list, tuple))
    return pl.pallas_call(
        kernel,
        out_shape=out_shapes,
        in_specs=[pl.BlockSpec(memory_space=pl.ANY) if loads else VM] * len(args),
        out_specs=out_specs or ([VM] * len(out_shapes) if many else VM),
        scratch_shapes=list(scratch),
        input_output_aliases=aliases or {},
        compiler_params=pltpu.CompilerParams(vmem_limit_bytes=VMEM_LIMIT),
        cost_estimate=pl.CostEstimate(flops=1000, bytes_accessed=1000, transcendentals=0),
    )(*[pltpu.with_memory_space_constraint(x, pltpu.HBM if loads else pltpu.VMEM) for x in args])


def pairs(axis, linked):
    n = lax.axis_size(axis)
    found = [(i, j) for i in range(n) for j in range(i + 1, n) if linked(i, j)]
    return found + [(j, i) for i, j in found]


def traded(block, axis, linked):
    return lax.ppermute(block, axis, pairs(axis, linked))


def flipped(block, axis, bit):
    return traded(block, axis, lambda i, j: j == i ^ bit)


def tie(value, *after):
    def kernel(*refs):
        refs[-1][...] = refs[0][...]

    return call(kernel, (value, *after), on_chip(*value.shape))


def merged(value, got, *after):
    def kernel(*refs):
        refs[-1][...] = refs[0][...] + refs[1][...]

    return call(kernel, (value, got, *after), on_chip(*value.shape))


def swap_face_a(x):
    return flipped(x, "col", 2)


def swap_face_b(x):
    return traded(x, "col", lambda i, j: j == i + 2 and (i // 2) % 2 == 1)


def swap_side(x):
    return flipped(x, "col", 1)


def swap_down_a(x):
    return flipped(x, "row", 4)


def swap_down_b(x):
    return traded(x, "row", lambda i, j: j == i + 4 and (i // 4) % 2 == 1)


def swap_across_a(x):
    return flipped(x, "row", 1)


def swap_across_b(x):
    return traded(x, "row", lambda i, j: j == i + 1 and i % 4 == 1)


def swap_bits(x, row_bits, col_bits):
    rows, cols = lax.axis_size("row"), lax.axis_size("col")
    route = [(r * cols + c, (r ^ row_bits) * cols + (c ^ col_bits)) for r in range(rows) for c in range(cols)]
    return lax.ppermute(x, ("row", "col"), route)


def first_exchange(faces, table, piece):
    face_a, face_b, side, down_a, down_b, across_a, across_b = faces
    face_a, face_b = swap_face_a(face_a), swap_face_b(face_b)
    got = flipped(table, "row", 4)
    part = piece(0, None)
    table = merged(table, got, part)
    got = flipped(table, "row", 12)
    side = swap_side(tie(side, table))
    down_a = swap_down_a(tie(down_a, table))
    part = piece(1, part, table)
    table = merged(table, got, part)
    got = flipped(table, "row", 1)
    down_b = swap_down_b(tie(down_b, table))
    part = piece(2, part, table)
    table = merged(table, got, part, side, face_a, face_b)
    got = flipped(table, "row", 2)
    across_a = swap_across_a(tie(across_a, table))
    across_b = swap_across_b(tie(across_b, table))
    part = piece(3, part, table)
    table = merged(table, got, part, down_a)
    table = merged(table, swap_bits(table, 2, 4), down_b)
    table = merged(table, flipped(table, "col", 1), across_a)
    table = merged(table, flipped(table, "col", 3), across_b)
    return part, (face_a, face_b, side, down_a, down_b, across_a, across_b, table)


def second_exchange(faces, table, piece):
    face_a, face_b, side, down_a, down_b, across_a, across_b = faces
    face_a, face_b = swap_face_a(face_a), swap_face_b(face_b)
    part = piece(0, None)
    side = swap_side(tie(side, part))
    down_a = swap_down_a(tie(down_a, part))
    down_b = swap_down_b(tie(down_b, part))
    part = piece(1, part)
    part = piece(2, part)
    across_a = swap_across_a(tie(across_a, part))
    across_b = swap_across_b(tie(across_b, part))
    part = piece(3, part, side, down_a, down_b)
    return part, (face_a, face_b, side, down_a, down_b, across_a, across_b, table)


PIECES = 4


def interior(final, y1, y, weights):
    def piece(n, part, *after):
        step = PATCH // PIECES
        kernel = functools.partial(interior_kernel, final, n * step, (n + 1) * step)
        args = (*after, y1, y, *weights)
        if n == 0:
            return call(kernel, args, on_chip(*STATE))
        return call(kernel, (part, *args), on_chip(*STATE), aliases={0: 0})

    return piece


def local(corr, bonds_down, bonds_across, repulsion):
    faces_out = [on_chip(*s) for s in FACES]
    e_scratch = [pltpu.VMEM((5 * LANES, LANES), F32), pltpu.VMEM((8, COLUMNS), F32)]
    y, roww, colw, *faces, table = call(
        first_kernel,
        (corr, bonds_down, bonds_across, repulsion),
        [on_chip(*STATE), on_chip(9, SQUARE, LANES), on_chip(17, 8, COLUMNS), *faces_out, on_chip(*TABLE)],
        [
            pltpu.VMEM((5 * LANES, LANES), F32),
            pltpu.VMEM((2, SLOT, LANES), F32),
            pltpu.VMEM((3, LATTICE, LATTICE), F32),
            pltpu.SemaphoreType.DMA((5,)),
        ],
        loads=True,
    )
    weights = (roww, colw)
    part, halos = first_exchange(faces, table, interior(False, y, y, weights))
    y1, *faces = call(middle_kernel, (part, y, *halos, *weights), [on_chip(*STATE), *faces_out], e_scratch)
    part, halos = second_exchange(faces, halos[-1], interior(True, y1, y, weights))
    return call(
        last_kernel,
        (part, y1, *halos, *weights),
        jax.ShapeDtypeStruct(STATE, F32),
        [*e_scratch, pltpu.VMEM(STATE, F32), pltpu.SemaphoreType.DMA((4,))],
        out_specs=pl.BlockSpec(memory_space=pl.ANY),
    )


def solution(mesh):
    in_specs = (P(None, "row", "col"), P(), P(), P())
    out_specs = P(None, "row", "col")
    return jax.shard_map(local, mesh=mesh, in_specs=in_specs, out_specs=out_specs, check_vma=False)
```

```python
import functools

import jax
import jax.numpy as jnp
from jax import lax
from jax.experimental import pallas as pl
from jax.experimental.pallas import tpu as pltpu
from jax.sharding import PartitionSpec as P

PATCH = 24
SQUARE = PATCH * PATCH
COLUMNS = 2 * SQUARE
LANES = 128
TILES = COLUMNS // LANES
LATTICE = 4 * PATCH
TIME_STEP = 0.04
F32 = jnp.float32
VMEM_LIMIT = 8 * 1024 * 1024

DN_IN, UP_IN, RT_IN, LF_IN, DN_RIM, UP_RIM, RT_RIM, LF_RIM, ROW_U = range(9)
C_DN, C_UP, C_RT, C_LF, C_DN_RIM, C_UP_RIM, C_RT_E, C_RT_F, C_LF_E, C_LF_F, C_X_E, C_X_F, COL_U, C_DN_ALL, C_UP_ALL, C_RT_ALL, C_LF_ALL = range(17)


def iota(shape, dim):
    return lax.broadcasted_iota(jnp.int32, shape, dim)


def over24(x):
    return ((x.astype(F32) + 0.5) * (1.0 / PATCH)).astype(jnp.int32)


def on(mask):
    return jnp.where(mask, 1.0, 0.0).astype(F32)


def within(x, lo, hi):
    return on(x >= lo) * on(x <= hi)


def place():
    return lax.axis_index("row"), lax.axis_index("col")


def tile(t):
    return pl.ds(t * LANES, LANES)


def tables(bonds):
    side = (LATTICE, LATTICE)
    down = jnp.where(iota(side, 0) < LATTICE - 1, bonds[0], 0.0)
    across = jnp.where(iota(side, 1) < LATTICE - 1, bonds[1], 0.0)
    rep = bonds[2]
    dot = functools.partial(jnp.dot, precision=lax.Precision.HIGHEST, preferred_element_type=F32)
    return down, across, rep, dot


def row_weights_kernel(bonds, roww):
    row_id, _ = place()
    down, across, rep, dot = tables(bonds)
    s = iota((SQUARE, LATTICE), 0)
    lane = iota((SQUARE, LATTICE), 1)
    a = over24(s)
    b = s - PATCH * a
    ga = PATCH * (row_id // 4) + a
    gb = PATCH * (row_id % 4) + b

    def pick_rows(table, da, db):
        rows = dot(on(lane == ga + da), table)
        return jnp.sum(jnp.where(lane == gb + db, rows, 0.0), axis=1, keepdims=True)

    a1 = a[:, 0:1]
    b1 = b[:, 0:1]
    last = PATCH - 1
    dn = -TIME_STEP * pick_rows(down, 0, 0)
    up = -TIME_STEP * pick_rows(down, -1, 0)
    rt = -TIME_STEP * pick_rows(across, 0, 0)
    lf = -TIME_STEP * pick_rows(across, 0, -1)
    values = {
        DN_IN: dn * on(a1 < last), UP_IN: up * on(a1 > 0), RT_IN: rt * on(b1 < last), LF_IN: lf * on(b1 > 0),
        DN_RIM: dn * on(a1 == last), UP_RIM: up * on(a1 == 0), RT_RIM: rt * on(b1 == last), LF_RIM: lf * on(b1 == 0),
        ROW_U: TIME_STEP * pick_rows(rep, 0, 0),
    }
    for k, v in values.items():
        roww[k] = jnp.broadcast_to(v, (SQUARE, LANES))


def col_weights(bonds, colw):
    _, col_id = place()
    down, across, rep, dot = tables(bonds)
    last = PATCH - 1
    wide = (LATTICE, COLUMNS)
    j = iota(wide, 1)
    g = (j >= SQUARE).astype(jnp.int32)
    jj = j - SQUARE * g
    a = over24(jj)
    b = jj - PATCH * a
    sub = iota(wide, 0)
    parity = col_id % 2
    ga = PATCH * (col_id // 2) + a
    gb = PATCH * (2 * parity + g) + b

    def pick_cols(table, da, db):
        cols = dot(table, on(sub == gb + db))
        return jnp.sum(jnp.where(sub == ga + da, cols, 0.0), axis=0, keepdims=True)

    a = a[0:1]
    b = b[0:1]
    g = g[0:1]
    dn = TIME_STEP * pick_cols(down, 0, 0)
    up = TIME_STEP * pick_cols(down, -1, 0)
    rt = TIME_STEP * pick_cols(across, 0, 0)
    lf = TIME_STEP * pick_cols(across, 0, -1)
    tails0 = rt * on(b == last) * on(g == 0)
    heads1 = lf * on(b == 0) * on(g == 1)
    tails1 = rt * on(b == last) * on(g == 1)
    heads0 = lf * on(b == 0) * on(g == 0)
    even = on(jnp.full(a.shape, parity, jnp.int32) == 0)
    x_even = even * tails1
    x_odd = (1.0 - even) * heads0
    rt_e = within(a, 3, 18)
    lf_e = within(a, 5, 20)
    xe_e = within(a, 6, 21)
    xo_e = within(a, 2, 17)
    values = {
        C_DN: dn * on(a < last), C_UP: up * on(a > 0), C_RT: rt * on(b < last), C_LF: lf * on(b > 0),
        C_DN_RIM: dn * on(a == last), C_UP_RIM: up * on(a == 0),
        C_RT_E: tails0 * rt_e, C_RT_F: tails0 * (1.0 - rt_e),
        C_LF_E: heads1 * lf_e, C_LF_F: heads1 * (1.0 - lf_e),
        C_X_E: x_even * xe_e + x_odd * xo_e, C_X_F: x_even * (1.0 - xe_e) + x_odd * (1.0 - xo_e),
        COL_U: TIME_STEP * pick_cols(rep, 0, 0),
        C_DN_ALL: dn, C_UP_ALL: up, C_RT_ALL: rt, C_LF_ALL: lf,
    }
    for k, v in values.items():
        colw[k] = jnp.broadcast_to(v, (8, COLUMNS))


STRIP = (PATCH, LANES)


def squeeze_cols(tiles, lane24, m1, m2, n0):
    e = jnp.where(lane24 == m1, tiles[1], jnp.where(lane24 == m2, tiles[2], tiles[3]))
    f = jnp.where(lane24 == n0, tiles[0], tiles[4])
    return e, f


def lane_maps(shape=STRIP):
    lane = iota(shape, 1)
    return lane, lane - PATCH * over24(lane)


def parities():
    row_id, col_id = place()
    return lax.rem(col_id // 2, 2) == 0, lax.rem(col_id, 2) == 0, lax.rem(row_id // 4, 2) == 0, lax.rem(row_id, 2) == 0


FOLDS = (((0, 24, 16), (16, 88, 8), (40, 96, 8)), ((48, 24, 16), (64, 88, 16)), ((80, 24, 8), (104, 32, 8), (112, 88, 16)))
QUARTER = SQUARE // 4


def pack_faces(src, face_a, face_b, side, down_a, down_b, across_a, across_b, ready=None):
    up_first, even, row_up_first, row_even = parities()
    base = jnp.where(even, 4 * LANES, 0)
    lane, lane24 = lane_maps()
    lane8 = lax.rem(lane, 8)
    m1 = jnp.where(even, 7, 16)
    m2 = jnp.where(even, 23, 8)
    n0 = jnp.where(even, 15, 0)
    v0 = jnp.where(even, 7, 0)
    low = lane < 64
    half = lax.rem(lane, 64)
    first_part = half < PATCH
    last_part = half >= 64 - PATCH

    def faces(rows):
        edge = [[src[p, rows, tile(t)] for t in (0, 4, 8)] for p in range(2)]
        top = [jnp.where(low, e[0], e[1]) for e in edge]
        bot = [jnp.where(low, e[1], e[2]) for e in edge]
        top = jnp.where(last_part, pltpu.roll(top[0], 40, 1), top[1])
        bot = jnp.where(first_part, pltpu.roll(bot[0], 88, 1), bot[1])
        return jnp.where(up_first, bot, top), jnp.where(up_first, top, bot)

    def squeezed(rows):
        out = []
        for p in range(2):
            tiles = [src[p, rows, pl.ds(pl.multiple_of(base + LANES * t, LANES), LANES)] for t in range(5)]
            out += squeeze_cols(tiles, lane24, m1, m2, n0)
        return out

    def step(k, carry):
        at = [pl.ds(pl.multiple_of(q * QUARTER + k * PATCH, 8), PATCH) for q in range(4)]
        whole = [faces(rows) for rows in at]
        for n, msg in enumerate((face_a, face_b)):
            turned = {d: pltpu.roll(whole[3][n], d, 1) for d in (24, 56, 72, 104)}
            for q in range(3):
                value = whole[q][n]
                for source, to, count in FOLDS[q]:
                    value = jnp.where(jnp.logical_and(lane >= to, lane < to + count), turned[(to - source) % LANES], value)
                msg[at[q], :] = value
        for h in range(2):
            msg = None
            for slot, v in enumerate(squeezed(at[h]) + squeezed(at[h + 2])):
                msg = v if slot == 0 else jnp.where(lane8 == lax.rem(v0 + slot, 8), pltpu.roll(v, slot, 1), msg)
            side[at[h], :] = msg
        return carry

    steps = PATCH // 4
    if ready is None:
        lax.fori_loop(0, steps, step, 0)
    else:
        for i in range(CHUNKS):
            ready(i)
            lax.fori_loop(i * steps // CHUNKS, (i + 1) * steps // CHUNKS, step, 0)
    for p in range(2):
        for out, flip in ((down_a, row_up_first), (down_b, jnp.logical_not(row_up_first))):
            out[p] = src[p, pl.ds(pl.multiple_of(jnp.where(flip, SQUARE - PATCH, 0), 8), PATCH), :]
        for a in range(PATCH):
            left = src[p, a * PATCH : a * PATCH + 1, :]
            right = src[p, a * PATCH + PATCH - 1 : a * PATCH + PATCH, :]
            across_a[p, a : a + 1, :] = jnp.where(row_even, right, left)
            across_b[p, a : a + 1, :] = jnp.where(row_even, left, right)


SLOT = 24


def pack_densities(src, colw, table, row_sums, slots, sums, codes):
    row_id, col_id = place()
    odd = lax.rem(row_id, 2)
    across = lax.rem(row_id, 4) - 2 * lax.rem(col_id, 2)
    along = row_id // 4 - col_id // 2
    beside = jnp.logical_and(along == 0, jnp.logical_and(across >= -1, across <= 2))
    over = jnp.logical_and(jnp.abs(along) == 1, jnp.logical_and(across >= 0, across <= 1))
    table[...] = jnp.zeros(table.shape, F32)

    @pl.when(jnp.logical_or(beside, over))
    def _():
        slots[...] = jnp.zeros(slots.shape, F32)
        row_sums[...] = jnp.zeros(row_sums.shape, F32)
        sums[...] = jnp.zeros(sums.shape, F32)
        lane = iota((8, LANES), 1)
        sub = iota((8, LANES), 0)
        for t in range(TILES):
            j = lane + t * LANES
            g = (j >= SQUARE).astype(jnp.int32)
            a = over24(j - SQUARE * g)
            b = j - SQUARE * g - PATCH * a
            codes[t] = 100 * (PATCH * (col_id // 2) + a) + PATCH * (2 * lax.rem(col_id, 2) + g) + b
        first = 100 * PATCH * (row_id // 4) + PATCH * lax.rem(row_id, 4)

        def share(a, tiles):
            along_rows = [jnp.zeros((8, LANES), F32) for _ in range(3)]
            for t in tiles:
                cols = pl.ds(pl.multiple_of(t * LANES, LANES), LANES)
                now = middle = jnp.zeros((8, LANES), F32)
                for k in range(3):
                    rows = pl.ds(pl.multiple_of(a * PATCH + 8 * k, 8), 8)
                    apart = first + 100 * a + 8 * k + sub - codes[t]
                    w = jnp.where(apart == 100, colw[C_DN_ALL, :, cols], 0.0)
                    w = jnp.where(apart == -100, colw[C_UP_ALL, :, cols], w)
                    w = jnp.where(apart == 1, colw[C_RT_ALL, :, cols], w)
                    w = jnp.where(apart == -1, colw[C_LF_ALL, :, cols], w)
                    flow = w * src[1, rows, cols]
                    own = jnp.where(apart == 0, src[0, rows, cols], 0.0)
                    now = now + own
                    middle = middle + own - flow
                    along_rows[k] = along_rows[k] + flow
                sums[0, t] += now
                sums[1, t] += middle
            for k in range(3):
                row_sums[pl.ds(pl.multiple_of(64 * odd + a * PATCH + 8 * k, 8), 8), :] = along_rows[k]

        @pl.when(beside)
        def _():
            def step(a, carry):
                starts = [jnp.clip(SQUARE * g + PATCH * (a - 1), 0, (TILES - 2) * LANES) // LANES for g in range(2)]
                share(a, [start + d for start in starts for d in range(2)])
                return carry

            lax.fori_loop(0, PATCH, step, 0)

        @pl.when(over)
        def _():
            start = jnp.where(along == 1, 4, 0)
            share(jnp.where(along == 1, 0, PATCH - 1), [start, start + 4])

        for t in range(TILES):
            slots[0, t : t + 1, :] = jnp.sum(sums[0, t], axis=0, keepdims=True)
            slots[0, TILES + t : TILES + t + 1, :] = jnp.sum(sums[1, t], axis=0, keepdims=True)
        for t in range(5):
            got = jnp.sum(row_sums[t * LANES : (t + 1) * LANES, :].T, axis=0, keepdims=True)
            slots[1, pl.ds(TILES + 4 * odd + t, 1), :] = got
        table[pl.ds(pl.multiple_of(SLOT * col_id, 8), SLOT), :] = slots[0]
        table[pl.ds(pl.multiple_of(SLOT * (row_id // 2), 8), SLOT), :] += slots[1]


CHUNKS = 3


def first_kernel(corr, down, across, rep, y, bonds, colw, *refs):
    faces, table, (*scratch, sems) = refs[:7], refs[7], refs[8:]
    tables_in = [pltpu.make_async_copy(v, bonds.at[n], sems.at[n]) for n, v in enumerate((down, across, rep))]
    step = QUARTER // CHUNKS
    chunks = []
    for i in range(CHUNKS):
        chunks.append([])
        for q in range(4):
            for p in range(2):
                rows = pl.ds(q * QUARTER + i * step, step)
                sem = sems.at[3 + (i * 4 + q) * 2 + p]
                chunks[-1].append(pltpu.make_async_copy(corr.at[p, rows], y.at[p, rows], sem))
    for c in sum([tables_in, *chunks], []):
        c.start()
    for c in tables_in:
        c.wait()
    col_weights(bonds, colw)

    def ready(i):
        for c in chunks[i]:
            c.wait()

    pack_faces(y, *faces, ready=ready)
    pack_densities(y, colw, table, *scratch)


def interior_kernel(final, first, last, *refs):
    y1, y, roww, colw, out = refs[-5:]
    sub = iota((8, LANES), 0)
    lane, lane24 = lane_maps((8, LANES))
    three = range(3)

    def strip(a, p):
        q = 1 - p
        here = pl.multiple_of(a * PATCH, 8)
        above = pl.multiple_of(jnp.maximum(a - 1, 0) * PATCH, 8)
        below = pl.multiple_of(jnp.minimum(a + 1, PATCH - 1) * PATCH, 8)

        def at(t, k, start=here):
            return y1[q, pl.ds(start + 8 * k, 8), tile(t)]

        def side(t0, m1, m2, n0, shift):
            pairs = [squeeze_cols([at(t0 + t, k) for t in range(5)], lane24, m1, m2, n0) for k in three]
            return [[pltpu.roll(v, shift, 1) for v in pair] for pair in pairs]

        def turned(t):
            x = [at(t, k) for k in three]
            return [[pltpu.roll(v, n, 1) for v in x] for n in (1, PATCH, LANES - 1, LANES - PATCH)]

        heads = side(4, 8, 0, 16, 87)
        tails = None
        before, now = None, turned(0)
        for t in range(TILES):
            later = turned(t + 1) if t < TILES - 1 else None
            if t == 4:
                tails = side(0, 15, 7, 23, 41)
            x = [at(t, k) for k in three]
            fwd = [pltpu.roll(v, 1, 0) for v in x]
            bwd = [pltpu.roll(v, 7, 0) for v in x]
            w = lambda n: colw[n, :, tile(t)]
            for k in three:
                rows = pl.ds(here + 8 * k, 8)
                rw = lambda n: roww[n, rows, :]
                left = fwd[0] if k == 0 else jnp.where(sub == 0, fwd[k - 1], fwd[k])
                right = bwd[2] if k == 2 else jnp.where(sub == 7, bwd[k + 1], bwd[k])
                minus_b = now[0][k] if t == 0 else jnp.where(lane < 1, before[0][k], now[0][k])
                minus_a = now[1][k] if t == 0 else jnp.where(lane < PATCH, before[1][k], now[1][k])
                plus_b = now[2][k] if later is None else jnp.where(lane >= LANES - 1, later[2][k], now[2][k])
                plus_a = now[3][k] if later is None else jnp.where(lane >= LANES - PATCH, later[3][k], now[3][k])
                acc = rw(DN_IN) * at(t, k, below) + rw(UP_IN) * at(t, k, above) + rw(RT_IN) * right + rw(LF_IN) * left
                acc = acc + w(C_DN) * plus_a + w(C_UP) * minus_a + w(C_RT) * plus_b + w(C_LF) * minus_b
                if t <= 3:
                    acc = acc + w(C_RT_E) * heads[k][0]
                if t in (0, 3, 4):
                    acc = acc + w(C_RT_F) * heads[k][1]
                if 5 <= t <= 8:
                    acc = acc + w(C_LF_E) * tails[k][0]
                if t in (4, 5, 8):
                    acc = acc + w(C_LF_F) * tails[k][1]
                old = y1[p, rows, tile(t)]
                if final:
                    old = old + y[p, rows, tile(t)]
                new = old + acc if p == 0 else old - acc
                out[p, rows, tile(t)] = 0.5 * new if final else new
            before, now = now, later

    def step(a, carry):
        for p in range(2):
            strip(a, p)
        return carry

    lax.fori_loop(first, last, step, 0, unroll=next(n for n in (4, 3, 2, 1) if (last - first) % n == 0))


def unfolded(msg, at, lane):
    value = None
    for q in range(3):
        carrier = msg[pl.ds(pl.multiple_of(q * QUARTER + at, 8), 8), :]
        for source, to, count in FOLDS[q]:
            turned = pltpu.roll(carrier, (source - to) % LANES, 1)
            inside = jnp.logical_and(lane >= source, lane < source + count)
            value = turned if value is None else jnp.where(inside, turned, value)
    return value


def finish(stage, base, y, halos, roww, colw, out, e_row, e_col, chunk_done=None):
    face_a, face_b, side, down_a, down_b, across_a, across_b, table = halos
    scale = 0.5 if stage else 1.0
    row_id, col_id = place()
    up_first, even, row_up_first, row_even = parities()
    row_odd = lax.rem(row_id, 2)
    shift = jnp.where(even, 87, 41)
    lane = iota((8, LANES), 1)
    row_slot = table[pl.ds(pl.multiple_of(SLOT * (row_id // 2), 8), SLOT), :]
    col_slot = table[pl.ds(pl.multiple_of(SLOT * col_id, 8), SLOT), :]
    for t in range(5):
        u = stage * TILES + t
        strip = jnp.where(row_odd == 1, row_slot[4 + u : 5 + u, :], row_slot[u : u + 1, :])
        e_row[t * LANES : (t + 1) * LANES, :] = jnp.broadcast_to(strip, (LANES, LANES)).T
    for t in range(TILES):
        e_col[:, tile(t)] = col_slot[stage * TILES + t : stage * TILES + t + 1, :] * colw[COL_U, :, tile(t)]

    def strip(a, folded):
        here = pl.multiple_of(a * PATCH, 8)
        near = pl.ds(pl.multiple_of(8 * (a // 8), 8), 8)
        to_first = lax.rem(8 - lax.rem(a, 8), 8)
        to_last = 7 - lax.rem(a, 8)
        half = a // (PATCH // 2)
        for k in range(3):
            rows = pl.ds(here + 8 * k, 8)
            es = e_row[pl.ds(64 * row_odd + here + 8 * k, 8), :] * roww[ROW_U, rows, :]
            if folded:
                got = [unfolded(m, here - 3 * QUARTER + 8 * k, lane) for m in (face_a, face_b)]
            else:
                got = [m[rows, :] for m in (face_a, face_b)]
            lower = jnp.where(up_first, got[0], got[1])
            upper = jnp.where(up_first, got[1], got[0])
            lowers = (lower, pltpu.roll(lower, 40, 1))
            uppers = (upper, pltpu.roll(upper, 88, 1))
            packed = side[pl.ds(pl.multiple_of(here - half * (SQUARE // 2), 8) + 8 * k, 8), :]
            gaps = [es - e_col[:, tile(t)] for t in range(TILES)]
            for p in range(2):
                q = 1 - p
                se, sf = [pltpu.roll(packed, lax.rem(shift + LANES - (4 * half + 2 * q + n), LANES), 1) for n in range(2)]
                for t in range(TILES):
                    w = lambda n: colw[n, :, tile(t)]
                    acc = gaps[t] * y[q, rows, tile(t)]
                    if t in (0, 4):
                        acc = acc + w(C_UP_RIM) * uppers[q]
                    if t in (4, 8):
                        acc = acc + w(C_DN_RIM) * lowers[q]
                    if t != 4:
                        acc = acc + w(C_X_E) * se
                    if t in (0, 3, 4, 5, 8):
                        acc = acc + w(C_X_F) * sf
                    if k != 1:
                        pair = [m[q, near, tile(t)] for m in (across_a, across_b)]
                    if k == 0:
                        left = pltpu.roll(jnp.where(row_even, pair[1], pair[0]), to_first, 0)
                        acc = acc + roww[LF_RIM, rows, :] * left
                    if k == 2:
                        right = pltpu.roll(jnp.where(row_even, pair[0], pair[1]), to_last, 0)
                        acc = acc + roww[RT_RIM, rows, :] * right
                    if scale != 1.0:
                        acc = scale * acc
                    old = base[p, rows, tile(t)]
                    out[p, rows, tile(t)] = old + acc if p == 0 else old - acc

    def rim(a, weight, first, second):
        for p in range(2):
            for k in range(3):
                rows = pl.ds(a * PATCH + 8 * k, 8)
                w = roww[weight, rows, :] * (scale if p == 0 else -scale)
                for t in range(TILES):
                    pair = [m[1 - p, 8 * k : 8 * k + 8, tile(t)] for m in (first, second)]
                    out[p, rows, tile(t)] += w * jnp.where(row_up_first, pair[0], pair[1])

    fold = 3 * PATCH // 4
    stops = (0, fold, PATCH) if chunk_done is None else (0, fold // 3, 2 * fold // 3, fold, PATCH - 2, PATCH)
    for start, stop in zip(stops, stops[1:]):
        lax.fori_loop(start, stop, lambda a, c, f=start >= fold: (strip(a, f), c)[1], 0, unroll=2)
        if start == 0:
            rim(0, UP_RIM, down_b, down_a)
        if stop == PATCH:
            rim(PATCH - 1, DN_RIM, down_a, down_b)
        if chunk_done is not None:
            chunk_done(start * PATCH, stop * PATCH)


def middle_kernel(base, y, *refs):
    halos, (roww, colw), (y1, *faces), (e_row, e_col) = refs[:8], refs[8:10], refs[10:18], refs[18:]
    finish(0, base, y, halos, roww, colw, y1, e_row, e_col)
    pack_faces(y1, *faces)


def last_kernel(base, y1, *refs):
    halos, (roww, colw), out_hbm, (e_row, e_col, out, sems) = refs[:8], refs[8:10], refs[10], refs[11:]
    copies = []

    def chunk_done(first, last):
        for p in range(2):
            rows = pl.ds(first, last - first)
            copies.append(pltpu.make_async_copy(out.at[p, rows], out_hbm.at[p, rows], sems.at[len(copies)]))
            copies[-1].start()

    finish(1, base, y1, halos, roww, colw, out, e_row, e_col, chunk_done)
    for c in copies:
        c.wait()


def on_chip(*shape):
    return pltpu.VMEM(shape, F32)


VM = pl.BlockSpec(memory_space=pltpu.VMEM)
STATE = (2, SQUARE, COLUMNS)
FACES = ((3 * QUARTER, LANES),) * 2 + ((SQUARE // 2, LANES),) + ((2, PATCH, COLUMNS),) * 4
TABLE = (8 * SLOT, LANES)


def call(kernel, args, out_shapes, scratch=(), out_specs=None, aliases=None, loads=False):
    many = isinstance(out_shapes, (list, tuple))
    return pl.pallas_call(
        kernel,
        out_shape=out_shapes,
        in_specs=[pl.BlockSpec(memory_space=pl.ANY) if loads else VM] * len(args),
        out_specs=out_specs or ([VM] * len(out_shapes) if many else VM),
        scratch_shapes=list(scratch),
        input_output_aliases=aliases or {},
        compiler_params=pltpu.CompilerParams(vmem_limit_bytes=VMEM_LIMIT),
        cost_estimate=pl.CostEstimate(flops=1000, bytes_accessed=1000, transcendentals=0),
    )(*[pltpu.with_memory_space_constraint(x, pltpu.HBM if loads else pltpu.VMEM) for x in args])


def pairs(axis, linked):
    n = lax.axis_size(axis)
    found = [(i, j) for i in range(n) for j in range(i + 1, n) if linked(i, j)]
    return found + [(j, i) for i, j in found]


def traded(block, axis, linked):
    return lax.ppermute(block, axis, pairs(axis, linked))


def flipped(block, axis, bit):
    return traded(block, axis, lambda i, j: j == i ^ bit)


def tie(value, *after):
    def kernel(*refs):
        refs[-1][...] = refs[0][...]

    return call(kernel, (value, *after), on_chip(*value.shape))


def merged(value, got, *after):
    def kernel(*refs):
        refs[-1][...] = refs[0][...] + refs[1][...]

    return call(kernel, (value, got, *after), on_chip(*value.shape))


def swap_face_a(x):
    return flipped(x, "col", 2)


def swap_face_b(x):
    return traded(x, "col", lambda i, j: j == i + 2 and (i // 2) % 2 == 1)


def swap_side(x):
    return flipped(x, "col", 1)


def swap_down_a(x):
    return flipped(x, "row", 4)


def swap_down_b(x):
    return traded(x, "row", lambda i, j: j == i + 4 and (i // 4) % 2 == 1)


def swap_across_a(x):
    return flipped(x, "row", 1)


def swap_across_b(x):
    return traded(x, "row", lambda i, j: j == i + 1 and i % 4 == 1)


def swap_bits(x, row_bits, col_bits):
    rows, cols = lax.axis_size("row"), lax.axis_size("col")
    route = [(r * cols + c, (r ^ row_bits) * cols + (c ^ col_bits)) for r in range(rows) for c in range(cols)]
    return lax.ppermute(x, ("row", "col"), route)


def first_exchange(faces, table, first_work, piece):
    face_a, face_b, side, down_a, down_b, across_a, across_b = faces
    face_a, face_b = swap_face_a(face_a), swap_face_b(face_b)
    table = merged(table, flipped(table, "row", 4), first_work)
    side = swap_side(tie(side, table))
    part = piece(0, None, table)
    table = merged(table, flipped(table, "row", 12), part)
    down_a = swap_down_a(tie(down_a, table))
    table = merged(table, flipped(table, "row", 1), face_a, face_b)
    down_b = swap_down_b(tie(down_b, table))
    part = piece(1, part, table)
    table = merged(table, flipped(table, "row", 2), part, side)
    across_a = swap_across_a(tie(across_a, table))
    part = piece(2, part, table)
    table = merged(table, swap_bits(table, 2, 4), part, down_a)
    across_b = swap_across_b(tie(across_b, table))
    part = piece(3, part, table)
    table = merged(table, flipped(table, "col", 1), part, down_b)
    part = piece(4, part, table)
    table = merged(table, flipped(table, "col", 3), part, across_a)
    return part, (face_a, face_b, side, down_a, down_b, across_a, across_b, table)


def second_exchange(faces, table, piece):
    face_a, face_b, side, down_a, down_b, across_a, across_b = faces
    face_a, face_b = swap_face_a(face_a), swap_face_b(face_b)
    part = piece(0, None)
    side = swap_side(tie(side, part))
    down_a = swap_down_a(tie(down_a, part))
    down_b = swap_down_b(tie(down_b, part))
    part = piece(1, part)
    part = piece(2, part)
    part = piece(3, part)
    across_a = swap_across_a(tie(across_a, part))
    across_b = swap_across_b(tie(across_b, part))
    part = piece(4, part)
    part = piece(5, part, face_a, face_b)
    return part, (face_a, face_b, side, down_a, down_b, across_a, across_b, table)


def interior(final, y1, y, weights, stops):
    def piece(n, part, *after):
        kernel = functools.partial(interior_kernel, final, stops[n], stops[n + 1])
        args = (*after, y1, y, *weights)
        if n == 0:
            return call(kernel, args, on_chip(*STATE))
        return call(kernel, (part, *args), on_chip(*STATE), aliases={0: 0})

    return piece


def local(corr, bonds_down, bonds_across, repulsion):
    faces_out = [on_chip(*s) for s in FACES]
    e_scratch = [pltpu.VMEM((5 * LANES, LANES), F32), pltpu.VMEM((8, COLUMNS), F32)]
    y, bonds, colw, *faces, table = call(
        first_kernel,
        (corr, bonds_down, bonds_across, repulsion),
        [on_chip(*STATE), on_chip(3, LATTICE, LATTICE), on_chip(17, 8, COLUMNS), *faces_out, on_chip(*TABLE)],
        [
            pltpu.VMEM((5 * LANES, LANES), F32),
            pltpu.VMEM((2, SLOT, LANES), F32),
            pltpu.VMEM((2, TILES, 8, LANES), F32),
            pltpu.VMEM((TILES, 8, LANES), jnp.int32),
            pltpu.SemaphoreType.DMA((3 + 8 * CHUNKS,)),
        ],
        loads=True,
    )
    weights = (call(row_weights_kernel, (bonds,), on_chip(9, SQUARE, LANES)), colw)
    part, halos = first_exchange(faces, table, weights[0], interior(False, y, y, weights, (0, 8, 10, 14, 18, 24)))
    y1, *faces = call(middle_kernel, (part, y, *halos, *weights), [on_chip(*STATE), *faces_out], e_scratch)
    part, halos = second_exchange(faces, halos[-1], interior(True, y1, y, weights, (0, 4, 8, 12, 16, 20, 24)))
    return call(
        last_kernel,
        (part, y1, *halos, *weights),
        jax.ShapeDtypeStruct(STATE, F32),
        [*e_scratch, pltpu.VMEM(STATE, F32), pltpu.SemaphoreType.DMA((10,))],
        out_specs=pl.BlockSpec(memory_space=pl.ANY),
    )


def solution(mesh):
    in_specs = (P(None, "row", "col"), P(), P(), P())
    out_specs = P(None, "row", "col")
    return jax.shard_map(local, mesh=mesh, in_specs=in_specs, out_specs=out_specs, check_vma=False)
```

```python
import functools

import jax
import jax.numpy as jnp
from jax import lax
from jax.experimental import pallas as pl
from jax.experimental.pallas import tpu as pltpu
from jax.sharding import PartitionSpec as P

PATCH = 24
SQUARE = PATCH * PATCH
COLUMNS = 2 * SQUARE
LANES = 128
TILES = COLUMNS // LANES
LATTICE = 4 * PATCH
TIME_STEP = 0.04
F32 = jnp.float32
VMEM_LIMIT = 8 * 1024 * 1024

DN_IN, UP_IN, RT_IN, LF_IN, DN_RIM, UP_RIM, RT_RIM, LF_RIM, ROW_U = range(9)
C_DN, C_UP, C_RT, C_LF, C_DN_RIM, C_UP_RIM, C_RT_E, C_RT_F, C_LF_E, C_LF_F, C_X_E, C_X_F, COL_U, C_DN_ALL, C_UP_ALL, C_RT_ALL, C_LF_ALL = range(17)


def iota(shape, dim):
    return lax.broadcasted_iota(jnp.int32, shape, dim)


def over24(x):
    return ((x.astype(F32) + 0.5) * (1.0 / PATCH)).astype(jnp.int32)


def on(mask):
    return jnp.where(mask, 1.0, 0.0).astype(F32)


def within(x, lo, hi):
    return on(x >= lo) * on(x <= hi)


def place():
    return lax.axis_index("row"), lax.axis_index("col")


def tile(t):
    return pl.ds(t * LANES, LANES)


def tables(bonds):
    side = (LATTICE, LATTICE)
    down = jnp.where(iota(side, 0) < LATTICE - 1, bonds[0], 0.0)
    across = jnp.where(iota(side, 1) < LATTICE - 1, bonds[1], 0.0)
    rep = bonds[2]
    dot = functools.partial(jnp.dot, precision=lax.Precision.HIGHEST, preferred_element_type=F32)
    return down, across, rep, dot


def row_weights_kernel(bonds, roww):
    row_id, _ = place()
    down, across, rep, dot = tables(bonds)
    s = iota((SQUARE, LATTICE), 0)
    lane = iota((SQUARE, LATTICE), 1)
    a = over24(s)
    b = s - PATCH * a
    ga = PATCH * (row_id // 4) + a
    gb = PATCH * (row_id % 4) + b

    def pick_rows(table, da, db):
        rows = dot(on(lane == ga + da), table)
        return jnp.sum(jnp.where(lane == gb + db, rows, 0.0), axis=1, keepdims=True)

    a1 = a[:, 0:1]
    b1 = b[:, 0:1]
    last = PATCH - 1
    dn = -TIME_STEP * pick_rows(down, 0, 0)
    up = -TIME_STEP * pick_rows(down, -1, 0)
    rt = -TIME_STEP * pick_rows(across, 0, 0)
    lf = -TIME_STEP * pick_rows(across, 0, -1)
    values = {
        DN_IN: dn * on(a1 < last), UP_IN: up * on(a1 > 0), RT_IN: rt * on(b1 < last), LF_IN: lf * on(b1 > 0),
        DN_RIM: dn * on(a1 == last), UP_RIM: up * on(a1 == 0), RT_RIM: rt * on(b1 == last), LF_RIM: lf * on(b1 == 0),
        ROW_U: TIME_STEP * pick_rows(rep, 0, 0),
    }
    for k, v in values.items():
        roww[k] = jnp.broadcast_to(v, (SQUARE, LANES))


def col_weights(bonds, colw):
    _, col_id = place()
    down, across, rep, dot = tables(bonds)
    last = PATCH - 1
    wide = (LATTICE, COLUMNS)
    j = iota(wide, 1)
    g = (j >= SQUARE).astype(jnp.int32)
    jj = j - SQUARE * g
    a = over24(jj)
    b = jj - PATCH * a
    sub = iota(wide, 0)
    parity = col_id % 2
    ga = PATCH * (col_id // 2) + a
    gb = PATCH * (2 * parity + g) + b

    def pick_cols(table, da, db):
        cols = dot(table, on(sub == gb + db))
        return jnp.sum(jnp.where(sub == ga + da, cols, 0.0), axis=0, keepdims=True)

    a = a[0:1]
    b = b[0:1]
    g = g[0:1]
    dn = TIME_STEP * pick_cols(down, 0, 0)
    up = TIME_STEP * pick_cols(down, -1, 0)
    rt = TIME_STEP * pick_cols(across, 0, 0)
    lf = TIME_STEP * pick_cols(across, 0, -1)
    tails0 = rt * on(b == last) * on(g == 0)
    heads1 = lf * on(b == 0) * on(g == 1)
    tails1 = rt * on(b == last) * on(g == 1)
    heads0 = lf * on(b == 0) * on(g == 0)
    even = on(jnp.full(a.shape, parity, jnp.int32) == 0)
    x_even = even * tails1
    x_odd = (1.0 - even) * heads0
    rt_e = within(a, 3, 18)
    lf_e = within(a, 5, 20)
    xe_e = within(a, 6, 21)
    xo_e = within(a, 2, 17)
    values = {
        C_DN: dn * on(a < last), C_UP: up * on(a > 0), C_RT: rt * on(b < last), C_LF: lf * on(b > 0),
        C_DN_RIM: dn * on(a == last), C_UP_RIM: up * on(a == 0),
        C_RT_E: tails0 * rt_e, C_RT_F: tails0 * (1.0 - rt_e),
        C_LF_E: heads1 * lf_e, C_LF_F: heads1 * (1.0 - lf_e),
        C_X_E: x_even * xe_e + x_odd * xo_e, C_X_F: x_even * (1.0 - xe_e) + x_odd * (1.0 - xo_e),
        COL_U: TIME_STEP * pick_cols(rep, 0, 0),
        C_DN_ALL: dn, C_UP_ALL: up, C_RT_ALL: rt, C_LF_ALL: lf,
    }
    for k, v in values.items():
        colw[k] = jnp.broadcast_to(v, (8, COLUMNS))


STRIP = (PATCH, LANES)


def squeeze_cols(tiles, lane24, m1, m2, n0):
    e = jnp.where(lane24 == m1, tiles[1], jnp.where(lane24 == m2, tiles[2], tiles[3]))
    f = jnp.where(lane24 == n0, tiles[0], tiles[4])
    return e, f


def lane_maps(shape=STRIP):
    lane = iota(shape, 1)
    return lane, lane - PATCH * over24(lane)


def parities():
    row_id, col_id = place()
    return lax.rem(col_id // 2, 2) == 0, lax.rem(col_id, 2) == 0, lax.rem(row_id // 4, 2) == 0, lax.rem(row_id, 2) == 0


FOLDS = (((0, 24, 16), (16, 88, 8), (40, 96, 8)), ((48, 24, 16), (64, 88, 16)), ((80, 24, 8), (104, 32, 8), (112, 88, 16)))
QUARTER = SQUARE // 4


def pack_faces(src, face_a, face_b, side, down_a, down_b, across_a, across_b, ready=None):
    up_first, even, row_up_first, row_even = parities()
    base = jnp.where(even, 4 * LANES, 0)
    lane, lane24 = lane_maps()
    lane8 = lax.rem(lane, 8)
    m1 = jnp.where(even, 7, 16)
    m2 = jnp.where(even, 23, 8)
    n0 = jnp.where(even, 15, 0)
    v0 = jnp.where(even, 7, 0)
    low = lane < 64
    half = lax.rem(lane, 64)
    first_part = half < PATCH
    last_part = half >= 64 - PATCH

    def faces(rows):
        edge = [[src[p, rows, tile(t)] for t in (0, 4, 8)] for p in range(2)]
        top = [jnp.where(low, e[0], e[1]) for e in edge]
        bot = [jnp.where(low, e[1], e[2]) for e in edge]
        top = jnp.where(last_part, pltpu.roll(top[0], 40, 1), top[1])
        bot = jnp.where(first_part, pltpu.roll(bot[0], 88, 1), bot[1])
        return jnp.where(up_first, bot, top), jnp.where(up_first, top, bot)

    def squeezed(rows):
        out = []
        for p in range(2):
            tiles = [src[p, rows, pl.ds(pl.multiple_of(base + LANES * t, LANES), LANES)] for t in range(5)]
            out += squeeze_cols(tiles, lane24, m1, m2, n0)
        return out

    def step(k, carry):
        at = [pl.ds(pl.multiple_of(q * QUARTER + k * PATCH, 8), PATCH) for q in range(4)]
        whole = [faces(rows) for rows in at]
        for n, msg in enumerate((face_a, face_b)):
            turned = {d: pltpu.roll(whole[3][n], d, 1) for d in (24, 56, 72, 104)}
            for q in range(3):
                value = whole[q][n]
                for source, to, count in FOLDS[q]:
                    value = jnp.where(jnp.logical_and(lane >= to, lane < to + count), turned[(to - source) % LANES], value)
                msg[at[q], :] = value
        for h in range(2):
            msg = None
            for slot, v in enumerate(squeezed(at[h]) + squeezed(at[h + 2])):
                msg = v if slot == 0 else jnp.where(lane8 == lax.rem(v0 + slot, 8), pltpu.roll(v, slot, 1), msg)
            side[at[h], :] = msg
        return carry

    steps = PATCH // 4
    if ready is None:
        lax.fori_loop(0, steps, step, 0)
    else:
        for i in range(CHUNKS):
            ready(i)
            lax.fori_loop(i * steps // CHUNKS, (i + 1) * steps // CHUNKS, step, 0)
    for p in range(2):
        for out, flip in ((down_a, row_up_first), (down_b, jnp.logical_not(row_up_first))):
            out[p] = src[p, pl.ds(pl.multiple_of(jnp.where(flip, SQUARE - PATCH, 0), 8), PATCH), :]
        for a in range(PATCH):
            left = src[p, a * PATCH : a * PATCH + 1, :]
            right = src[p, a * PATCH + PATCH - 1 : a * PATCH + PATCH, :]
            across_a[p, a : a + 1, :] = jnp.where(row_even, right, left)
            across_b[p, a : a + 1, :] = jnp.where(row_even, left, right)


SLOT = 24


def pack_densities(src, colw, slots, row_sums, sums, codes):
    row_id, col_id = place()
    odd = lax.rem(row_id, 2)
    across = lax.rem(row_id, 4) - 2 * lax.rem(col_id, 2)
    along = row_id // 4 - col_id // 2
    beside = jnp.logical_and(along == 0, jnp.logical_and(across >= -1, across <= 2))
    over = jnp.logical_and(jnp.abs(along) == 1, jnp.logical_and(across >= 0, across <= 1))
    slots[...] = jnp.zeros(slots.shape, F32)

    @pl.when(jnp.logical_or(beside, over))
    def _():
        row_sums[...] = jnp.zeros(row_sums.shape, F32)
        sums[...] = jnp.zeros(sums.shape, F32)
        lane = iota((8, LANES), 1)
        sub = iota((8, LANES), 0)
        for t in range(TILES):
            j = lane + t * LANES
            g = (j >= SQUARE).astype(jnp.int32)
            a = over24(j - SQUARE * g)
            b = j - SQUARE * g - PATCH * a
            codes[t] = 100 * (PATCH * (col_id // 2) + a) + PATCH * (2 * lax.rem(col_id, 2) + g) + b
        first = 100 * PATCH * (row_id // 4) + PATCH * lax.rem(row_id, 4)

        def share(a, tiles):
            along_rows = [jnp.zeros((8, LANES), F32) for _ in range(3)]
            for t in tiles:
                cols = pl.ds(pl.multiple_of(t * LANES, LANES), LANES)
                now = middle = jnp.zeros((8, LANES), F32)
                for k in range(3):
                    rows = pl.ds(pl.multiple_of(a * PATCH + 8 * k, 8), 8)
                    apart = first + 100 * a + 8 * k + sub - codes[t]
                    w = jnp.where(apart == 100, colw[C_DN_ALL, :, cols], 0.0)
                    w = jnp.where(apart == -100, colw[C_UP_ALL, :, cols], w)
                    w = jnp.where(apart == 1, colw[C_RT_ALL, :, cols], w)
                    w = jnp.where(apart == -1, colw[C_LF_ALL, :, cols], w)
                    flow = w * src[1, rows, cols]
                    own = jnp.where(apart == 0, src[0, rows, cols], 0.0)
                    now = now + own
                    middle = middle + own - flow
                    along_rows[k] = along_rows[k] + flow
                sums[0, t] += now
                sums[1, t] += middle
            for k in range(3):
                row_sums[pl.ds(pl.multiple_of(64 * odd + a * PATCH + 8 * k, 8), 8), :] = along_rows[k]

        @pl.when(beside)
        def _():
            def step(a, carry):
                starts = [jnp.clip(SQUARE * g + PATCH * (a - 1), 0, (TILES - 2) * LANES) // LANES for g in range(2)]
                share(a, [start + d for start in starts for d in range(2)])
                return carry

            lax.fori_loop(0, PATCH, step, 0)

        @pl.when(over)
        def _():
            start = jnp.where(along == 1, 4, 0)
            share(jnp.where(along == 1, 0, PATCH - 1), [start, start + 4])

        for t in range(TILES):
            slots[t : t + 1, :] = jnp.sum(sums[0, t], axis=0, keepdims=True)
            slots[TILES + t : TILES + t + 1, :] = jnp.sum(sums[1, t], axis=0, keepdims=True)
        for t in range(5):
            got = jnp.sum(row_sums[t * LANES : (t + 1) * LANES, :].T, axis=0, keepdims=True)
            slots[pl.ds(SLOT + TILES + 4 * odd + t, 1), :] = got


CHUNKS = 3


def first_kernel(corr, down, across, rep, y, bonds, colw, *refs):
    faces, table, (*scratch, sems) = refs[:7], refs[7], refs[8:]
    tables_in = [pltpu.make_async_copy(v, bonds.at[n], sems.at[n]) for n, v in enumerate((down, across, rep))]
    step = QUARTER // CHUNKS
    chunks = []
    for i in range(CHUNKS):
        chunks.append([])
        for q in range(4):
            for p in range(2):
                rows = pl.ds(q * QUARTER + i * step, step)
                sem = sems.at[3 + (i * 4 + q) * 2 + p]
                chunks[-1].append(pltpu.make_async_copy(corr.at[p, rows], y.at[p, rows], sem))
    for c in sum([tables_in, *chunks], []):
        c.start()
    for c in tables_in:
        c.wait()
    col_weights(bonds, colw)

    def ready(i):
        for c in chunks[i]:
            c.wait()

    pack_faces(y, *faces, ready=ready)
    pack_densities(y, colw, table, *scratch)


def interior_kernel(final, first, last, *refs):
    y1, y, roww, colw, out = refs[-5:]
    sub = iota((8, LANES), 0)
    lane, lane24 = lane_maps((8, LANES))
    three = range(3)

    def strip(a, p):
        q = 1 - p
        here = pl.multiple_of(a * PATCH, 8)
        above = pl.multiple_of(jnp.maximum(a - 1, 0) * PATCH, 8)
        below = pl.multiple_of(jnp.minimum(a + 1, PATCH - 1) * PATCH, 8)

        def at(t, k, start=here):
            return y1[q, pl.ds(start + 8 * k, 8), tile(t)]

        def side(t0, m1, m2, n0, shift):
            pairs = [squeeze_cols([at(t0 + t, k) for t in range(5)], lane24, m1, m2, n0) for k in three]
            return [[pltpu.roll(v, shift, 1) for v in pair] for pair in pairs]

        def turned(t):
            x = [at(t, k) for k in three]
            return [[pltpu.roll(v, n, 1) for v in x] for n in (1, PATCH, LANES - 1, LANES - PATCH)]

        heads = side(4, 8, 0, 16, 87)
        tails = None
        before, now = None, turned(0)
        for t in range(TILES):
            later = turned(t + 1) if t < TILES - 1 else None
            if t == 4:
                tails = side(0, 15, 7, 23, 41)
            x = [at(t, k) for k in three]
            fwd = [pltpu.roll(v, 1, 0) for v in x]
            bwd = [pltpu.roll(v, 7, 0) for v in x]
            w = lambda n: colw[n, :, tile(t)]
            for k in three:
                rows = pl.ds(here + 8 * k, 8)
                rw = lambda n: roww[n, rows, :]
                left = fwd[0] if k == 0 else jnp.where(sub == 0, fwd[k - 1], fwd[k])
                right = bwd[2] if k == 2 else jnp.where(sub == 7, bwd[k + 1], bwd[k])
                minus_b = now[0][k] if t == 0 else jnp.where(lane < 1, before[0][k], now[0][k])
                minus_a = now[1][k] if t == 0 else jnp.where(lane < PATCH, before[1][k], now[1][k])
                plus_b = now[2][k] if later is None else jnp.where(lane >= LANES - 1, later[2][k], now[2][k])
                plus_a = now[3][k] if later is None else jnp.where(lane >= LANES - PATCH, later[3][k], now[3][k])
                acc = rw(DN_IN) * at(t, k, below) + rw(UP_IN) * at(t, k, above) + rw(RT_IN) * right + rw(LF_IN) * left
                acc = acc + w(C_DN) * plus_a + w(C_UP) * minus_a + w(C_RT) * plus_b + w(C_LF) * minus_b
                if t <= 3:
                    acc = acc + w(C_RT_E) * heads[k][0]
                if t in (0, 3, 4):
                    acc = acc + w(C_RT_F) * heads[k][1]
                if 5 <= t <= 8:
                    acc = acc + w(C_LF_E) * tails[k][0]
                if t in (4, 5, 8):
                    acc = acc + w(C_LF_F) * tails[k][1]
                old = y1[p, rows, tile(t)]
                if final:
                    old = old + y[p, rows, tile(t)]
                new = old + acc if p == 0 else old - acc
                out[p, rows, tile(t)] = 0.5 * new if final else new
            before, now = now, later

    def step(a, carry):
        for p in range(2):
            strip(a, p)
        return carry

    lax.fori_loop(first, last, step, 0, unroll=next(n for n in (4, 3, 2, 1) if (last - first) % n == 0))


def unfolded(msg, at, lane):
    value = None
    for q in range(3):
        carrier = msg[pl.ds(pl.multiple_of(q * QUARTER + at, 8), 8), :]
        for source, to, count in FOLDS[q]:
            turned = pltpu.roll(carrier, (source - to) % LANES, 1)
            inside = jnp.logical_and(lane >= source, lane < source + count)
            value = turned if value is None else jnp.where(inside, turned, value)
    return value


def finish(stage, base, y, halos, roww, colw, out, e_row, e_col, chunk_done=None):
    face_a, face_b, side, down_a, down_b, across_a, across_b, table = halos
    scale = 0.5 if stage else 1.0
    row_id, col_id = place()
    up_first, even, row_up_first, row_even = parities()
    row_odd = lax.rem(row_id, 2)
    shift = jnp.where(even, 87, 41)
    lane = iota((8, LANES), 1)
    col_slot, row_slot = table[0:SLOT, :], table[SLOT : 2 * SLOT, :]
    for t in range(5):
        u = stage * TILES + t
        strip = jnp.where(row_odd == 1, row_slot[4 + u : 5 + u, :], row_slot[u : u + 1, :])
        e_row[t * LANES : (t + 1) * LANES, :] = jnp.broadcast_to(strip, (LANES, LANES)).T
    for t in range(TILES):
        e_col[:, tile(t)] = col_slot[stage * TILES + t : stage * TILES + t + 1, :] * colw[COL_U, :, tile(t)]

    def strip(a, folded):
        here = pl.multiple_of(a * PATCH, 8)
        near = pl.ds(pl.multiple_of(8 * (a // 8), 8), 8)
        to_first = lax.rem(8 - lax.rem(a, 8), 8)
        to_last = 7 - lax.rem(a, 8)
        half = a // (PATCH // 2)
        for k in range(3):
            rows = pl.ds(here + 8 * k, 8)
            es = e_row[pl.ds(64 * row_odd + here + 8 * k, 8), :] * roww[ROW_U, rows, :]
            if folded:
                got = [unfolded(m, here - 3 * QUARTER + 8 * k, lane) for m in (face_a, face_b)]
            else:
                got = [m[rows, :] for m in (face_a, face_b)]
            lower = jnp.where(up_first, got[0], got[1])
            upper = jnp.where(up_first, got[1], got[0])
            lowers = (lower, pltpu.roll(lower, 40, 1))
            uppers = (upper, pltpu.roll(upper, 88, 1))
            packed = side[pl.ds(pl.multiple_of(here - half * (SQUARE // 2), 8) + 8 * k, 8), :]
            gaps = [es - e_col[:, tile(t)] for t in range(TILES)]
            for p in range(2):
                q = 1 - p
                se, sf = [pltpu.roll(packed, lax.rem(shift + LANES - (4 * half + 2 * q + n), LANES), 1) for n in range(2)]
                for t in range(TILES):
                    w = lambda n: colw[n, :, tile(t)]
                    acc = gaps[t] * y[q, rows, tile(t)]
                    if t in (0, 4):
                        acc = acc + w(C_UP_RIM) * uppers[q]
                    if t in (4, 8):
                        acc = acc + w(C_DN_RIM) * lowers[q]
                    if t != 4:
                        acc = acc + w(C_X_E) * se
                    if t in (0, 3, 4, 5, 8):
                        acc = acc + w(C_X_F) * sf
                    if k != 1:
                        pair = [m[q, near, tile(t)] for m in (across_a, across_b)]
                    if k == 0:
                        left = pltpu.roll(jnp.where(row_even, pair[1], pair[0]), to_first, 0)
                        acc = acc + roww[LF_RIM, rows, :] * left
                    if k == 2:
                        right = pltpu.roll(jnp.where(row_even, pair[0], pair[1]), to_last, 0)
                        acc = acc + roww[RT_RIM, rows, :] * right
                    if scale != 1.0:
                        acc = scale * acc
                    old = base[p, rows, tile(t)]
                    out[p, rows, tile(t)] = old + acc if p == 0 else old - acc

    def rim(a, weight, first, second):
        for p in range(2):
            for k in range(3):
                rows = pl.ds(a * PATCH + 8 * k, 8)
                w = roww[weight, rows, :] * (scale if p == 0 else -scale)
                for t in range(TILES):
                    pair = [m[1 - p, 8 * k : 8 * k + 8, tile(t)] for m in (first, second)]
                    out[p, rows, tile(t)] += w * jnp.where(row_up_first, pair[0], pair[1])

    fold = 3 * PATCH // 4
    stops = (0, fold, PATCH) if chunk_done is None else (0, fold // 3, 2 * fold // 3, fold, PATCH - 2, PATCH)
    for start, stop in zip(stops, stops[1:]):
        lax.fori_loop(start, stop, lambda a, c, f=start >= fold: (strip(a, f), c)[1], 0, unroll=2)
        if start == 0:
            rim(0, UP_RIM, down_b, down_a)
        if stop == PATCH:
            rim(PATCH - 1, DN_RIM, down_a, down_b)
        if chunk_done is not None:
            chunk_done(start * PATCH, stop * PATCH)


def middle_kernel(base, y, *refs):
    halos, (roww, colw), (y1, *faces), (e_row, e_col) = refs[:8], refs[8:10], refs[10:18], refs[18:]
    finish(0, base, y, halos, roww, colw, y1, e_row, e_col)
    pack_faces(y1, *faces)


def last_kernel(base, y1, *refs):
    halos, (roww, colw), out_hbm, (e_row, e_col, out, sems) = refs[:8], refs[8:10], refs[10], refs[11:]
    copies = []

    def chunk_done(first, last):
        for p in range(2):
            rows = pl.ds(first, last - first)
            copies.append(pltpu.make_async_copy(out.at[p, rows], out_hbm.at[p, rows], sems.at[len(copies)]))
            copies[-1].start()

    finish(1, base, y1, halos, roww, colw, out, e_row, e_col, chunk_done)
    for c in copies:
        c.wait()


def on_chip(*shape):
    return pltpu.VMEM(shape, F32)


VM = pl.BlockSpec(memory_space=pltpu.VMEM)
STATE = (2, SQUARE, COLUMNS)
FACES = ((3 * QUARTER, LANES),) * 2 + ((SQUARE // 2, LANES),) + ((2, PATCH, COLUMNS),) * 4


def call(kernel, args, out_shapes, scratch=(), out_specs=None, aliases=None, loads=False):
    many = isinstance(out_shapes, (list, tuple))
    return pl.pallas_call(
        kernel,
        out_shape=out_shapes,
        in_specs=[pl.BlockSpec(memory_space=pl.ANY) if loads else VM] * len(args),
        out_specs=out_specs or ([VM] * len(out_shapes) if many else VM),
        scratch_shapes=list(scratch),
        input_output_aliases=aliases or {},
        compiler_params=pltpu.CompilerParams(vmem_limit_bytes=VMEM_LIMIT),
        cost_estimate=pl.CostEstimate(flops=1000, bytes_accessed=1000, transcendentals=0),
    )(*[pltpu.with_memory_space_constraint(x, pltpu.HBM if loads else pltpu.VMEM) for x in args])


def pairs(axis, linked):
    n = lax.axis_size(axis)
    found = [(i, j) for i in range(n) for j in range(i + 1, n) if linked(i, j)]
    return found + [(j, i) for i, j in found]


def traded(block, axis, linked):
    return lax.ppermute(block, axis, pairs(axis, linked))


def flipped(block, axis, bit):
    return traded(block, axis, lambda i, j: j == i ^ bit)


def tie(value, *after):
    def kernel(*refs):
        refs[-1][...] = refs[0][...]

    return call(kernel, (value, *after), on_chip(*value.shape))


def rows_of(*slots):
    return on_chip(sum(slots) * SLOT, LANES)


def slot(n):
    return pl.ds(pl.multiple_of(SLOT * n, 8), SLOT)


def grow(known, got, *after):
    rows = known.shape[0]

    def kernel(known, got, *refs):
        out = refs[-1]
        out[0:SLOT, :] = known[0:SLOT, :] + got[0:SLOT, :]
        out[SLOT:rows, :] = known[SLOT:rows, :]
        out[rows : 2 * rows - SLOT, :] = got[SLOT:rows, :]

    return call(kernel, (known, got, *after), on_chip(2 * rows - SLOT, LANES))


def added(known, got, *after):
    def kernel(known, got, *refs):
        refs[-1][...] = known[...] + got[...]

    return call(kernel, (known, got, *after), on_chip(*known.shape))


def halve_all(known, got, *after):
    def kernel(known, got, *refs):
        keep, send, table = refs[-3:]
        row_id, col_id = place()
        mine = row_id // 2
        for n, bits in enumerate((0, 2, 6, 4)):
            rows = slice(SLOT * (n + 1), SLOT * (n + 2))
            table[slot(mine ^ bits), :] = known[rows, :]
            table[slot(mine ^ 1 ^ bits), :] = got[rows, :]
        table[slot(col_id), :] += known[0:SLOT, :] + got[0:SLOT, :]
        half = col_id // 4
        for n in range(4):
            keep[SLOT * n : SLOT * (n + 1), :] = table[slot(4 * half + n), :]
            send[SLOT * n : SLOT * (n + 1), :] = table[slot(4 * (1 - half) + n), :]
        keep[4 * SLOT :, :] = table[slot(mine), :]
        send[4 * SLOT :, :] = table[slot(mine ^ 1), :]

    scratch = [pltpu.VMEM((8 * SLOT, LANES), F32)]
    return call(kernel, (known, got, *after), [rows_of(5), rows_of(5)], scratch)


def halve_four(known, got, *after):
    def kernel(known, got, *refs):
        keep, send, total = refs[-3:]
        z = lax.rem(place()[1], 4)
        total[...] = known[...] + got[...]
        for out, bits in ((keep, (0, 3)), (send, (1, 2))):
            for n in range(2):
                out[SLOT * n : SLOT * (n + 1), :] = total[slot(z ^ bits[n]), :]
            out[2 * SLOT :, :] = total[4 * SLOT :, :]

    return call(kernel, (known, got, *after), [rows_of(3), rows_of(3)], [pltpu.VMEM((5 * SLOT, LANES), F32)])


def halve_two(known, got, *after):
    def kernel(known, got, *refs):
        keep, send = refs[-2:]
        total = known[...] + got[...]
        keep[0:SLOT, :] = total[0:SLOT]
        send[0:SLOT, :] = total[SLOT : 2 * SLOT]
        keep[SLOT:, :] = total[2 * SLOT :]
        send[SLOT:, :] = total[2 * SLOT :]

    return call(kernel, (known, got, *after), [rows_of(2), rows_of(2)])


def swap_face_a(x):
    return flipped(x, "col", 2)


def swapped(x, partner):
    rows, cols = lax.axis_size("row"), lax.axis_size("col")
    places = [(r, c) for r in range(rows) for c in range(cols)]
    route = [(r * cols + c, partner(r, c)[0] * cols + partner(r, c)[1]) for r, c in places]
    return lax.ppermute(x, ("row", "col"), route)


def swap_face_b(x):
    return swapped(x, lambda r, c: (r, c ^ 6) if c // 2 in (1, 2) else (r ^ 1, c))


def swap_side(x):
    return flipped(x, "col", 1)


def swap_down_a(x):
    return flipped(x, "row", 4)


def swap_down_b(x):
    return flipped(x, "row", 12)


def swap_across_a(x):
    return flipped(x, "row", 1)


def swap_across_b(x):
    return swapped(x, lambda r, c: (r ^ 3, c) if r % 4 in (1, 2) else (r ^ 4, c))


def swap_bits(x, row_bits, col_bits):
    return swapped(x, lambda r, c: (r ^ row_bits, c ^ col_bits))


def first_exchange(faces, share, first_work, piece):
    face_a, face_b, side, down_a, down_b, across_a, across_b = faces
    side = swap_side(side)
    face_b = swap_face_b(face_b)
    face_a = swap_face_a(face_a)
    known = grow(share, flipped(share, "row", 4), first_work)
    part = piece(0, None, known)
    known = grow(known, flipped(known, "row", 12), part)
    down_a = swap_down_a(tie(down_a, known))
    known = added(known, flipped(known, "row", 1), side)
    down_b = swap_down_b(tie(down_b, known))
    known, send = halve_all(known, flipped(known, "row", 2), face_a, face_b)
    across_b = swap_across_b(tie(across_b, known))
    part = piece(1, part, known)
    known, send = halve_four(known, swap_bits(send, 2, 4), part, down_a, down_b)
    across_a = swap_across_a(tie(across_a, known))
    part = piece(2, part, known)
    known, send = halve_two(known, flipped(send, "col", 1), part, across_b)
    part = piece(3, part, known)
    table = added(known, flipped(send, "col", 3), part, across_a)
    return part, (face_a, face_b, side, down_a, down_b, across_a, across_b, table)


def second_exchange(faces, table, piece):
    face_a, face_b, side, down_a, down_b, across_a, across_b = faces
    face_b = swap_face_b(face_b)
    face_a = swap_face_a(face_a)
    across_a = swap_across_a(across_a)
    across_b = swap_across_b(across_b)
    side = swap_side(side)
    part = piece(0, None)
    down_a = swap_down_a(tie(down_a, part))
    part = piece(1, part, across_a)
    down_b = swap_down_b(tie(down_b, part))
    part = piece(2, part, side)
    part = piece(3, part)
    part = piece(4, part)
    part = piece(5, part)
    return part, (face_a, face_b, side, down_a, down_b, across_a, across_b, table)


def interior(final, y1, y, weights, stops):
    def piece(n, part, *after):
        kernel = functools.partial(interior_kernel, final, stops[n], stops[n + 1])
        args = (*after, y1, y, *weights)
        if n == 0:
            return call(kernel, args, on_chip(*STATE))
        return call(kernel, (part, *args), on_chip(*STATE), aliases={0: 0})

    return piece


def local(corr, bonds_down, bonds_across, repulsion):
    faces_out = [on_chip(*s) for s in FACES]
    e_scratch = [pltpu.VMEM((5 * LANES, LANES), F32), pltpu.VMEM((8, COLUMNS), F32)]
    y, bonds, colw, *faces, share = call(
        first_kernel,
        (corr, bonds_down, bonds_across, repulsion),
        [on_chip(*STATE), on_chip(3, LATTICE, LATTICE), on_chip(17, 8, COLUMNS), *faces_out, on_chip(2 * SLOT, LANES)],
        [
            pltpu.VMEM((5 * LANES, LANES), F32),
            pltpu.VMEM((2, TILES, 8, LANES), F32),
            pltpu.VMEM((TILES, 8, LANES), jnp.int32),
            pltpu.SemaphoreType.DMA((3 + 8 * CHUNKS,)),
        ],
        loads=True,
    )
    weights = (call(row_weights_kernel, (bonds,), on_chip(9, SQUARE, LANES)), colw)
    part, halos = first_exchange(faces, share, weights[0], interior(False, y, y, weights, (0, 8, 12, 18, 24)))
    y1, *faces = call(middle_kernel, (part, y, *halos, *weights), [on_chip(*STATE), *faces_out], e_scratch)
    part, halos = second_exchange(faces, halos[-1], interior(True, y1, y, weights, (0, 4, 8, 12, 16, 20, 24)))
    return call(
        last_kernel,
        (part, y1, *halos, *weights),
        jax.ShapeDtypeStruct(STATE, F32),
        [*e_scratch, pltpu.VMEM(STATE, F32), pltpu.SemaphoreType.DMA((10,))],
        out_specs=pl.BlockSpec(memory_space=pl.ANY),
    )


def solution(mesh):
    in_specs = (P(None, "row", "col"), P(), P(), P())
    out_specs = P(None, "row", "col")
    return jax.shard_map(local, mesh=mesh, in_specs=in_specs, out_specs=out_specs, check_vma=False)
```

```python
import functools

import jax
import jax.numpy as jnp
from jax import lax
from jax.experimental import pallas as pl
from jax.experimental.pallas import tpu as pltpu
from jax.sharding import PartitionSpec as P

PATCH = 24
SQUARE = PATCH * PATCH
COLUMNS = 2 * SQUARE
LANES = 128
TILES = COLUMNS // LANES
LATTICE = 4 * PATCH
TIME_STEP = 0.04
F32 = jnp.float32
VMEM_LIMIT = 8 * 1024 * 1024

DN_IN, UP_IN, RT_IN, LF_IN, DN_RIM, UP_RIM, RT_RIM, LF_RIM, ROW_U = range(9)
C_DN, C_UP, C_RT, C_LF, C_DN_RIM, C_UP_RIM, C_RT_E, C_RT_F, C_LF_E, C_LF_F, C_X_E, C_X_F, COL_U, C_DN_ALL, C_UP_ALL, C_RT_ALL, C_LF_ALL = range(17)


def iota(shape, dim):
    return lax.broadcasted_iota(jnp.int32, shape, dim)


def over24(x):
    return ((x.astype(F32) + 0.5) * (1.0 / PATCH)).astype(jnp.int32)


def on(mask):
    return jnp.where(mask, 1.0, 0.0).astype(F32)


def within(x, lo, hi):
    return on(x >= lo) * on(x <= hi)


def place():
    return lax.axis_index("row"), lax.axis_index("col")


def tile(t):
    return pl.ds(t * LANES, LANES)


def tables(bonds):
    side = (LATTICE, LATTICE)
    down = jnp.where(iota(side, 0) < LATTICE - 1, bonds[0], 0.0)
    across = jnp.where(iota(side, 1) < LATTICE - 1, bonds[1], 0.0)
    rep = bonds[2]
    dot = functools.partial(jnp.dot, precision=lax.Precision.HIGHEST, preferred_element_type=F32)
    return down, across, rep, dot


def row_weights_kernel(bonds, roww):
    row_id, _ = place()
    down, across, rep, dot = tables(bonds)
    s = iota((SQUARE, LATTICE), 0)
    lane = iota((SQUARE, LATTICE), 1)
    a = over24(s)
    b = s - PATCH * a
    ga = PATCH * (row_id // 4) + a
    gb = PATCH * (row_id % 4) + b

    def pick_rows(table, da, db):
        rows = dot(on(lane == ga + da), table)
        return jnp.sum(jnp.where(lane == gb + db, rows, 0.0), axis=1, keepdims=True)

    a1 = a[:, 0:1]
    b1 = b[:, 0:1]
    last = PATCH - 1
    dn = -TIME_STEP * pick_rows(down, 0, 0)
    up = -TIME_STEP * pick_rows(down, -1, 0)
    rt = -TIME_STEP * pick_rows(across, 0, 0)
    lf = -TIME_STEP * pick_rows(across, 0, -1)
    values = {
        DN_IN: dn * on(a1 < last), UP_IN: up * on(a1 > 0), RT_IN: rt * on(b1 < last), LF_IN: lf * on(b1 > 0),
        DN_RIM: dn * on(a1 == last), UP_RIM: up * on(a1 == 0), RT_RIM: rt * on(b1 == last), LF_RIM: lf * on(b1 == 0),
        ROW_U: TIME_STEP * pick_rows(rep, 0, 0),
    }
    for k, v in values.items():
        roww[k] = jnp.broadcast_to(v, (SQUARE, LANES))


def col_weights(bonds, colw):
    _, col_id = place()
    down, across, rep, _ = tables(bonds)
    last = PATCH - 1
    wide = (LATTICE, COLUMNS)
    j = iota(wide, 1)
    g = (j >= SQUARE).astype(jnp.int32)
    jj = j - SQUARE * g
    a = over24(jj)
    b = jj - PATCH * a
    sub = iota(wide, 0)
    parity = col_id % 2
    ga = PATCH * (col_id // 2) + a
    gb = PATCH * (2 * parity + g) + b

    def columns_of(tables, db):
        stacked = jnp.concatenate(tables, 0)
        parts = []
        for _ in range(3):
            parts.append(stacked.astype(jnp.bfloat16))
            stacked = stacked - parts[-1].astype(F32)
        hot = on(sub == gb + db).astype(jnp.bfloat16)
        high, mid, low = [jnp.dot(v, hot, preferred_element_type=F32) for v in parts]
        return (high + mid) + low

    def pick(columns, n, da):
        rows = columns[n * LATTICE : (n + 1) * LATTICE]
        return jnp.sum(jnp.where(sub == ga + da, rows, 0.0), axis=0, keepdims=True)

    here = columns_of([down, across, rep], 0)
    before = columns_of([across], -1)
    a = a[0:1]
    b = b[0:1]
    g = g[0:1]
    dn = TIME_STEP * pick(here, 0, 0)
    up = TIME_STEP * pick(here, 0, -1)
    rt = TIME_STEP * pick(here, 1, 0)
    lf = TIME_STEP * pick(before, 0, 0)
    tails0 = rt * on(b == last) * on(g == 0)
    heads1 = lf * on(b == 0) * on(g == 1)
    tails1 = rt * on(b == last) * on(g == 1)
    heads0 = lf * on(b == 0) * on(g == 0)
    even = on(jnp.full(a.shape, parity, jnp.int32) == 0)
    x_even = even * tails1
    x_odd = (1.0 - even) * heads0
    rt_e = within(a, 3, 18)
    lf_e = within(a, 5, 20)
    xe_e = within(a, 6, 21)
    xo_e = within(a, 2, 17)
    values = {
        C_DN: dn * on(a < last), C_UP: up * on(a > 0), C_RT: rt * on(b < last), C_LF: lf * on(b > 0),
        C_DN_RIM: dn * on(a == last), C_UP_RIM: up * on(a == 0),
        C_RT_E: tails0 * rt_e, C_RT_F: tails0 * (1.0 - rt_e),
        C_LF_E: heads1 * lf_e, C_LF_F: heads1 * (1.0 - lf_e),
        C_X_E: x_even * xe_e + x_odd * xo_e, C_X_F: x_even * (1.0 - xe_e) + x_odd * (1.0 - xo_e),
        COL_U: TIME_STEP * pick(here, 2, 0),
        C_DN_ALL: dn, C_UP_ALL: up, C_RT_ALL: rt, C_LF_ALL: lf,
    }
    for k, v in values.items():
        colw[k] = jnp.broadcast_to(v, (8, COLUMNS))


STRIP = (PATCH, LANES)


def squeeze_cols(tiles, lane24, m1, m2, n0):
    e = jnp.where(lane24 == m1, tiles[1], jnp.where(lane24 == m2, tiles[2], tiles[3]))
    f = jnp.where(lane24 == n0, tiles[0], tiles[4])
    return e, f


def lane_maps(shape=STRIP):
    lane = iota(shape, 1)
    return lane, lane - PATCH * over24(lane)


def parities():
    row_id, col_id = place()
    return lax.rem(col_id // 2, 2) == 0, lax.rem(col_id, 2) == 0, lax.rem(row_id // 4, 2) == 0, lax.rem(row_id, 2) == 0


FOLDS = (((0, 24, 16), (16, 88, 8), (40, 96, 8)), ((48, 24, 16), (64, 88, 16)), ((80, 24, 8), (104, 32, 8), (112, 88, 16)))
QUARTER = SQUARE // 4


def pack_faces(src, face_a, face_b, side, down_a, down_b, across_a, across_b, ready=None):
    up_first, even, row_up_first, row_even = parities()
    base = jnp.where(even, 4 * LANES, 0)
    lane, lane24 = lane_maps()
    lane8 = lax.rem(lane, 8)
    m1 = jnp.where(even, 7, 16)
    m2 = jnp.where(even, 23, 8)
    n0 = jnp.where(even, 15, 0)
    v0 = jnp.where(even, 7, 0)
    low = lane < 64
    half = lax.rem(lane, 64)
    first_part = half < PATCH
    last_part = half >= 64 - PATCH

    def faces(rows):
        edge = [[src[p, rows, tile(t)] for t in (0, 4, 8)] for p in range(2)]
        top = [jnp.where(low, e[0], e[1]) for e in edge]
        bot = [jnp.where(low, e[1], e[2]) for e in edge]
        top = jnp.where(last_part, pltpu.roll(top[0], 40, 1), top[1])
        bot = jnp.where(first_part, pltpu.roll(bot[0], 88, 1), bot[1])
        return jnp.where(up_first, bot, top), jnp.where(up_first, top, bot)

    def squeezed(rows):
        out = []
        for p in range(2):
            tiles = [src[p, rows, pl.ds(pl.multiple_of(base + LANES * t, LANES), LANES)] for t in range(5)]
            out += squeeze_cols(tiles, lane24, m1, m2, n0)
        return out

    def step(k, carry):
        at = [pl.ds(pl.multiple_of(q * QUARTER + k * PATCH, 8), PATCH) for q in range(4)]
        whole = [faces(rows) for rows in at]
        for n, msg in enumerate((face_a, face_b)):
            turned = {d: pltpu.roll(whole[3][n], d, 1) for d in (24, 56, 72, 104)}
            for q in range(3):
                value = whole[q][n]
                for source, to, count in FOLDS[q]:
                    value = jnp.where(jnp.logical_and(lane >= to, lane < to + count), turned[(to - source) % LANES], value)
                msg[at[q], :] = value
        for h in range(2):
            msg = None
            for slot, v in enumerate(squeezed(at[h]) + squeezed(at[h + 2])):
                msg = v if slot == 0 else jnp.where(lane8 == lax.rem(v0 + slot, 8), pltpu.roll(v, slot, 1), msg)
            side[at[h], :] = msg
        return carry

    steps = PATCH // 4
    if ready is None:
        lax.fori_loop(0, steps, step, 0, unroll=2)
    else:
        for i in range(CHUNKS):
            ready(i)
            lax.fori_loop(i * steps // CHUNKS, (i + 1) * steps // CHUNKS, step, 0, unroll=2)
    for p in range(2):
        for out, flip in ((down_a, row_up_first), (down_b, jnp.logical_not(row_up_first))):
            out[p] = src[p, pl.ds(pl.multiple_of(jnp.where(flip, SQUARE - PATCH, 0), 8), PATCH), :]
        for a in range(PATCH):
            left = src[p, a * PATCH : a * PATCH + 1, :]
            right = src[p, a * PATCH + PATCH - 1 : a * PATCH + PATCH, :]
            across_a[p, a : a + 1, :] = jnp.where(row_even, right, left)
            across_b[p, a : a + 1, :] = jnp.where(row_even, left, right)


SLOT = 24


def pack_densities(src, colw, slots, row_sums, sums, codes):
    row_id, col_id = place()
    odd = lax.rem(row_id, 2)
    across = lax.rem(row_id, 4) - 2 * lax.rem(col_id, 2)
    along = row_id // 4 - col_id // 2
    beside = jnp.logical_and(along == 0, jnp.logical_and(across >= -1, across <= 2))
    over = jnp.logical_and(jnp.abs(along) == 1, jnp.logical_and(across >= 0, across <= 1))
    slots[...] = jnp.zeros(slots.shape, F32)

    @pl.when(jnp.logical_or(beside, over))
    def _():
        row_sums[...] = jnp.zeros(row_sums.shape, F32)
        sums[...] = jnp.zeros(sums.shape, F32)
        lane = iota((8, LANES), 1)
        sub = iota((8, LANES), 0)
        for t in range(TILES):
            j = lane + t * LANES
            g = (j >= SQUARE).astype(jnp.int32)
            a = over24(j - SQUARE * g)
            b = j - SQUARE * g - PATCH * a
            codes[t] = 100 * (PATCH * (col_id // 2) + a) + PATCH * (2 * lax.rem(col_id, 2) + g) + b
        first = 100 * PATCH * (row_id // 4) + PATCH * lax.rem(row_id, 4)

        def share(a, tiles):
            along_rows = [jnp.zeros((8, LANES), F32) for _ in range(3)]
            for t in tiles:
                cols = pl.ds(pl.multiple_of(t * LANES, LANES), LANES)
                now = middle = jnp.zeros((8, LANES), F32)
                for k in range(3):
                    rows = pl.ds(pl.multiple_of(a * PATCH + 8 * k, 8), 8)
                    apart = first + 100 * a + 8 * k + sub - codes[t]
                    w = jnp.where(apart == 100, colw[C_DN_ALL, :, cols], 0.0)
                    w = jnp.where(apart == -100, colw[C_UP_ALL, :, cols], w)
                    w = jnp.where(apart == 1, colw[C_RT_ALL, :, cols], w)
                    w = jnp.where(apart == -1, colw[C_LF_ALL, :, cols], w)
                    flow = w * src[1, rows, cols]
                    own = jnp.where(apart == 0, src[0, rows, cols], 0.0)
                    now = now + own
                    middle = middle + own - flow
                    along_rows[k] = along_rows[k] + flow
                sums[0, t] += now
                sums[1, t] += middle
            for k in range(3):
                row_sums[pl.ds(pl.multiple_of(64 * odd + a * PATCH + 8 * k, 8), 8), :] = along_rows[k]

        @pl.when(beside)
        def _():
            def step(a, carry):
                starts = [jnp.clip(SQUARE * g + PATCH * (a - 1), 0, (TILES - 2) * LANES) // LANES for g in range(2)]
                share(a, [start + d for start in starts for d in range(2)])
                return carry

            lax.fori_loop(0, PATCH, step, 0, unroll=3)

        @pl.when(over)
        def _():
            start = jnp.where(along == 1, 4, 0)
            share(jnp.where(along == 1, 0, PATCH - 1), [start, start + 4])

        for t in range(TILES):
            slots[t : t + 1, :] = jnp.sum(sums[0, t], axis=0, keepdims=True)
            slots[TILES + t : TILES + t + 1, :] = jnp.sum(sums[1, t], axis=0, keepdims=True)
        for t in range(5):
            got = jnp.sum(row_sums[t * LANES : (t + 1) * LANES, :].T, axis=0, keepdims=True)
            slots[pl.ds(SLOT + TILES + 4 * odd + t, 1), :] = got


CHUNKS = 3


def first_kernel(corr, down, across, rep, y, bonds, colw, *refs):
    faces, table, (*scratch, sems) = refs[:7], refs[7], refs[8:]
    tables_in = [pltpu.make_async_copy(v, bonds.at[n], sems.at[n]) for n, v in enumerate((down, across, rep))]
    step = QUARTER // CHUNKS
    chunks = []
    for i in range(CHUNKS):
        chunks.append([])
        for q in range(4):
            for p in range(2):
                rows = pl.ds(q * QUARTER + i * step, step)
                sem = sems.at[3 + (i * 4 + q) * 2 + p]
                chunks[-1].append(pltpu.make_async_copy(corr.at[p, rows], y.at[p, rows], sem))
    for c in sum([tables_in, *chunks], []):
        c.start()
    for c in tables_in:
        c.wait()
    col_weights(bonds, colw)

    def ready(i):
        for c in chunks[i]:
            c.wait()

    pack_faces(y, *faces, ready=ready)
    pack_densities(y, colw, table, *scratch)


def interior_kernel(final, first, last, *refs):
    y1, y, roww, colw, out = refs[-5:]
    sub = iota((8, LANES), 0)
    lane, lane24 = lane_maps((8, LANES))
    three = range(3)

    def strip(a, p):
        q = 1 - p
        here = pl.multiple_of(a * PATCH, 8)
        above = pl.multiple_of(jnp.maximum(a - 1, 0) * PATCH, 8)
        below = pl.multiple_of(jnp.minimum(a + 1, PATCH - 1) * PATCH, 8)

        def at(t, k, start=here):
            return y1[q, pl.ds(start + 8 * k, 8), tile(t)]

        def side(t0, m1, m2, n0, shift):
            pairs = [squeeze_cols([at(t0 + t, k) for t in range(5)], lane24, m1, m2, n0) for k in three]
            return [[pltpu.roll(v, shift, 1) for v in pair] for pair in pairs]

        def turned(t):
            x = [at(t, k) for k in three]
            return [[pltpu.roll(v, n, 1) for v in x] for n in (1, PATCH, LANES - 1, LANES - PATCH)]

        heads = side(4, 8, 0, 16, 87)
        tails = None
        before, now = None, turned(0)
        for t in range(TILES):
            later = turned(t + 1) if t < TILES - 1 else None
            if t == 4:
                tails = side(0, 15, 7, 23, 41)
            x = [at(t, k) for k in three]
            fwd = [pltpu.roll(v, 1, 0) for v in x]
            bwd = [pltpu.roll(v, 7, 0) for v in x]
            w = lambda n: colw[n, :, tile(t)]
            for k in three:
                rows = pl.ds(here + 8 * k, 8)
                rw = lambda n: roww[n, rows, :]
                left = fwd[0] if k == 0 else jnp.where(sub == 0, fwd[k - 1], fwd[k])
                right = bwd[2] if k == 2 else jnp.where(sub == 7, bwd[k + 1], bwd[k])
                minus_b = now[0][k] if t == 0 else jnp.where(lane < 1, before[0][k], now[0][k])
                minus_a = now[1][k] if t == 0 else jnp.where(lane < PATCH, before[1][k], now[1][k])
                plus_b = now[2][k] if later is None else jnp.where(lane >= LANES - 1, later[2][k], now[2][k])
                plus_a = now[3][k] if later is None else jnp.where(lane >= LANES - PATCH, later[3][k], now[3][k])
                acc = rw(DN_IN) * at(t, k, below) + rw(UP_IN) * at(t, k, above) + rw(RT_IN) * right + rw(LF_IN) * left
                acc = acc + w(C_DN) * plus_a + w(C_UP) * minus_a + w(C_RT) * plus_b + w(C_LF) * minus_b
                if t <= 3:
                    acc = acc + w(C_RT_E) * heads[k][0]
                if t in (0, 3, 4):
                    acc = acc + w(C_RT_F) * heads[k][1]
                if 5 <= t <= 8:
                    acc = acc + w(C_LF_E) * tails[k][0]
                if t in (4, 5, 8):
                    acc = acc + w(C_LF_F) * tails[k][1]
                old = y1[p, rows, tile(t)]
                if final:
                    old = old + y[p, rows, tile(t)]
                new = old + acc if p == 0 else old - acc
                out[p, rows, tile(t)] = 0.5 * new if final else new
            before, now = now, later

    def step(a, carry):
        for p in range(2):
            strip(a, p)
        return carry

    lax.fori_loop(first, last, step, 0, unroll=next(n for n in (4, 3, 2, 1) if (last - first) % n == 0))


def unfolded(msg, at, lane):
    value = None
    for q in range(3):
        carrier = msg[pl.ds(pl.multiple_of(q * QUARTER + at, 8), 8), :]
        for source, to, count in FOLDS[q]:
            turned = pltpu.roll(carrier, (source - to) % LANES, 1)
            inside = jnp.logical_and(lane >= source, lane < source + count)
            value = turned if value is None else jnp.where(inside, turned, value)
    return value


def finish(stage, base, y, halos, roww, colw, out, e_row, e_col, chunk_done=None):
    face_a, face_b, side, down_a, down_b, across_a, across_b, table = halos
    scale = 0.5 if stage else 1.0
    row_id, col_id = place()
    up_first, even, row_up_first, row_even = parities()
    row_odd = lax.rem(row_id, 2)
    shift = jnp.where(even, 87, 41)
    lane = iota((8, LANES), 1)
    col_slot, row_slot = table[0:SLOT, :], table[SLOT : 2 * SLOT, :]
    for t in range(5):
        u = stage * TILES + t
        strip = jnp.where(row_odd == 1, row_slot[4 + u : 5 + u, :], row_slot[u : u + 1, :])
        e_row[t * LANES : (t + 1) * LANES, :] = jnp.broadcast_to(strip, (LANES, LANES)).T
    for t in range(TILES):
        e_col[:, tile(t)] = col_slot[stage * TILES + t : stage * TILES + t + 1, :] * colw[COL_U, :, tile(t)]

    def strip(a, folded):
        here = pl.multiple_of(a * PATCH, 8)
        near = pl.ds(pl.multiple_of(8 * (a // 8), 8), 8)
        to_first = lax.rem(8 - lax.rem(a, 8), 8)
        to_last = 7 - lax.rem(a, 8)
        half = a // (PATCH // 2)
        for k in range(3):
            rows = pl.ds(here + 8 * k, 8)
            es = e_row[pl.ds(64 * row_odd + here + 8 * k, 8), :] * roww[ROW_U, rows, :]
            if folded:
                got = [unfolded(m, here - 3 * QUARTER + 8 * k, lane) for m in (face_a, face_b)]
            else:
                got = [m[rows, :] for m in (face_a, face_b)]
            lower = jnp.where(up_first, got[0], got[1])
            upper = jnp.where(up_first, got[1], got[0])
            lowers = (lower, pltpu.roll(lower, 40, 1))
            uppers = (upper, pltpu.roll(upper, 88, 1))
            packed = side[pl.ds(pl.multiple_of(here - half * (SQUARE // 2), 8) + 8 * k, 8), :]
            gaps = [es - e_col[:, tile(t)] for t in range(TILES)]
            for p in range(2):
                q = 1 - p
                se, sf = [pltpu.roll(packed, lax.rem(shift + LANES - (4 * half + 2 * q + n), LANES), 1) for n in range(2)]
                for t in range(TILES):
                    w = lambda n: colw[n, :, tile(t)]
                    acc = gaps[t] * y[q, rows, tile(t)]
                    if t in (0, 4):
                        acc = acc + w(C_UP_RIM) * uppers[q]
                    if t in (4, 8):
                        acc = acc + w(C_DN_RIM) * lowers[q]
                    if t != 4:
                        acc = acc + w(C_X_E) * se
                    if t in (0, 3, 4, 5, 8):
                        acc = acc + w(C_X_F) * sf
                    if k != 1:
                        pair = [m[q, near, tile(t)] for m in (across_a, across_b)]
                    if k == 0:
                        left = pltpu.roll(jnp.where(row_even, pair[1], pair[0]), to_first, 0)
                        acc = acc + roww[LF_RIM, rows, :] * left
                    if k == 2:
                        right = pltpu.roll(jnp.where(row_even, pair[0], pair[1]), to_last, 0)
                        acc = acc + roww[RT_RIM, rows, :] * right
                    if scale != 1.0:
                        acc = scale * acc
                    old = base[p, rows, tile(t)]
                    out[p, rows, tile(t)] = old + acc if p == 0 else old - acc

    def rim(a, weight, first, second):
        for p in range(2):
            for k in range(3):
                rows = pl.ds(a * PATCH + 8 * k, 8)
                w = roww[weight, rows, :] * (scale if p == 0 else -scale)
                for t in range(TILES):
                    pair = [m[1 - p, 8 * k : 8 * k + 8, tile(t)] for m in (first, second)]
                    out[p, rows, tile(t)] += w * jnp.where(row_up_first, pair[0], pair[1])

    fold = 3 * PATCH // 4
    stops = (0, fold, PATCH) if chunk_done is None else (0, fold // 3, 2 * fold // 3, fold, PATCH - 2, PATCH)
    for start, stop in zip(stops, stops[1:]):
        lax.fori_loop(start, stop, lambda a, c, f=start >= fold: (strip(a, f), c)[1], 0, unroll=3 if (stop - start) % 3 == 0 else 2)
        if start == 0:
            rim(0, UP_RIM, down_b, down_a)
        if stop == PATCH:
            rim(PATCH - 1, DN_RIM, down_a, down_b)
        if chunk_done is not None:
            chunk_done(start * PATCH, stop * PATCH)


def middle_kernel(base, y, *refs):
    halos, (roww, colw), (y1, *faces), (e_row, e_col) = refs[:8], refs[8:10], refs[10:18], refs[18:]
    finish(0, base, y, halos, roww, colw, y1, e_row, e_col)
    pack_faces(y1, *faces)


def last_kernel(base, y1, *refs):
    halos, (roww, colw), out_hbm, (e_row, e_col, out, sems) = refs[:8], refs[8:10], refs[10], refs[11:]
    copies = []

    def chunk_done(first, last):
        for p in range(2):
            rows = pl.ds(first, last - first)
            copies.append(pltpu.make_async_copy(out.at[p, rows], out_hbm.at[p, rows], sems.at[len(copies)]))
            copies[-1].start()

    finish(1, base, y1, halos, roww, colw, out, e_row, e_col, chunk_done)
    for c in copies:
        c.wait()


def on_chip(*shape):
    return pltpu.VMEM(shape, F32)


VM = pl.BlockSpec(memory_space=pltpu.VMEM)
STATE = (2, SQUARE, COLUMNS)
FACES = ((3 * QUARTER, LANES),) * 2 + ((SQUARE // 2, LANES),) + ((2, PATCH, COLUMNS),) * 4


def call(kernel, args, out_shapes, scratch=(), out_specs=None, aliases=None, loads=False):
    many = isinstance(out_shapes, (list, tuple))
    return pl.pallas_call(
        kernel,
        out_shape=out_shapes,
        in_specs=[pl.BlockSpec(memory_space=pl.ANY) if loads else VM] * len(args),
        out_specs=out_specs or ([VM] * len(out_shapes) if many else VM),
        scratch_shapes=list(scratch),
        input_output_aliases=aliases or {},
        compiler_params=pltpu.CompilerParams(vmem_limit_bytes=VMEM_LIMIT),
        cost_estimate=pl.CostEstimate(flops=1000, bytes_accessed=1000, transcendentals=0),
    )(*[pltpu.with_memory_space_constraint(x, pltpu.HBM if loads else pltpu.VMEM) for x in args])


def pairs(axis, linked):
    n = lax.axis_size(axis)
    found = [(i, j) for i in range(n) for j in range(i + 1, n) if linked(i, j)]
    return found + [(j, i) for i, j in found]


def traded(block, axis, linked):
    return lax.ppermute(block, axis, pairs(axis, linked))


def flipped(block, axis, bit):
    return traded(block, axis, lambda i, j: j == i ^ bit)


def tie(value, *after):
    def kernel(*refs):
        refs[-1][...] = refs[0][...]

    return call(kernel, (value, *after), on_chip(*value.shape))


def rows_of(*slots):
    return on_chip(sum(slots) * SLOT, LANES)


def slot(n):
    return pl.ds(pl.multiple_of(SLOT * n, 8), SLOT)


def grow(known, got, *after):
    rows = known.shape[0]

    def kernel(known, got, *refs):
        out = refs[-1]
        out[0:SLOT, :] = known[0:SLOT, :] + got[0:SLOT, :]
        out[SLOT:rows, :] = known[SLOT:rows, :]
        out[rows : 2 * rows - SLOT, :] = got[SLOT:rows, :]

    return call(kernel, (known, got, *after), on_chip(2 * rows - SLOT, LANES))


def added(known, got, *after):
    def kernel(known, got, *refs):
        refs[-1][...] = known[...] + got[...]

    return call(kernel, (known, got, *after), on_chip(*known.shape))


def halve_all(known, got, *after):
    def kernel(known, got, *refs):
        keep, send, table = refs[-3:]
        row_id, col_id = place()
        mine = row_id // 2
        for n, bits in enumerate((0, 2, 6, 4)):
            rows = slice(SLOT * (n + 1), SLOT * (n + 2))
            table[slot(mine ^ bits), :] = known[rows, :]
            table[slot(mine ^ 1 ^ bits), :] = got[rows, :]
        table[slot(col_id), :] += known[0:SLOT, :] + got[0:SLOT, :]
        half = col_id // 4
        for n in range(4):
            keep[SLOT * n : SLOT * (n + 1), :] = table[slot(4 * half + n), :]
            send[SLOT * n : SLOT * (n + 1), :] = table[slot(4 * (1 - half) + n), :]
        keep[4 * SLOT :, :] = table[slot(mine), :]
        send[4 * SLOT :, :] = table[slot(mine ^ 1), :]

    scratch = [pltpu.VMEM((8 * SLOT, LANES), F32)]
    return call(kernel, (known, got, *after), [rows_of(5), rows_of(5)], scratch)


def halve_four(known, got, *after):
    def kernel(known, got, *refs):
        keep, send, total = refs[-3:]
        z = lax.rem(place()[1], 4)
        total[...] = known[...] + got[...]
        for out, bits in ((keep, (0, 3)), (send, (1, 2))):
            for n in range(2):
                out[SLOT * n : SLOT * (n + 1), :] = total[slot(z ^ bits[n]), :]
            out[2 * SLOT :, :] = total[4 * SLOT :, :]

    return call(kernel, (known, got, *after), [rows_of(3), rows_of(3)], [pltpu.VMEM((5 * SLOT, LANES), F32)])


def halve_two(known, got, *after):
    def kernel(known, got, *refs):
        keep, send = refs[-2:]
        total = known[...] + got[...]
        keep[0:SLOT, :] = total[0:SLOT]
        send[0:SLOT, :] = total[SLOT : 2 * SLOT]
        keep[SLOT:, :] = total[2 * SLOT :]
        send[SLOT:, :] = total[2 * SLOT :]

    return call(kernel, (known, got, *after), [rows_of(2), rows_of(2)])


def swap_face_a(x):
    return flipped(x, "col", 2)


def swapped(x, partner):
    rows, cols = lax.axis_size("row"), lax.axis_size("col")
    places = [(r, c) for r in range(rows) for c in range(cols)]
    route = [(r * cols + c, partner(r, c)[0] * cols + partner(r, c)[1]) for r, c in places]
    return lax.ppermute(x, ("row", "col"), route)


def swap_face_b(x):
    return swapped(x, lambda r, c: (r, c ^ 6) if c // 2 in (1, 2) else (r ^ 1, c))


def swap_side(x):
    return flipped(x, "col", 1)


def swap_down_a(x):
    return flipped(x, "row", 4)


def swap_down_b(x):
    return flipped(x, "row", 12)


def swap_across_a(x):
    return flipped(x, "row", 1)


def swap_across_b(x):
    return swapped(x, lambda r, c: (r ^ 3, c) if r % 4 in (1, 2) else (r ^ 4, c))


def swap_bits(x, row_bits, col_bits):
    return swapped(x, lambda r, c: (r ^ row_bits, c ^ col_bits))


def first_exchange(faces, share, first_work, piece):
    face_a, face_b, side, down_a, down_b, across_a, across_b = faces
    side = swap_side(side)
    face_b = swap_face_b(face_b)
    face_a = swap_face_a(face_a)
    known = grow(share, flipped(share, "row", 4), first_work)
    known = grow(known, flipped(known, "row", 12))
    down_a = swap_down_a(tie(down_a, known))
    known = added(known, flipped(known, "row", 1), side)
    down_b = swap_down_b(tie(down_b, known))
    part = piece(0, None, known)
    known, send = halve_all(known, flipped(known, "row", 2), part, face_b, face_a)
    across_b = swap_across_b(tie(across_b, known))
    part = piece(1, part, known)
    known, send = halve_four(known, swap_bits(send, 2, 4), part, down_a, down_b)
    across_a = swap_across_a(tie(across_a, known))
    part = piece(2, part, known)
    known, send = halve_two(known, flipped(send, "col", 1), part, across_b)
    part = piece(3, part, known)
    table = added(known, flipped(send, "col", 3), part, across_a)
    return part, (face_a, face_b, side, down_a, down_b, across_a, across_b, table)


def second_exchange(faces, table, piece):
    face_a, face_b, side, down_a, down_b, across_a, across_b = faces
    face_b = swap_face_b(face_b)
    face_a = swap_face_a(face_a)
    across_a = swap_across_a(across_a)
    across_b = swap_across_b(across_b)
    side = swap_side(side)
    part = piece(0, None)
    down_a = swap_down_a(tie(down_a, part))
    part = piece(1, part, across_a)
    down_b = swap_down_b(tie(down_b, part))
    part = piece(2, part, side)
    part = piece(3, part)
    part = piece(4, part)
    part = piece(5, part)
    return part, (face_a, face_b, side, down_a, down_b, across_a, across_b, table)


def interior(final, y1, y, weights, stops):
    def piece(n, part, *after):
        kernel = functools.partial(interior_kernel, final, stops[n], stops[n + 1])
        args = (*after, y1, y, *weights)
        if n == 0:
            return call(kernel, args, on_chip(*STATE))
        return call(kernel, (part, *args), on_chip(*STATE), aliases={0: 0})

    return piece


def local(corr, bonds_down, bonds_across, repulsion):
    faces_out = [on_chip(*s) for s in FACES]
    e_scratch = [pltpu.VMEM((5 * LANES, LANES), F32), pltpu.VMEM((8, COLUMNS), F32)]
    y, bonds, colw, *faces, share = call(
        first_kernel,
        (corr, bonds_down, bonds_across, repulsion),
        [on_chip(*STATE), on_chip(3, LATTICE, LATTICE), on_chip(17, 8, COLUMNS), *faces_out, on_chip(2 * SLOT, LANES)],
        [
            pltpu.VMEM((5 * LANES, LANES), F32),
            pltpu.VMEM((2, TILES, 8, LANES), F32),
            pltpu.VMEM((TILES, 8, LANES), jnp.int32),
            pltpu.SemaphoreType.DMA((3 + 8 * CHUNKS,)),
        ],
        loads=True,
    )
    weights = (call(row_weights_kernel, (bonds,), on_chip(9, SQUARE, LANES)), colw)
    part, halos = first_exchange(faces, share, weights[0], interior(False, y, y, weights, (0, 8, 12, 18, 24)))
    y1, *faces = call(middle_kernel, (part, y, *halos, *weights), [on_chip(*STATE), *faces_out], e_scratch)
    part, halos = second_exchange(faces, halos[-1], interior(True, y1, y, weights, (0, 4, 8, 12, 16, 20, 24)))
    return call(
        last_kernel,
        (part, y1, *halos, *weights),
        jax.ShapeDtypeStruct(STATE, F32),
        [*e_scratch, pltpu.VMEM(STATE, F32), pltpu.SemaphoreType.DMA((10,))],
        out_specs=pl.BlockSpec(memory_space=pl.ANY),
    )


def solution(mesh):
    in_specs = (P(None, "row", "col"), P(), P(), P())
    out_specs = P(None, "row", "col")
    return jax.shard_map(local, mesh=mesh, in_specs=in_specs, out_specs=out_specs, check_vma=False)
```

```python
import functools

import jax
import jax.numpy as jnp
from jax import lax
from jax.experimental import pallas as pl
from jax.experimental.pallas import tpu as pltpu
from jax.sharding import PartitionSpec as P

PATCH = 24
SQUARE = PATCH * PATCH
COLUMNS = 2 * SQUARE
LANES = 128
TILES = COLUMNS // LANES
LATTICE = 4 * PATCH
TIME_STEP = 0.04
F32 = jnp.float32
VMEM_LIMIT = 8 * 1024 * 1024

DN_IN, UP_IN, RT_IN, LF_IN, DN_RIM, UP_RIM, RT_RIM, LF_RIM, ROW_U = range(9)
C_DN, C_UP, C_RT, C_LF, C_DN_RIM, C_UP_RIM, C_RT_E, C_RT_F, C_LF_E, C_LF_F, C_X_E, C_X_F, COL_U, C_DN_ALL, C_UP_ALL, C_RT_ALL, C_LF_ALL = range(17)


def iota(shape, dim):
    return lax.broadcasted_iota(jnp.int32, shape, dim)


def over24(x):
    return ((x.astype(F32) + 0.5) * (1.0 / PATCH)).astype(jnp.int32)


def on(mask):
    return jnp.where(mask, 1.0, 0.0).astype(F32)


def within(x, lo, hi):
    return on(x >= lo) * on(x <= hi)


def place():
    return lax.axis_index("row"), lax.axis_index("col")


def tile(t):
    return pl.ds(t * LANES, LANES)


def tables(bonds):
    side = (LATTICE, LATTICE)
    down = jnp.where(iota(side, 0) < LATTICE - 1, bonds[0], 0.0)
    across = jnp.where(iota(side, 1) < LATTICE - 1, bonds[1], 0.0)
    rep = bonds[2]
    dot = functools.partial(jnp.dot, precision=lax.Precision.HIGHEST, preferred_element_type=F32)
    return down, across, rep, dot


def row_weights_kernel(bonds, roww):
    row_id, _ = place()
    down, across, rep, dot = tables(bonds)
    s = iota((SQUARE, LATTICE), 0)
    lane = iota((SQUARE, LATTICE), 1)
    a = over24(s)
    b = s - PATCH * a
    ga = PATCH * (row_id // 4) + a
    gb = PATCH * (row_id % 4) + b

    def pick_rows(table, da, db):
        rows = dot(on(lane == ga + da), table)
        return jnp.sum(jnp.where(lane == gb + db, rows, 0.0), axis=1, keepdims=True)

    a1 = a[:, 0:1]
    b1 = b[:, 0:1]
    last = PATCH - 1
    dn = -TIME_STEP * pick_rows(down, 0, 0)
    up = -TIME_STEP * pick_rows(down, -1, 0)
    rt = -TIME_STEP * pick_rows(across, 0, 0)
    lf = -TIME_STEP * pick_rows(across, 0, -1)
    values = {
        DN_IN: dn * on(a1 < last), UP_IN: up * on(a1 > 0), RT_IN: rt * on(b1 < last), LF_IN: lf * on(b1 > 0),
        DN_RIM: dn * on(a1 == last), UP_RIM: up * on(a1 == 0), RT_RIM: rt * on(b1 == last), LF_RIM: lf * on(b1 == 0),
        ROW_U: TIME_STEP * pick_rows(rep, 0, 0),
    }
    for k, v in values.items():
        roww[k] = jnp.broadcast_to(v, (SQUARE, LANES))


def col_weights(bonds, colw):
    _, col_id = place()
    down, across, rep, _ = tables(bonds)
    last = PATCH - 1
    wide = (LATTICE, COLUMNS)
    j = iota(wide, 1)
    g = (j >= SQUARE).astype(jnp.int32)
    jj = j - SQUARE * g
    a = over24(jj)
    b = jj - PATCH * a
    sub = iota(wide, 0)
    parity = col_id % 2
    ga = PATCH * (col_id // 2) + a
    gb = PATCH * (2 * parity + g) + b

    def columns_of(tables, db):
        stacked = jnp.concatenate(tables, 0)
        parts = []
        for _ in range(3):
            parts.append(stacked.astype(jnp.bfloat16))
            stacked = stacked - parts[-1].astype(F32)
        hot = on(sub == gb + db).astype(jnp.bfloat16)
        high, mid, low = [jnp.dot(v, hot, preferred_element_type=F32) for v in parts]
        return (high + mid) + low

    def pick(columns, n, da):
        rows = columns[n * LATTICE : (n + 1) * LATTICE]
        return jnp.sum(jnp.where(sub == ga + da, rows, 0.0), axis=0, keepdims=True)

    here = columns_of([down, across, rep], 0)
    before = columns_of([across], -1)
    a = a[0:1]
    b = b[0:1]
    g = g[0:1]
    dn = TIME_STEP * pick(here, 0, 0)
    up = TIME_STEP * pick(here, 0, -1)
    rt = TIME_STEP * pick(here, 1, 0)
    lf = TIME_STEP * pick(before, 0, 0)
    tails0 = rt * on(b == last) * on(g == 0)
    heads1 = lf * on(b == 0) * on(g == 1)
    tails1 = rt * on(b == last) * on(g == 1)
    heads0 = lf * on(b == 0) * on(g == 0)
    even = on(jnp.full(a.shape, parity, jnp.int32) == 0)
    x_even = even * tails1
    x_odd = (1.0 - even) * heads0
    rt_e = within(a, 3, 18)
    lf_e = within(a, 5, 20)
    xe_e = within(a, 6, 21)
    xo_e = within(a, 2, 17)
    values = {
        C_DN: dn * on(a < last), C_UP: up * on(a > 0), C_RT: rt * on(b < last), C_LF: lf * on(b > 0),
        C_DN_RIM: dn * on(a == last), C_UP_RIM: up * on(a == 0),
        C_RT_E: tails0 * rt_e, C_RT_F: tails0 * (1.0 - rt_e),
        C_LF_E: heads1 * lf_e, C_LF_F: heads1 * (1.0 - lf_e),
        C_X_E: x_even * xe_e + x_odd * xo_e, C_X_F: x_even * (1.0 - xe_e) + x_odd * (1.0 - xo_e),
        COL_U: TIME_STEP * pick(here, 2, 0),
        C_DN_ALL: dn, C_UP_ALL: up, C_RT_ALL: rt, C_LF_ALL: lf,
    }
    for k, v in values.items():
        colw[k] = jnp.broadcast_to(v, (8, COLUMNS))


STRIP = (PATCH, LANES)


def squeeze_cols(tiles, lane24, m1, m2, n0):
    e = jnp.where(lane24 == m1, tiles[1], jnp.where(lane24 == m2, tiles[2], tiles[3]))
    f = jnp.where(lane24 == n0, tiles[0], tiles[4])
    return e, f


def lane_maps(shape=STRIP):
    lane = iota(shape, 1)
    return lane, lane - PATCH * over24(lane)


def parities():
    row_id, col_id = place()
    return lax.rem(col_id // 2, 2) == 0, lax.rem(col_id, 2) == 0, lax.rem(row_id // 4, 2) == 0, lax.rem(row_id, 2) == 0


FOLDS = (((0, 24, 16), (16, 88, 8), (40, 96, 8)), ((48, 24, 16), (64, 88, 16)), ((80, 24, 8), (104, 32, 8), (112, 88, 16)))
QUARTER = SQUARE // 4


def pack_faces(src, face_a, face_b, side, down_a, down_b, across_a, across_b, ready=None):
    up_first, even, row_up_first, row_even = parities()
    base = jnp.where(even, 4 * LANES, 0)
    lane, lane24 = lane_maps()
    lane8 = lax.rem(lane, 8)
    m1 = jnp.where(even, 7, 16)
    m2 = jnp.where(even, 23, 8)
    n0 = jnp.where(even, 15, 0)
    v0 = jnp.where(even, 7, 0)
    low = lane < 64
    half = lax.rem(lane, 64)
    first_part = half < PATCH
    last_part = half >= 64 - PATCH

    def faces(rows):
        edge = [[src[p, rows, tile(t)] for t in (0, 4, 8)] for p in range(2)]
        top = [jnp.where(low, e[0], e[1]) for e in edge]
        bot = [jnp.where(low, e[1], e[2]) for e in edge]
        top = jnp.where(last_part, pltpu.roll(top[0], 40, 1), top[1])
        bot = jnp.where(first_part, pltpu.roll(bot[0], 88, 1), bot[1])
        return jnp.where(up_first, bot, top), jnp.where(up_first, top, bot)

    def squeezed(rows):
        out = []
        for p in range(2):
            tiles = [src[p, rows, pl.ds(pl.multiple_of(base + LANES * t, LANES), LANES)] for t in range(5)]
            out += squeeze_cols(tiles, lane24, m1, m2, n0)
        return out

    def step(k, carry):
        at = [pl.ds(pl.multiple_of(q * QUARTER + k * PATCH, 8), PATCH) for q in range(4)]
        whole = [faces(rows) for rows in at]
        for n, msg in enumerate((face_a, face_b)):
            turned = {d: pltpu.roll(whole[3][n], d, 1) for d in (24, 56, 72, 104)}
            for q in range(3):
                value = whole[q][n]
                for source, to, count in FOLDS[q]:
                    value = jnp.where(jnp.logical_and(lane >= to, lane < to + count), turned[(to - source) % LANES], value)
                msg[at[q], :] = value
        for h in range(2):
            msg = None
            for slot, v in enumerate(squeezed(at[h]) + squeezed(at[h + 2])):
                msg = v if slot == 0 else jnp.where(lane8 == lax.rem(v0 + slot, 8), pltpu.roll(v, slot, 1), msg)
            side[at[h], :] = msg
        return carry

    steps = PATCH // 4
    if ready is None:
        lax.fori_loop(0, steps, step, 0, unroll=2)
    else:
        for i in range(CHUNKS):
            ready(i)
            lax.fori_loop(i * steps // CHUNKS, (i + 1) * steps // CHUNKS, step, 0, unroll=2)
    for p in range(2):
        for out, flip in ((down_a, row_up_first), (down_b, jnp.logical_not(row_up_first))):
            out[p] = src[p, pl.ds(pl.multiple_of(jnp.where(flip, SQUARE - PATCH, 0), 8), PATCH), :]
        for a in range(PATCH):
            left = src[p, a * PATCH : a * PATCH + 1, :]
            right = src[p, a * PATCH + PATCH - 1 : a * PATCH + PATCH, :]
            across_a[p, a : a + 1, :] = jnp.where(row_even, right, left)
            across_b[p, a : a + 1, :] = jnp.where(row_even, left, right)


SLOT = 24


def pack_densities(src, colw, slots, row_sums, sums, codes):
    row_id, col_id = place()
    odd = lax.rem(row_id, 2)
    across = lax.rem(row_id, 4) - 2 * lax.rem(col_id, 2)
    along = row_id // 4 - col_id // 2
    beside = jnp.logical_and(along == 0, jnp.logical_and(across >= -1, across <= 2))
    over = jnp.logical_and(jnp.abs(along) == 1, jnp.logical_and(across >= 0, across <= 1))
    slots[...] = jnp.zeros(slots.shape, F32)

    @pl.when(jnp.logical_or(beside, over))
    def _():
        row_sums[...] = jnp.zeros(row_sums.shape, F32)
        sums[...] = jnp.zeros(sums.shape, F32)
        lane = iota((8, LANES), 1)
        sub = iota((8, LANES), 0)
        for t in range(TILES):
            j = lane + t * LANES
            g = (j >= SQUARE).astype(jnp.int32)
            a = over24(j - SQUARE * g)
            b = j - SQUARE * g - PATCH * a
            codes[t] = 100 * (PATCH * (col_id // 2) + a) + PATCH * (2 * lax.rem(col_id, 2) + g) + b
        first = 100 * PATCH * (row_id // 4) + PATCH * lax.rem(row_id, 4)

        def share(a, tiles):
            along_rows = [jnp.zeros((8, LANES), F32) for _ in range(3)]
            for t in tiles:
                cols = pl.ds(pl.multiple_of(t * LANES, LANES), LANES)
                now = middle = jnp.zeros((8, LANES), F32)
                for k in range(3):
                    rows = pl.ds(pl.multiple_of(a * PATCH + 8 * k, 8), 8)
                    apart = first + 100 * a + 8 * k + sub - codes[t]
                    w = jnp.where(apart == 100, colw[C_DN_ALL, :, cols], 0.0)
                    w = jnp.where(apart == -100, colw[C_UP_ALL, :, cols], w)
                    w = jnp.where(apart == 1, colw[C_RT_ALL, :, cols], w)
                    w = jnp.where(apart == -1, colw[C_LF_ALL, :, cols], w)
                    flow = w * src[1, rows, cols]
                    own = jnp.where(apart == 0, src[0, rows, cols], 0.0)
                    now = now + own
                    middle = middle + own - flow
                    along_rows[k] = along_rows[k] + flow
                sums[0, t] += now
                sums[1, t] += middle
            for k in range(3):
                row_sums[pl.ds(pl.multiple_of(64 * odd + a * PATCH + 8 * k, 8), 8), :] = along_rows[k]

        @pl.when(beside)
        def _():
            def step(a, carry):
                starts = [jnp.clip(SQUARE * g + PATCH * (a - 1), 0, (TILES - 2) * LANES) // LANES for g in range(2)]
                share(a, [start + d for start in starts for d in range(2)])
                return carry

            lax.fori_loop(0, PATCH, step, 0, unroll=3)

        @pl.when(over)
        def _():
            start = jnp.where(along == 1, 4, 0)
            share(jnp.where(along == 1, 0, PATCH - 1), [start, start + 4])

        for t in range(TILES):
            slots[t : t + 1, :] = jnp.sum(sums[0, t], axis=0, keepdims=True)
            slots[TILES + t : TILES + t + 1, :] = jnp.sum(sums[1, t], axis=0, keepdims=True)
        for t in range(5):
            got = jnp.sum(row_sums[t * LANES : (t + 1) * LANES, :].T, axis=0, keepdims=True)
            slots[pl.ds(SLOT + TILES + 4 * odd + t, 1), :] = got


CHUNKS = 3


def first_kernel(corr, down, across, rep, y, bonds, colw, *refs):
    faces, table, (*scratch, sems) = refs[:7], refs[7], refs[8:]
    tables_in = [pltpu.make_async_copy(v, bonds.at[n], sems.at[n]) for n, v in enumerate((down, across, rep))]
    step = QUARTER // CHUNKS
    chunks = []
    for i in range(CHUNKS):
        chunks.append([])
        for q in range(4):
            for p in range(2):
                rows = pl.ds(q * QUARTER + i * step, step)
                sem = sems.at[3 + (i * 4 + q) * 2 + p]
                chunks[-1].append(pltpu.make_async_copy(corr.at[p, rows], y.at[p, rows], sem))
    for c in sum([tables_in, *chunks], []):
        c.start()
    for c in tables_in:
        c.wait()
    col_weights(bonds, colw)

    def ready(i):
        for c in chunks[i]:
            c.wait()

    pack_faces(y, *faces, ready=ready)
    pack_densities(y, colw, table, *scratch)


def interior_kernel(final, first, last, *refs):
    y1, y, roww, colw, out = refs[-5:]
    sub = iota((8, LANES), 0)
    lane, lane24 = lane_maps((8, LANES))
    three = range(3)

    def strip(a, p):
        q = 1 - p
        here = pl.multiple_of(a * PATCH, 8)
        above = pl.multiple_of(jnp.maximum(a - 1, 0) * PATCH, 8)
        below = pl.multiple_of(jnp.minimum(a + 1, PATCH - 1) * PATCH, 8)

        def at(t, k, start=here):
            return y1[q, pl.ds(start + 8 * k, 8), tile(t)]

        def side(t0, m1, m2, n0, shift):
            pairs = [squeeze_cols([at(t0 + t, k) for t in range(5)], lane24, m1, m2, n0) for k in three]
            return [[pltpu.roll(v, shift, 1) for v in pair] for pair in pairs]

        def turned(t):
            x = [at(t, k) for k in three]
            return [[pltpu.roll(v, n, 1) for v in x] for n in (1, PATCH, LANES - 1, LANES - PATCH)]

        heads = side(4, 8, 0, 16, 87)
        tails = None
        before, now = None, turned(0)
        for t in range(TILES):
            later = turned(t + 1) if t < TILES - 1 else None
            if t == 4:
                tails = side(0, 15, 7, 23, 41)
            x = [at(t, k) for k in three]
            fwd = [pltpu.roll(v, 1, 0) for v in x]
            bwd = [pltpu.roll(v, 7, 0) for v in x]
            w = lambda n: colw[n, :, tile(t)]
            for k in three:
                rows = pl.ds(here + 8 * k, 8)
                rw = lambda n: roww[n, rows, :]
                left = fwd[0] if k == 0 else jnp.where(sub == 0, fwd[k - 1], fwd[k])
                right = bwd[2] if k == 2 else jnp.where(sub == 7, bwd[k + 1], bwd[k])
                minus_b = now[0][k] if t == 0 else jnp.where(lane < 1, before[0][k], now[0][k])
                minus_a = now[1][k] if t == 0 else jnp.where(lane < PATCH, before[1][k], now[1][k])
                plus_b = now[2][k] if later is None else jnp.where(lane >= LANES - 1, later[2][k], now[2][k])
                plus_a = now[3][k] if later is None else jnp.where(lane >= LANES - PATCH, later[3][k], now[3][k])
                acc = rw(DN_IN) * at(t, k, below) + rw(UP_IN) * at(t, k, above) + rw(RT_IN) * right + rw(LF_IN) * left
                acc = acc + w(C_DN) * plus_a + w(C_UP) * minus_a + w(C_RT) * plus_b + w(C_LF) * minus_b
                if t <= 3:
                    acc = acc + w(C_RT_E) * heads[k][0]
                if t in (0, 3, 4):
                    acc = acc + w(C_RT_F) * heads[k][1]
                if 5 <= t <= 8:
                    acc = acc + w(C_LF_E) * tails[k][0]
                if t in (4, 5, 8):
                    acc = acc + w(C_LF_F) * tails[k][1]
                old = y1[p, rows, tile(t)]
                if final:
                    old = old + y[p, rows, tile(t)]
                new = old + acc if p == 0 else old - acc
                out[p, rows, tile(t)] = 0.5 * new if final else new
            before, now = now, later

    def step(a, carry):
        for p in range(2):
            strip(a, p)
        return carry

    lax.fori_loop(first, last, step, 0, unroll=next(n for n in (4, 3, 2, 1) if (last - first) % n == 0))


def unfolded(msg, at, lane):
    value = None
    for q in range(3):
        carrier = msg[pl.ds(pl.multiple_of(q * QUARTER + at, 8), 8), :]
        for source, to, count in FOLDS[q]:
            turned = pltpu.roll(carrier, (source - to) % LANES, 1)
            inside = jnp.logical_and(lane >= source, lane < source + count)
            value = turned if value is None else jnp.where(inside, turned, value)
    return value


def finish(stage, base, y, halos, roww, colw, out, e_row, e_col, chunk_done=None):
    face_a, face_b, side, down_a, down_b, across_a, across_b, table = halos
    scale = 0.5 if stage else 1.0
    row_id, col_id = place()
    up_first, even, row_up_first, row_even = parities()
    row_odd = lax.rem(row_id, 2)
    shift = jnp.where(even, 87, 41)
    lane = iota((8, LANES), 1)
    col_slot, row_slot = table[0:SLOT, :], table[SLOT : 2 * SLOT, :]
    for t in range(5):
        u = stage * TILES + t
        strip = jnp.where(row_odd == 1, row_slot[4 + u : 5 + u, :], row_slot[u : u + 1, :])
        e_row[t * LANES : (t + 1) * LANES, :] = jnp.broadcast_to(strip, (LANES, LANES)).T
    for t in range(TILES):
        e_col[:, tile(t)] = col_slot[stage * TILES + t : stage * TILES + t + 1, :] * colw[COL_U, :, tile(t)]

    def strip(a, folded):
        here = pl.multiple_of(a * PATCH, 8)
        near = pl.ds(pl.multiple_of(8 * (a // 8), 8), 8)
        to_first = lax.rem(8 - lax.rem(a, 8), 8)
        to_last = 7 - lax.rem(a, 8)
        half = a // (PATCH // 2)
        for k in range(3):
            rows = pl.ds(here + 8 * k, 8)
            es = e_row[pl.ds(64 * row_odd + here + 8 * k, 8), :] * roww[ROW_U, rows, :]
            if folded:
                got = [unfolded(m, here - 3 * QUARTER + 8 * k, lane) for m in (face_a, face_b)]
            else:
                got = [m[rows, :] for m in (face_a, face_b)]
            lower = jnp.where(up_first, got[0], got[1])
            upper = jnp.where(up_first, got[1], got[0])
            lowers = (lower, pltpu.roll(lower, 40, 1))
            uppers = (upper, pltpu.roll(upper, 88, 1))
            packed = side[pl.ds(pl.multiple_of(here - half * (SQUARE // 2), 8) + 8 * k, 8), :]
            gaps = [es - e_col[:, tile(t)] for t in range(TILES)]
            for p in range(2):
                q = 1 - p
                se, sf = [pltpu.roll(packed, lax.rem(shift + LANES - (4 * half + 2 * q + n), LANES), 1) for n in range(2)]
                for t in range(TILES):
                    w = lambda n: colw[n, :, tile(t)]
                    acc = gaps[t] * y[q, rows, tile(t)]
                    if t in (0, 4):
                        acc = acc + w(C_UP_RIM) * uppers[q]
                    if t in (4, 8):
                        acc = acc + w(C_DN_RIM) * lowers[q]
                    if t != 4:
                        acc = acc + w(C_X_E) * se
                    if t in (0, 3, 4, 5, 8):
                        acc = acc + w(C_X_F) * sf
                    if k != 1:
                        pair = [m[q, near, tile(t)] for m in (across_a, across_b)]
                    if k == 0:
                        left = pltpu.roll(jnp.where(row_even, pair[1], pair[0]), to_first, 0)
                        acc = acc + roww[LF_RIM, rows, :] * left
                    if k == 2:
                        right = pltpu.roll(jnp.where(row_even, pair[0], pair[1]), to_last, 0)
                        acc = acc + roww[RT_RIM, rows, :] * right
                    if scale != 1.0:
                        acc = scale * acc
                    old = base[p, rows, tile(t)]
                    out[p, rows, tile(t)] = old + acc if p == 0 else old - acc

    def rim(a, weight, first, second):
        for p in range(2):
            for k in range(3):
                rows = pl.ds(a * PATCH + 8 * k, 8)
                w = roww[weight, rows, :] * (scale if p == 0 else -scale)
                for t in range(TILES):
                    pair = [m[1 - p, 8 * k : 8 * k + 8, tile(t)] for m in (first, second)]
                    out[p, rows, tile(t)] += w * jnp.where(row_up_first, pair[0], pair[1])

    fold = 3 * PATCH // 4
    stops = (0, fold, PATCH) if chunk_done is None else (0, fold // 3, 2 * fold // 3, fold, PATCH - 2, PATCH)
    for start, stop in zip(stops, stops[1:]):
        lax.fori_loop(start, stop, lambda a, c, f=start >= fold: (strip(a, f), c)[1], 0, unroll=3 if (stop - start) % 3 == 0 else 2)
        if start == 0:
            rim(0, UP_RIM, down_b, down_a)
        if stop == PATCH:
            rim(PATCH - 1, DN_RIM, down_a, down_b)
        if chunk_done is not None:
            chunk_done(start * PATCH, stop * PATCH)


def middle_kernel(base, y, *refs):
    halos, (roww, colw), (y1, *faces), (e_row, e_col) = refs[:8], refs[8:10], refs[10:18], refs[18:]
    finish(0, base, y, halos, roww, colw, y1, e_row, e_col)
    pack_faces(y1, *faces)


def last_kernel(base, y1, *refs):
    halos, (roww, colw), out_hbm, (e_row, e_col, out, sems) = refs[:8], refs[8:10], refs[10], refs[11:]
    copies = []

    def chunk_done(first, last):
        for p in range(2):
            rows = pl.ds(first, last - first)
            copies.append(pltpu.make_async_copy(out.at[p, rows], out_hbm.at[p, rows], sems.at[len(copies)]))
            copies[-1].start()

    finish(1, base, y1, halos, roww, colw, out, e_row, e_col, chunk_done)
    for c in copies:
        c.wait()


def on_chip(*shape):
    return pltpu.VMEM(shape, F32)


VM = pl.BlockSpec(memory_space=pltpu.VMEM)
STATE = (2, SQUARE, COLUMNS)
FACES = ((3 * QUARTER, LANES),) * 2 + ((SQUARE // 2, LANES),) + ((2, PATCH, COLUMNS),) * 4


def call(kernel, args, out_shapes, scratch=(), out_specs=None, aliases=None, loads=False):
    many = isinstance(out_shapes, (list, tuple))
    return pl.pallas_call(
        kernel,
        out_shape=out_shapes,
        in_specs=[pl.BlockSpec(memory_space=pl.ANY) if loads else VM] * len(args),
        out_specs=out_specs or ([VM] * len(out_shapes) if many else VM),
        scratch_shapes=list(scratch),
        input_output_aliases=aliases or {},
        compiler_params=pltpu.CompilerParams(vmem_limit_bytes=VMEM_LIMIT),
        cost_estimate=pl.CostEstimate(flops=1000, bytes_accessed=1000, transcendentals=0),
    )(*[pltpu.with_memory_space_constraint(x, pltpu.HBM if loads else pltpu.VMEM) for x in args])


def pairs(axis, linked):
    n = lax.axis_size(axis)
    found = [(i, j) for i in range(n) for j in range(i + 1, n) if linked(i, j)]
    return found + [(j, i) for i, j in found]


def traded(block, axis, linked):
    return lax.ppermute(block, axis, pairs(axis, linked))


def flipped(block, axis, bit):
    return traded(block, axis, lambda i, j: j == i ^ bit)


def tie(value, *after):
    def kernel(*refs):
        refs[-1][...] = refs[0][...]

    return call(kernel, (value, *after), on_chip(*value.shape))


def rows_of(*slots):
    return on_chip(sum(slots) * SLOT, LANES)


def slot(n):
    return pl.ds(pl.multiple_of(SLOT * n, 8), SLOT)


def grow(known, got, *after):
    rows = known.shape[0]

    def kernel(known, got, *refs):
        out = refs[-1]
        out[0:SLOT, :] = known[0:SLOT, :] + got[0:SLOT, :]
        out[SLOT:rows, :] = known[SLOT:rows, :]
        out[rows : 2 * rows - SLOT, :] = got[SLOT:rows, :]

    return call(kernel, (known, got, *after), on_chip(2 * rows - SLOT, LANES))


def added(known, got, *after):
    def kernel(known, got, *refs):
        refs[-1][...] = known[...] + got[...]

    return call(kernel, (known, got, *after), on_chip(*known.shape))


def halve_all(known, got, *after):
    def kernel(known, got, *refs):
        keep, send, table = refs[-3:]
        row_id, col_id = place()
        mine = row_id // 2
        for n, bits in enumerate((0, 2, 6, 4)):
            rows = slice(SLOT * (n + 1), SLOT * (n + 2))
            table[slot(mine ^ bits), :] = known[rows, :]
            table[slot(mine ^ 1 ^ bits), :] = got[rows, :]
        table[slot(col_id), :] += known[0:SLOT, :] + got[0:SLOT, :]
        half = col_id // 4
        for n in range(4):
            keep[SLOT * n : SLOT * (n + 1), :] = table[slot(4 * half + n), :]
            send[SLOT * n : SLOT * (n + 1), :] = table[slot(4 * (1 - half) + n), :]
        keep[4 * SLOT :, :] = table[slot(mine), :]
        send[4 * SLOT :, :] = table[slot(mine ^ 1), :]

    scratch = [pltpu.VMEM((8 * SLOT, LANES), F32)]
    return call(kernel, (known, got, *after), [rows_of(5), rows_of(5)], scratch)


def halve_four(known, got, *after):
    def kernel(known, got, *refs):
        keep, send, total = refs[-3:]
        z = lax.rem(place()[1], 4)
        total[...] = known[...] + got[...]
        for out, bits in ((keep, (0, 3)), (send, (1, 2))):
            for n in range(2):
                out[SLOT * n : SLOT * (n + 1), :] = total[slot(z ^ bits[n]), :]
            out[2 * SLOT :, :] = total[4 * SLOT :, :]

    return call(kernel, (known, got, *after), [rows_of(3), rows_of(3)], [pltpu.VMEM((5 * SLOT, LANES), F32)])


def halve_two(known, got, *after):
    def kernel(known, got, *refs):
        keep, send = refs[-2:]
        total = known[...] + got[...]
        keep[0:SLOT, :] = total[0:SLOT]
        send[0:SLOT, :] = total[SLOT : 2 * SLOT]
        keep[SLOT:, :] = total[2 * SLOT :]
        send[SLOT:, :] = total[2 * SLOT :]

    return call(kernel, (known, got, *after), [rows_of(2), rows_of(2)])


def swap_face_a(x):
    return flipped(x, "col", 2)


def swapped(x, partner):
    rows, cols = lax.axis_size("row"), lax.axis_size("col")
    places = [(r, c) for r in range(rows) for c in range(cols)]
    route = [(r * cols + c, partner(r, c)[0] * cols + partner(r, c)[1]) for r, c in places]
    return lax.ppermute(x, ("row", "col"), route)


def swap_face_b(x):
    return swapped(x, lambda r, c: (r, c ^ 6) if c // 2 in (1, 2) else (r ^ 1, c))


def swap_side(x):
    return flipped(x, "col", 1)


def swap_down_a(x):
    return flipped(x, "row", 4)


def swap_down_b(x):
    return flipped(x, "row", 12)


def swap_across_a(x):
    return flipped(x, "row", 1)


def swap_across_b(x):
    return swapped(x, lambda r, c: (r ^ 3, c) if r % 4 in (1, 2) else (r ^ 4, c))


def swap_bits(x, row_bits, col_bits):
    return swapped(x, lambda r, c: (r ^ row_bits, c ^ col_bits))


def first_exchange(faces, share, first_work, piece):
    face_a, face_b, side, down_a, down_b, across_a, across_b = faces
    side = swap_side(side)
    face_b = swap_face_b(face_b)
    face_a = swap_face_a(face_a)
    known = grow(share, flipped(share, "row", 4), first_work)
    part = piece(0, None, known)
    known = grow(known, flipped(known, "row", 12), part)
    down_a = swap_down_a(tie(down_a, known))
    known = added(known, flipped(known, "row", 1), side)
    down_b = swap_down_b(tie(down_b, known))
    known, send = halve_all(known, flipped(known, "row", 2), face_a, face_b)
    across_b = swap_across_b(tie(across_b, known))
    part = piece(1, part, known)
    known, send = halve_four(known, swap_bits(send, 2, 4), part, down_a, down_b)
    across_a = swap_across_a(tie(across_a, known))
    part = piece(2, part, known)
    known, send = halve_two(known, flipped(send, "col", 1), part, across_b)
    part = piece(3, part, known)
    table = added(known, flipped(send, "col", 3), part, across_a)
    return part, (face_a, face_b, side, down_a, down_b, across_a, across_b, table)


def second_exchange(faces, table, piece):
    face_a, face_b, side, down_a, down_b, across_a, across_b = faces
    face_b = swap_face_b(face_b)
    face_a = swap_face_a(face_a)
    across_a = swap_across_a(across_a)
    across_b = swap_across_b(across_b)
    side = swap_side(side)
    part = piece(0, None)
    down_a = swap_down_a(tie(down_a, part))
    down_b = swap_down_b(tie(down_b, part))
    part = piece(1, part, across_a, side)
    part = piece(2, part)
    part = piece(3, part)
    part = piece(4, part)
    part = piece(5, part)
    return part, (face_a, face_b, side, down_a, down_b, across_a, across_b, table)


def interior(final, y1, y, weights, stops):
    def piece(n, part, *after):
        kernel = functools.partial(interior_kernel, final, stops[n], stops[n + 1])
        args = (*after, y1, y, *weights)
        if n == 0:
            return call(kernel, args, on_chip(*STATE))
        return call(kernel, (part, *args), on_chip(*STATE), aliases={0: 0})

    return piece


def local(corr, bonds_down, bonds_across, repulsion):
    faces_out = [on_chip(*s) for s in FACES]
    e_scratch = [pltpu.VMEM((5 * LANES, LANES), F32), pltpu.VMEM((8, COLUMNS), F32)]
    y, bonds, colw, *faces, share = call(
        first_kernel,
        (corr, bonds_down, bonds_across, repulsion),
        [on_chip(*STATE), on_chip(3, LATTICE, LATTICE), on_chip(17, 8, COLUMNS), *faces_out, on_chip(2 * SLOT, LANES)],
        [
            pltpu.VMEM((5 * LANES, LANES), F32),
            pltpu.VMEM((2, TILES, 8, LANES), F32),
            pltpu.VMEM((TILES, 8, LANES), jnp.int32),
            pltpu.SemaphoreType.DMA((3 + 8 * CHUNKS,)),
        ],
        loads=True,
    )
    weights = (call(row_weights_kernel, (bonds,), on_chip(9, SQUARE, LANES)), colw)
    part, halos = first_exchange(faces, share, weights[0], interior(False, y, y, weights, (0, 2, 8, 16, 24)))
    y1, *faces = call(middle_kernel, (part, y, *halos, *weights), [on_chip(*STATE), *faces_out], e_scratch)
    part, halos = second_exchange(faces, halos[-1], interior(True, y1, y, weights, (0, 4, 8, 12, 16, 20, 24)))
    return call(
        last_kernel,
        (part, y1, *halos, *weights),
        jax.ShapeDtypeStruct(STATE, F32),
        [*e_scratch, pltpu.VMEM(STATE, F32), pltpu.SemaphoreType.DMA((10,))],
        out_specs=pl.BlockSpec(memory_space=pl.ANY),
    )


def solution(mesh):
    in_specs = (P(None, "row", "col"), P(), P(), P())
    out_specs = P(None, "row", "col")
    return jax.shard_map(local, mesh=mesh, in_specs=in_specs, out_specs=out_specs, check_vma=False)
```

```python
import functools

import jax
import jax.numpy as jnp
from jax import lax
from jax.experimental import pallas as pl
from jax.experimental.pallas import tpu as pltpu
from jax.sharding import PartitionSpec as P

PATCH = 24
SQUARE = PATCH * PATCH
COLUMNS = 2 * SQUARE
LANES = 128
TILES = COLUMNS // LANES
LATTICE = 4 * PATCH
TIME_STEP = 0.04
F32 = jnp.float32
VMEM_LIMIT = 8 * 1024 * 1024

DN_IN, UP_IN, RT_IN, LF_IN, DN_RIM, UP_RIM, RT_RIM, LF_RIM, ROW_U = range(9)
C_DN, C_UP, C_RT, C_LF, C_DN_RIM, C_UP_RIM, C_RT_E, C_RT_F, C_LF_E, C_LF_F, C_X_E, C_X_F, COL_U, C_DN_ALL, C_UP_ALL, C_RT_ALL, C_LF_ALL = range(17)


def iota(shape, dim):
    return lax.broadcasted_iota(jnp.int32, shape, dim)


def over24(x):
    return ((x.astype(F32) + 0.5) * (1.0 / PATCH)).astype(jnp.int32)


def on(mask):
    return jnp.where(mask, 1.0, 0.0).astype(F32)


def within(x, lo, hi):
    return on(x >= lo) * on(x <= hi)


def place():
    return lax.axis_index("row"), lax.axis_index("col")


def tile(t):
    return pl.ds(t * LANES, LANES)


def tables(bonds):
    side = (LATTICE, LATTICE)
    down = jnp.where(iota(side, 0) < LATTICE - 1, bonds[0], 0.0)
    across = jnp.where(iota(side, 1) < LATTICE - 1, bonds[1], 0.0)
    rep = bonds[2]
    dot = functools.partial(jnp.dot, precision=lax.Precision.HIGHEST, preferred_element_type=F32)
    return down, across, rep, dot


def row_weights_kernel(bonds, roww):
    row_id, _ = place()
    down, across, rep, dot = tables(bonds)
    s = iota((SQUARE, LATTICE), 0)
    lane = iota((SQUARE, LATTICE), 1)
    a = over24(s)
    b = s - PATCH * a
    ga = PATCH * (row_id // 4) + a
    gb = PATCH * (row_id % 4) + b

    def pick_rows(table, da, db):
        rows = dot(on(lane == ga + da), table)
        return jnp.sum(jnp.where(lane == gb + db, rows, 0.0), axis=1, keepdims=True)

    a1 = a[:, 0:1]
    b1 = b[:, 0:1]
    last = PATCH - 1
    dn = -TIME_STEP * pick_rows(down, 0, 0)
    up = -TIME_STEP * pick_rows(down, -1, 0)
    rt = -TIME_STEP * pick_rows(across, 0, 0)
    lf = -TIME_STEP * pick_rows(across, 0, -1)
    values = {
        DN_IN: dn * on(a1 < last), UP_IN: up * on(a1 > 0), RT_IN: rt * on(b1 < last), LF_IN: lf * on(b1 > 0),
        DN_RIM: dn * on(a1 == last), UP_RIM: up * on(a1 == 0), RT_RIM: rt * on(b1 == last), LF_RIM: lf * on(b1 == 0),
        ROW_U: TIME_STEP * pick_rows(rep, 0, 0),
    }
    for k, v in values.items():
        roww[k] = jnp.broadcast_to(v, (SQUARE, LANES))


def col_weights(bonds, colw):
    _, col_id = place()
    down, across, rep, _ = tables(bonds)
    last = PATCH - 1
    wide = (LATTICE, COLUMNS)
    j = iota(wide, 1)
    g = (j >= SQUARE).astype(jnp.int32)
    jj = j - SQUARE * g
    a = over24(jj)
    b = jj - PATCH * a
    sub = iota(wide, 0)
    parity = col_id % 2
    ga = PATCH * (col_id // 2) + a
    gb = PATCH * (2 * parity + g) + b

    def columns_of(tables, db):
        stacked = jnp.concatenate(tables, 0)
        parts = []
        for _ in range(3):
            parts.append(stacked.astype(jnp.bfloat16))
            stacked = stacked - parts[-1].astype(F32)
        hot = on(sub == gb + db).astype(jnp.bfloat16)
        high, mid, low = [jnp.dot(v, hot, preferred_element_type=F32) for v in parts]
        return (high + mid) + low

    def pick(columns, n, da):
        rows = columns[n * LATTICE : (n + 1) * LATTICE]
        return jnp.sum(jnp.where(sub == ga + da, rows, 0.0), axis=0, keepdims=True)

    here = columns_of([down, across, rep], 0)
    before = columns_of([across], -1)
    a = a[0:1]
    b = b[0:1]
    g = g[0:1]
    dn = TIME_STEP * pick(here, 0, 0)
    up = TIME_STEP * pick(here, 0, -1)
    rt = TIME_STEP * pick(here, 1, 0)
    lf = TIME_STEP * pick(before, 0, 0)
    tails0 = rt * on(b == last) * on(g == 0)
    heads1 = lf * on(b == 0) * on(g == 1)
    tails1 = rt * on(b == last) * on(g == 1)
    heads0 = lf * on(b == 0) * on(g == 0)
    even = on(jnp.full(a.shape, parity, jnp.int32) == 0)
    x_even = even * tails1
    x_odd = (1.0 - even) * heads0
    rt_e = within(a, 3, 18)
    lf_e = within(a, 5, 20)
    xe_e = within(a, 6, 21)
    xo_e = within(a, 2, 17)
    values = {
        C_DN: dn * on(a < last), C_UP: up * on(a > 0), C_RT: rt * on(b < last), C_LF: lf * on(b > 0),
        C_DN_RIM: dn * on(a == last), C_UP_RIM: up * on(a == 0),
        C_RT_E: tails0 * rt_e, C_RT_F: tails0 * (1.0 - rt_e),
        C_LF_E: heads1 * lf_e, C_LF_F: heads1 * (1.0 - lf_e),
        C_X_E: x_even * xe_e + x_odd * xo_e, C_X_F: x_even * (1.0 - xe_e) + x_odd * (1.0 - xo_e),
        COL_U: TIME_STEP * pick(here, 2, 0),
        C_DN_ALL: dn, C_UP_ALL: up, C_RT_ALL: rt, C_LF_ALL: lf,
    }
    for k, v in values.items():
        colw[k] = jnp.broadcast_to(v, (8, COLUMNS))


STRIP = (PATCH, LANES)


def squeeze_cols(tiles, lane24, m1, m2, n0):
    e = jnp.where(lane24 == m1, tiles[1], jnp.where(lane24 == m2, tiles[2], tiles[3]))
    f = jnp.where(lane24 == n0, tiles[0], tiles[4])
    return e, f


def lane_maps(shape=STRIP):
    lane = iota(shape, 1)
    return lane, lane - PATCH * over24(lane)


def parities():
    row_id, col_id = place()
    return lax.rem(col_id // 2, 2) == 0, lax.rem(col_id, 2) == 0, lax.rem(row_id // 4, 2) == 0, lax.rem(row_id, 2) == 0


FOLDS = (((0, 24, 16), (16, 88, 8), (40, 96, 8)), ((48, 24, 16), (64, 88, 16)), ((80, 24, 8), (104, 32, 8), (112, 88, 16)))
QUARTER = SQUARE // 4


def pack_faces(src, face_a, face_b, side, down_a, down_b, across_a, across_b, ready=None):
    up_first, even, row_up_first, row_even = parities()
    base = jnp.where(even, 4 * LANES, 0)
    lane, lane24 = lane_maps()
    lane8 = lax.rem(lane, 8)
    m1 = jnp.where(even, 7, 16)
    m2 = jnp.where(even, 23, 8)
    n0 = jnp.where(even, 15, 0)
    v0 = jnp.where(even, 7, 0)
    low = lane < 64
    half = lax.rem(lane, 64)
    first_part = half < PATCH
    last_part = half >= 64 - PATCH

    def faces(rows):
        edge = [[src[p, rows, tile(t)] for t in (0, 4, 8)] for p in range(2)]
        top = [jnp.where(low, e[0], e[1]) for e in edge]
        bot = [jnp.where(low, e[1], e[2]) for e in edge]
        top = jnp.where(last_part, pltpu.roll(top[0], 40, 1), top[1])
        bot = jnp.where(first_part, pltpu.roll(bot[0], 88, 1), bot[1])
        return jnp.where(up_first, bot, top), jnp.where(up_first, top, bot)

    def squeezed(rows):
        out = []
        for p in range(2):
            tiles = [src[p, rows, pl.ds(pl.multiple_of(base + LANES * t, LANES), LANES)] for t in range(5)]
            out += squeeze_cols(tiles, lane24, m1, m2, n0)
        return out

    def step(k, carry):
        at = [pl.ds(pl.multiple_of(q * QUARTER + k * PATCH, 8), PATCH) for q in range(4)]
        whole = [faces(rows) for rows in at]
        for n, msg in enumerate((face_a, face_b)):
            turned = {d: pltpu.roll(whole[3][n], d, 1) for d in (24, 56, 72, 104)}
            for q in range(3):
                value = whole[q][n]
                for source, to, count in FOLDS[q]:
                    value = jnp.where(jnp.logical_and(lane >= to, lane < to + count), turned[(to - source) % LANES], value)
                msg[at[q], :] = value
        for h in range(2):
            msg = None
            for slot, v in enumerate(squeezed(at[h]) + squeezed(at[h + 2])):
                msg = v if slot == 0 else jnp.where(lane8 == lax.rem(v0 + slot, 8), pltpu.roll(v, slot, 1), msg)
            side[at[h], :] = msg
        return carry

    steps = PATCH // 4
    if ready is None:
        lax.fori_loop(0, steps, step, 0, unroll=2)
    else:
        for i in range(CHUNKS):
            ready(i)
            lax.fori_loop(i * steps // CHUNKS, (i + 1) * steps // CHUNKS, step, 0, unroll=2)
    for p in range(2):
        for out, flip in ((down_a, row_up_first), (down_b, jnp.logical_not(row_up_first))):
            out[p] = src[p, pl.ds(pl.multiple_of(jnp.where(flip, SQUARE - PATCH, 0), 8), PATCH), :]
        for a in range(PATCH):
            left = src[p, a * PATCH : a * PATCH + 1, :]
            right = src[p, a * PATCH + PATCH - 1 : a * PATCH + PATCH, :]
            across_a[p, a : a + 1, :] = jnp.where(row_even, right, left)
            across_b[p, a : a + 1, :] = jnp.where(row_even, left, right)


SLOT = 24


def pack_densities(src, colw, slots, row_sums, sums, codes):
    row_id, col_id = place()
    odd = lax.rem(row_id, 2)
    across = lax.rem(row_id, 4) - 2 * lax.rem(col_id, 2)
    along = row_id // 4 - col_id // 2
    beside = jnp.logical_and(along == 0, jnp.logical_and(across >= -1, across <= 2))
    over = jnp.logical_and(jnp.abs(along) == 1, jnp.logical_and(across >= 0, across <= 1))
    slots[...] = jnp.zeros(slots.shape, F32)

    @pl.when(jnp.logical_or(beside, over))
    def _():
        row_sums[...] = jnp.zeros(row_sums.shape, F32)
        sums[...] = jnp.zeros(sums.shape, F32)
        lane = iota((8, LANES), 1)
        sub = iota((8, LANES), 0)
        for t in range(TILES):
            j = lane + t * LANES
            g = (j >= SQUARE).astype(jnp.int32)
            a = over24(j - SQUARE * g)
            b = j - SQUARE * g - PATCH * a
            codes[t] = 100 * (PATCH * (col_id // 2) + a) + PATCH * (2 * lax.rem(col_id, 2) + g) + b
        first = 100 * PATCH * (row_id // 4) + PATCH * lax.rem(row_id, 4)

        def share(a, tiles):
            along_rows = [jnp.zeros((8, LANES), F32) for _ in range(3)]
            for t in tiles:
                cols = pl.ds(pl.multiple_of(t * LANES, LANES), LANES)
                now = middle = jnp.zeros((8, LANES), F32)
                for k in range(3):
                    rows = pl.ds(pl.multiple_of(a * PATCH + 8 * k, 8), 8)
                    apart = first + 100 * a + 8 * k + sub - codes[t]
                    w = jnp.where(apart == 100, colw[C_DN_ALL, :, cols], 0.0)
                    w = jnp.where(apart == -100, colw[C_UP_ALL, :, cols], w)
                    w = jnp.where(apart == 1, colw[C_RT_ALL, :, cols], w)
                    w = jnp.where(apart == -1, colw[C_LF_ALL, :, cols], w)
                    flow = w * src[1, rows, cols]
                    own = jnp.where(apart == 0, src[0, rows, cols], 0.0)
                    now = now + own
                    middle = middle + own - flow
                    along_rows[k] = along_rows[k] + flow
                sums[0, t] += now
                sums[1, t] += middle
            for k in range(3):
                row_sums[pl.ds(pl.multiple_of(64 * odd + a * PATCH + 8 * k, 8), 8), :] = along_rows[k]

        @pl.when(beside)
        def _():
            def step(a, carry):
                starts = [jnp.clip(SQUARE * g + PATCH * (a - 1), 0, (TILES - 2) * LANES) // LANES for g in range(2)]
                share(a, [start + d for start in starts for d in range(2)])
                return carry

            lax.fori_loop(0, PATCH, step, 0, unroll=3)

        @pl.when(over)
        def _():
            start = jnp.where(along == 1, 4, 0)
            share(jnp.where(along == 1, 0, PATCH - 1), [start, start + 4])

        for t in range(TILES):
            slots[t : t + 1, :] = jnp.sum(sums[0, t], axis=0, keepdims=True)
            slots[TILES + t : TILES + t + 1, :] = jnp.sum(sums[1, t], axis=0, keepdims=True)
        for t in range(5):
            got = jnp.sum(row_sums[t * LANES : (t + 1) * LANES, :].T, axis=0, keepdims=True)
            slots[pl.ds(SLOT + TILES + 4 * odd + t, 1), :] = got


CHUNKS = 3


def first_kernel(corr, down, across, rep, y, bonds, colw, *refs):
    faces, table, (*scratch, sems) = refs[:7], refs[7], refs[8:]
    tables_in = [pltpu.make_async_copy(v, bonds.at[n], sems.at[n]) for n, v in enumerate((down, across, rep))]
    step = QUARTER // CHUNKS
    chunks = []
    for i in range(CHUNKS):
        chunks.append([])
        for q in range(4):
            for p in range(2):
                rows = pl.ds(q * QUARTER + i * step, step)
                sem = sems.at[3 + (i * 4 + q) * 2 + p]
                chunks[-1].append(pltpu.make_async_copy(corr.at[p, rows], y.at[p, rows], sem))
    for c in sum([tables_in, *chunks], []):
        c.start()
    for c in tables_in:
        c.wait()
    col_weights(bonds, colw)

    def ready(i):
        for c in chunks[i]:
            c.wait()

    pack_faces(y, *faces, ready=ready)
    pack_densities(y, colw, table, *scratch)


def interior_kernel(final, first, last, *refs):
    y1, y, roww, colw, out = refs[-5:]
    sub = iota((8, LANES), 0)
    lane, lane24 = lane_maps((8, LANES))
    three = range(3)

    def strip(a, p):
        q = 1 - p
        here = pl.multiple_of(a * PATCH, 8)
        above = pl.multiple_of(jnp.maximum(a - 1, 0) * PATCH, 8)
        below = pl.multiple_of(jnp.minimum(a + 1, PATCH - 1) * PATCH, 8)

        def at(t, k, start=here):
            return y1[q, pl.ds(start + 8 * k, 8), tile(t)]

        def side(t0, m1, m2, n0, shift):
            pairs = [squeeze_cols([at(t0 + t, k) for t in range(5)], lane24, m1, m2, n0) for k in three]
            return [[pltpu.roll(v, shift, 1) for v in pair] for pair in pairs]

        def turned(t):
            x = [at(t, k) for k in three]
            return [[pltpu.roll(v, n, 1) for v in x] for n in (1, PATCH, LANES - 1, LANES - PATCH)]

        heads = side(4, 8, 0, 16, 87)
        tails = None
        before, now = None, turned(0)
        for t in range(TILES):
            later = turned(t + 1) if t < TILES - 1 else None
            if t == 4:
                tails = side(0, 15, 7, 23, 41)
            x = [at(t, k) for k in three]
            fwd = [pltpu.roll(v, 1, 0) for v in x]
            bwd = [pltpu.roll(v, 7, 0) for v in x]
            w = lambda n: colw[n, :, tile(t)]
            for k in three:
                rows = pl.ds(here + 8 * k, 8)
                rw = lambda n: roww[n, rows, :]
                left = fwd[0] if k == 0 else jnp.where(sub == 0, fwd[k - 1], fwd[k])
                right = bwd[2] if k == 2 else jnp.where(sub == 7, bwd[k + 1], bwd[k])
                minus_b = now[0][k] if t == 0 else jnp.where(lane < 1, before[0][k], now[0][k])
                minus_a = now[1][k] if t == 0 else jnp.where(lane < PATCH, before[1][k], now[1][k])
                plus_b = now[2][k] if later is None else jnp.where(lane >= LANES - 1, later[2][k], now[2][k])
                plus_a = now[3][k] if later is None else jnp.where(lane >= LANES - PATCH, later[3][k], now[3][k])
                acc = rw(DN_IN) * at(t, k, below) + rw(UP_IN) * at(t, k, above) + rw(RT_IN) * right + rw(LF_IN) * left
                acc = acc + w(C_DN) * plus_a + w(C_UP) * minus_a + w(C_RT) * plus_b + w(C_LF) * minus_b
                if t <= 3:
                    acc = acc + w(C_RT_E) * heads[k][0]
                if t in (0, 3, 4):
                    acc = acc + w(C_RT_F) * heads[k][1]
                if 5 <= t <= 8:
                    acc = acc + w(C_LF_E) * tails[k][0]
                if t in (4, 5, 8):
                    acc = acc + w(C_LF_F) * tails[k][1]
                old = y1[p, rows, tile(t)]
                if final:
                    old = old + y[p, rows, tile(t)]
                new = old + acc if p == 0 else old - acc
                out[p, rows, tile(t)] = 0.5 * new if final else new
            before, now = now, later

    def step(a, carry):
        for p in range(2):
            strip(a, p)
        return carry

    lax.fori_loop(first, last, step, 0, unroll=next(n for n in (5, 4, 3, 2, 1) if (last - first) % n == 0))


def unfolded(msg, at, lane):
    value = None
    for q in range(3):
        carrier = msg[pl.ds(pl.multiple_of(q * QUARTER + at, 8), 8), :]
        for source, to, count in FOLDS[q]:
            turned = pltpu.roll(carrier, (source - to) % LANES, 1)
            inside = jnp.logical_and(lane >= source, lane < source + count)
            value = turned if value is None else jnp.where(inside, turned, value)
    return value


def finish(stage, base, y, halos, roww, colw, out, e_row, e_col, chunk_done=None):
    face_a, face_b, side, down_a, down_b, across_a, across_b, table = halos
    scale = 0.5 if stage else 1.0
    row_id, col_id = place()
    up_first, even, row_up_first, row_even = parities()
    row_odd = lax.rem(row_id, 2)
    shift = jnp.where(even, 87, 41)
    lane = iota((8, LANES), 1)
    col_slot, row_slot = table[0:SLOT, :], table[SLOT : 2 * SLOT, :]
    for t in range(5):
        u = stage * TILES + t
        strip = jnp.where(row_odd == 1, row_slot[4 + u : 5 + u, :], row_slot[u : u + 1, :])
        e_row[t * LANES : (t + 1) * LANES, :] = jnp.broadcast_to(strip, (LANES, LANES)).T
    for t in range(TILES):
        e_col[:, tile(t)] = col_slot[stage * TILES + t : stage * TILES + t + 1, :] * colw[COL_U, :, tile(t)]

    def strip(a, folded):
        here = pl.multiple_of(a * PATCH, 8)
        near = pl.ds(pl.multiple_of(8 * (a // 8), 8), 8)
        to_first = lax.rem(8 - lax.rem(a, 8), 8)
        to_last = 7 - lax.rem(a, 8)
        half = a // (PATCH // 2)
        for k in range(3):
            rows = pl.ds(here + 8 * k, 8)
            es = e_row[pl.ds(64 * row_odd + here + 8 * k, 8), :] * roww[ROW_U, rows, :]
            if folded:
                got = [unfolded(m, here - 3 * QUARTER + 8 * k, lane) for m in (face_a, face_b)]
            else:
                got = [m[rows, :] for m in (face_a, face_b)]
            lower = jnp.where(up_first, got[0], got[1])
            upper = jnp.where(up_first, got[1], got[0])
            lowers = (lower, pltpu.roll(lower, 40, 1))
            uppers = (upper, pltpu.roll(upper, 88, 1))
            packed = side[pl.ds(pl.multiple_of(here - half * (SQUARE // 2), 8) + 8 * k, 8), :]
            gaps = [es - e_col[:, tile(t)] for t in range(TILES)]
            for p in range(2):
                q = 1 - p
                se, sf = [pltpu.roll(packed, lax.rem(shift + LANES - (4 * half + 2 * q + n), LANES), 1) for n in range(2)]
                for t in range(TILES):
                    w = lambda n: colw[n, :, tile(t)]
                    acc = gaps[t] * y[q, rows, tile(t)]
                    if t in (0, 4):
                        acc = acc + w(C_UP_RIM) * uppers[q]
                    if t in (4, 8):
                        acc = acc + w(C_DN_RIM) * lowers[q]
                    if t != 4:
                        acc = acc + w(C_X_E) * se
                    if t in (0, 3, 4, 5, 8):
                        acc = acc + w(C_X_F) * sf
                    if k != 1:
                        pair = [m[q, near, tile(t)] for m in (across_a, across_b)]
                    if k == 0:
                        left = pltpu.roll(jnp.where(row_even, pair[1], pair[0]), to_first, 0)
                        acc = acc + roww[LF_RIM, rows, :] * left
                    if k == 2:
                        right = pltpu.roll(jnp.where(row_even, pair[0], pair[1]), to_last, 0)
                        acc = acc + roww[RT_RIM, rows, :] * right
                    if scale != 1.0:
                        acc = scale * acc
                    old = base[p, rows, tile(t)]
                    out[p, rows, tile(t)] = old + acc if p == 0 else old - acc

    def rim(a, weight, first, second):
        for p in range(2):
            for k in range(3):
                rows = pl.ds(a * PATCH + 8 * k, 8)
                w = roww[weight, rows, :] * (scale if p == 0 else -scale)
                for t in range(TILES):
                    pair = [m[1 - p, 8 * k : 8 * k + 8, tile(t)] for m in (first, second)]
                    out[p, rows, tile(t)] += w * jnp.where(row_up_first, pair[0], pair[1])

    fold = 3 * PATCH // 4
    stops = (0, fold, PATCH) if chunk_done is None else (0, fold // 3, 2 * fold // 3, fold, PATCH - 2, PATCH)
    for start, stop in zip(stops, stops[1:]):
        lax.fori_loop(start, stop, lambda a, c, f=start >= fold: (strip(a, f), c)[1], 0, unroll=3 if (stop - start) % 3 == 0 else 2)
        if start == 0:
            rim(0, UP_RIM, down_b, down_a)
        if stop == PATCH:
            rim(PATCH - 1, DN_RIM, down_a, down_b)
        if chunk_done is not None:
            chunk_done(start * PATCH, stop * PATCH)


def middle_kernel(base, y, *refs):
    halos, (roww, colw), (y1, *faces), (e_row, e_col) = refs[:8], refs[8:10], refs[10:18], refs[18:]
    finish(0, base, y, halos, roww, colw, y1, e_row, e_col)
    pack_faces(y1, *faces)


def last_kernel(base, y1, *refs):
    halos, (roww, colw), out_hbm, (e_row, e_col, out, sems) = refs[:8], refs[8:10], refs[10], refs[11:]
    copies = []

    def chunk_done(first, last):
        for p in range(2):
            rows = pl.ds(first, last - first)
            copies.append(pltpu.make_async_copy(out.at[p, rows], out_hbm.at[p, rows], sems.at[len(copies)]))
            copies[-1].start()

    finish(1, base, y1, halos, roww, colw, out, e_row, e_col, chunk_done)
    for c in copies:
        c.wait()


def on_chip(*shape):
    return pltpu.VMEM(shape, F32)


VM = pl.BlockSpec(memory_space=pltpu.VMEM)
STATE = (2, SQUARE, COLUMNS)
FACES = ((3 * QUARTER, LANES),) * 2 + ((SQUARE // 2, LANES),) + ((2, PATCH, COLUMNS),) * 4


def call(kernel, args, out_shapes, scratch=(), out_specs=None, aliases=None, loads=False):
    many = isinstance(out_shapes, (list, tuple))
    return pl.pallas_call(
        kernel,
        out_shape=out_shapes,
        in_specs=[pl.BlockSpec(memory_space=pl.ANY) if loads else VM] * len(args),
        out_specs=out_specs or ([VM] * len(out_shapes) if many else VM),
        scratch_shapes=list(scratch),
        input_output_aliases=aliases or {},
        compiler_params=pltpu.CompilerParams(vmem_limit_bytes=VMEM_LIMIT),
        cost_estimate=pl.CostEstimate(flops=1000, bytes_accessed=1000, transcendentals=0),
    )(*[pltpu.with_memory_space_constraint(x, pltpu.HBM if loads else pltpu.VMEM) for x in args])


def pairs(axis, linked):
    n = lax.axis_size(axis)
    found = [(i, j) for i in range(n) for j in range(i + 1, n) if linked(i, j)]
    return found + [(j, i) for i, j in found]


def traded(block, axis, linked):
    return lax.ppermute(block, axis, pairs(axis, linked))


def flipped(block, axis, bit):
    return traded(block, axis, lambda i, j: j == i ^ bit)


def tie(value, *after):
    def kernel(*refs):
        refs[-1][...] = refs[0][...]

    return call(kernel, (value, *after), on_chip(*value.shape))


def rows_of(*slots):
    return on_chip(sum(slots) * SLOT, LANES)


def slot(n):
    return pl.ds(pl.multiple_of(SLOT * n, 8), SLOT)


def grow(known, got, *after):
    rows = known.shape[0]

    def kernel(known, got, *refs):
        out = refs[-1]
        out[0:SLOT, :] = known[0:SLOT, :] + got[0:SLOT, :]
        out[SLOT:rows, :] = known[SLOT:rows, :]
        out[rows : 2 * rows - SLOT, :] = got[SLOT:rows, :]

    return call(kernel, (known, got, *after), on_chip(2 * rows - SLOT, LANES))


def added(known, got, *after):
    def kernel(known, got, *refs):
        refs[-1][...] = known[...] + got[...]

    return call(kernel, (known, got, *after), on_chip(*known.shape))


def halve_all(known, got, *after):
    def kernel(known, got, *refs):
        keep, send, table = refs[-3:]
        row_id, col_id = place()
        mine = row_id // 2
        for n, bits in enumerate((0, 2, 6, 4)):
            rows = slice(SLOT * (n + 1), SLOT * (n + 2))
            table[slot(mine ^ bits), :] = known[rows, :]
            table[slot(mine ^ 1 ^ bits), :] = got[rows, :]
        table[slot(col_id), :] += known[0:SLOT, :] + got[0:SLOT, :]
        half = col_id // 4
        for n in range(4):
            keep[SLOT * n : SLOT * (n + 1), :] = table[slot(4 * half + n), :]
            send[SLOT * n : SLOT * (n + 1), :] = table[slot(4 * (1 - half) + n), :]
        keep[4 * SLOT :, :] = table[slot(mine), :]
        send[4 * SLOT :, :] = table[slot(mine ^ 1), :]

    scratch = [pltpu.VMEM((8 * SLOT, LANES), F32)]
    return call(kernel, (known, got, *after), [rows_of(5), rows_of(5)], scratch)


def halve_four(known, got, *after):
    def kernel(known, got, *refs):
        keep, send, total = refs[-3:]
        z = lax.rem(place()[1], 4)
        total[...] = known[...] + got[...]
        for out, bits in ((keep, (0, 3)), (send, (1, 2))):
            for n in range(2):
                out[SLOT * n : SLOT * (n + 1), :] = total[slot(z ^ bits[n]), :]
            out[2 * SLOT :, :] = total[4 * SLOT :, :]

    return call(kernel, (known, got, *after), [rows_of(3), rows_of(3)], [pltpu.VMEM((5 * SLOT, LANES), F32)])


def halve_two(known, got, *after):
    def kernel(known, got, *refs):
        keep, send = refs[-2:]
        total = known[...] + got[...]
        keep[0:SLOT, :] = total[0:SLOT]
        send[0:SLOT, :] = total[SLOT : 2 * SLOT]
        keep[SLOT:, :] = total[2 * SLOT :]
        send[SLOT:, :] = total[2 * SLOT :]

    return call(kernel, (known, got, *after), [rows_of(2), rows_of(2)])


def swap_face_a(x):
    return flipped(x, "col", 2)


def swapped(x, partner):
    rows, cols = lax.axis_size("row"), lax.axis_size("col")
    places = [(r, c) for r in range(rows) for c in range(cols)]
    route = [(r * cols + c, partner(r, c)[0] * cols + partner(r, c)[1]) for r, c in places]
    return lax.ppermute(x, ("row", "col"), route)


def swap_face_b(x):
    return swapped(x, lambda r, c: (r, c ^ 6) if c // 2 in (1, 2) else (r ^ 1, c))


def swap_side(x):
    return flipped(x, "col", 1)


def swap_down_a(x):
    return flipped(x, "row", 4)


def swap_down_b(x):
    return flipped(x, "row", 12)


def swap_across_a(x):
    return flipped(x, "row", 1)


def swap_across_b(x):
    return swapped(x, lambda r, c: (r ^ 3, c) if r % 4 in (1, 2) else (r ^ 4, c))


def swap_bits(x, row_bits, col_bits):
    return swapped(x, lambda r, c: (r ^ row_bits, c ^ col_bits))


def first_exchange(faces, share, first_work, piece):
    face_a, face_b, side, down_a, down_b, across_a, across_b = faces
    side = swap_side(side)
    face_b = swap_face_b(face_b)
    face_a = swap_face_a(face_a)
    known = grow(share, flipped(share, "row", 4), first_work)
    part = piece(0, None, known)
    known = grow(known, flipped(known, "row", 12), part)
    down_a = swap_down_a(tie(down_a, known))
    known = added(known, flipped(known, "row", 1), side)
    down_b = swap_down_b(tie(down_b, known))
    known, send = halve_all(known, flipped(known, "row", 2), face_a, face_b)
    across_b = swap_across_b(tie(across_b, known))
    part = piece(1, part, known)
    known, send = halve_four(known, swap_bits(send, 2, 4), part, down_a, down_b)
    across_a = swap_across_a(tie(across_a, known))
    part = piece(2, part, known)
    known, send = halve_two(known, flipped(send, "col", 1), part, across_b)
    part = piece(3, part, known)
    table = added(known, flipped(send, "col", 3), part, across_a)
    return part, (face_a, face_b, side, down_a, down_b, across_a, across_b, table)


def second_exchange(faces, table, piece):
    face_a, face_b, side, down_a, down_b, across_a, across_b = faces
    face_b = swap_face_b(face_b)
    face_a = swap_face_a(face_a)
    across_a = swap_across_a(across_a)
    across_b = swap_across_b(across_b)
    side = swap_side(side)
    part = piece(0, None)
    down_a = swap_down_a(tie(down_a, part))
    down_b = swap_down_b(tie(down_b, part))
    part = piece(1, part, across_a, side)
    part = piece(2, part)
    part = piece(3, part)
    part = piece(4, part)
    part = piece(5, part)
    return part, (face_a, face_b, side, down_a, down_b, across_a, across_b, table)


def interior(final, y1, y, weights, stops):
    def piece(n, part, *after):
        kernel = functools.partial(interior_kernel, final, stops[n], stops[n + 1])
        args = (*after, y1, y, *weights)
        if n == 0:
            return call(kernel, args, on_chip(*STATE))
        return call(kernel, (part, *args), on_chip(*STATE), aliases={0: 0})

    return piece


def local(corr, bonds_down, bonds_across, repulsion):
    faces_out = [on_chip(*s) for s in FACES]
    e_scratch = [pltpu.VMEM((5 * LANES, LANES), F32), pltpu.VMEM((8, COLUMNS), F32)]
    y, bonds, colw, *faces, share = call(
        first_kernel,
        (corr, bonds_down, bonds_across, repulsion),
        [on_chip(*STATE), on_chip(3, LATTICE, LATTICE), on_chip(17, 8, COLUMNS), *faces_out, on_chip(2 * SLOT, LANES)],
        [
            pltpu.VMEM((5 * LANES, LANES), F32),
            pltpu.VMEM((2, TILES, 8, LANES), F32),
            pltpu.VMEM((TILES, 8, LANES), jnp.int32),
            pltpu.SemaphoreType.DMA((3 + 8 * CHUNKS,)),
        ],
        loads=True,
    )
    weights = (call(row_weights_kernel, (bonds,), on_chip(9, SQUARE, LANES)), colw)
    part, halos = first_exchange(faces, share, weights[0], interior(False, y, y, weights, (0, 1, 5, 14, 24)))
    y1, *faces = call(middle_kernel, (part, y, *halos, *weights), [on_chip(*STATE), *faces_out], e_scratch)
    part, halos = second_exchange(faces, halos[-1], interior(True, y1, y, weights, (0, 4, 8, 12, 16, 20, 24)))
    return call(
        last_kernel,
        (part, y1, *halos, *weights),
        jax.ShapeDtypeStruct(STATE, F32),
        [*e_scratch, pltpu.VMEM(STATE, F32), pltpu.SemaphoreType.DMA((10,))],
        out_specs=pl.BlockSpec(memory_space=pl.ANY),
    )


def solution(mesh):
    in_specs = (P(None, "row", "col"), P(), P(), P())
    out_specs = P(None, "row", "col")
    return jax.shard_map(local, mesh=mesh, in_specs=in_specs, out_specs=out_specs, check_vma=False)
```
